256 devices in a mesh: dp: 16 (over x, y_lo, core), seq: 16 (over y_hi, z).
Axes of the slice: x: 4, y: 4 (y_hi: 2, y_lo: 2; y = y_hi * 2 + y_lo), z: 8, core: 2. Of those that a mesh axis runs over, the one named last changes fastest.
Arguments:
- queries: bfloat16 [65536, 32, 128], P(('dp', 'seq')), may hold values from -40 to 40
- keys: bfloat16 [65536, 4, 128], P(('dp', 'seq')), may hold values from -6 to 6
- values: bfloat16 [65536, 4, 128], P(('dp', 'seq')), may hold values from -6 to 6
- upstream: bfloat16 [65536, 32, 128], P(('dp', 'seq')), may hold values from -6 to 6
- rewards: float32 [16, 11], replicated, may hold values from 0 to 4
- response_length: int32 [16, 11], replicated, may hold values from 96 to 1024, as said below
- block_start: int32 [16, 11], replicated, may hold values from 0 to 24, as said below
- move_plan: int32 [16, 11], replicated, may hold values from 0 to 15, as said below
Outputs:
- attn_out: bfloat16 [65536, 32, 128], P(('dp', 'seq'))
- grad_queries: bfloat16 [65536, 32, 128], P(('dp', 'seq'))
- grad_keys: bfloat16 [65536, 4, 128], P(('dp', 'seq'))
- grad_values: bfloat16 [65536, 4, 128], P(('dp', 'seq'))
The draws below stay inside these ranges and needn't reach their ends.
Inputs may be any that keep to these rules, and one draw needn't show every extreme that they name: `response_length`: rollouts 0 to 7 of a group are short, at most 128 tokens and at least three quarters of that; the others are long, at least 384 tokens. Some short rollout has exactly 128 tokens and some long one exactly 1024 in every draw. `block_start`: short rollout j starts at block j; the long rollouts follow in order, each at the first whole block after the previous one ends. `move_plan`: long rollouts stay in their group. Short rollout j of group g goes to group (g + o_j) mod 16, with 8 distinct offsets o_j: every group receives exactly one short rollout for each slot j and sends at most one to any group.
All inputs are finite; a program needn't handle non-finite values.
Results may differ from the reference program's by a relative error of at most 0.029.
Values may be sent and summed in bfloat16 or wider, within the bound.
A program may use at most 128 MiB of HBM per device.

```python
import jax
import jax.numpy as jnp
from jax import lax

H = 32
KV = 4
DH = 128
BLK = 128
LONGS = 3
SHORTS = 8
ROLLS = 11
LW = 1024
GRP_TOK = 4096
TOKENS = 65536
N_DP = 16


def rollout_layout(key):
    perm_key, order_key, short_key, long_key, pick_key = jax.random.split(key, 5)
    every = jnp.arange(N_DP, dtype=jnp.int32)
    shuffled = jax.random.permutation(perm_key, N_DP).astype(jnp.int32)
    position = jnp.argsort(shuffled, stable=True).astype(jnp.int32)
    priority = jnp.where(every == N_DP // 2, -3, jnp.where(every == 1, -2, jnp.where(every == N_DP - 1, -1, position)))
    chosen = jnp.argsort(priority, stable=True)[:SHORTS].astype(jnp.int32)
    offsets = chosen[jax.random.permutation(order_key, SHORTS)]
    short_length = jax.random.randint(short_key, (N_DP, SHORTS), 3 * BLK // 4, BLK + 1)
    long_length = jax.random.randint(long_key, (N_DP, LONGS), 3 * LW // 8, LW + 1)
    selected = jax.random.randint(pick_key, (5,), 0, 1 << 20)
    short_length = short_length.at[selected[0] % N_DP, selected[1] % SHORTS].set(BLK)
    short_length = short_length.at[selected[2] % N_DP, (selected[1] + 1) % SHORTS].set(3 * BLK // 4)
    long_length = long_length.at[selected[3] % N_DP].set(LW)
    lengths = jnp.concatenate([short_length, long_length], axis=1).astype(jnp.int32)
    blocks = (long_length + BLK - 1) // BLK
    starts = SHORTS + jnp.cumsum(blocks, axis=1) - blocks
    first_blocks = jnp.concatenate([jnp.broadcast_to(jnp.arange(SHORTS, dtype=jnp.int32)[None, :], (N_DP, SHORTS)), starts], axis=1).astype(jnp.int32)
    groups = every[:, None]
    destination = jnp.concatenate([(groups + offsets[None, :]) % N_DP, jnp.broadcast_to(groups, (N_DP, LONGS))], axis=1).astype(jnp.int32)
    return (lengths, first_blocks, destination)


def draw_queries(key, part):
    key = jax.random.fold_in(key, 7)
    return jnp.clip(jax.random.normal(key, (TOKENS, H, DH), jnp.float32), -6.0, 6.0).astype(jnp.bfloat16)


def draw_keys(key, part):
    key = jax.random.fold_in(key, 9)
    return jnp.clip(jax.random.normal(key, (TOKENS, KV, DH), jnp.float32), -6.0, 6.0).astype(jnp.bfloat16)


def draw_response_length(key, part):
    layout = rollout_layout(key)
    return layout[0]


def draw_block_start(key, part):
    layout = rollout_layout(key)
    return layout[1]


def draw_move_plan(key, part):
    layout = rollout_layout(key)
    return layout[2]


def block_scale(rng, dims, shards, smallest, largest):
    def one(dim, shards_of):
        steps = jax.random.uniform(jax.random.fold_in(jax.random.fold_in(rng, 6), dim), (shards_of,), jnp.float32, smallest / len(shards), largest / len(shards))
        return jnp.repeat(jnp.exp(steps), dims[dim] // shards_of).reshape((-1,) + (1,) * (len(dims) - dim - 1))

    level = one(*shards[0])
    for cut in shards[1:]:
        level = level * one(*cut)
    return level


def bell_draw(key, shape, width, limit, shards=(), kind=jnp.bfloat16):
    loudness = block_scale(key, shape, shards, -0.22, 0.18) if shards else 1.0
    values = jax.random.normal(key, shape, jnp.float32) * width * loudness
    return jnp.minimum(jnp.maximum(values, -limit), limit).astype(kind)


def setup_inputs(seed: int = 0) -> dict:
    splits = jax.random.split(jax.random.key(seed), 9)
    return {
        "queries": draw_queries(jax.random.fold_in(splits[8], 71), 0),
        "keys": draw_keys(jax.random.fold_in(splits[8], 71), 0),
        "values": bell_draw(splits[2], (TOKENS, KV, DH), 1.0, 6.0, ((0, 256),)),
        "upstream": bell_draw(splits[3], (TOKENS, H, DH), 1.0, 6.0, ((0, 256),)),
        "rewards": jnp.clip(jax.random.uniform(splits[4], (N_DP, ROLLS), jnp.float32, 0.0, 4.0), 0.0, 4.0),
        "response_length": draw_response_length(jax.random.fold_in(splits[8], 71), 0),
        "block_start": draw_block_start(jax.random.fold_in(splits[8], 71), 0),
        "move_plan": draw_move_plan(jax.random.fold_in(splits[8], 71), 0),
    }


def masked_scores(query_f, key_f, lengths):
    extent = query_f.shape[1]
    products = jnp.einsum('blcgd,bmcd->bcglm', query_f, key_f) * (DH ** -0.5)
    rows = jnp.arange(extent, dtype=jnp.int32)
    allowed = (rows[None, None, :] <= rows[None, :, None]) & (rows[None, :, None] < lengths[:, None, None])
    return jnp.where(allowed[:, None, None], products, -1e30), allowed


def rollout_attention(query_part, key_part, value_part, grad_in, lengths):
    query_f = query_part.astype(jnp.float32)
    key_f = key_part.astype(jnp.float32)
    value_f = value_part.astype(jnp.float32)
    grad_f = grad_in.astype(jnp.float32)
    scores, allowed = masked_scores(query_f, key_f, lengths)
    highest = jnp.max(scores, axis=-1, keepdims=True)
    exponent = jnp.exp(scores - highest)
    row_sum = jnp.sum(exponent, axis=-1, keepdims=True)
    probability = jnp.where(allowed[:, None, None, :, :1], exponent / row_sum, 0.0)
    prob_half = probability.astype(jnp.bfloat16)
    result = jnp.einsum('bcglm,bmcd->blcgd', prob_half.astype(jnp.float32), value_f).astype(jnp.bfloat16)
    grad_prob = jnp.einsum('blcgd,bmcd->bcglm', grad_f, value_f)
    row_delta = jnp.einsum('blcgd,blcgd->bcgl', grad_f, result.astype(jnp.float32))
    grad_score = (probability * (grad_prob - row_delta[..., None])).astype(jnp.bfloat16).astype(jnp.float32)
    grad_query = (jnp.einsum('bcglm,bmcd->blcgd', grad_score, key_f) * (DH ** -0.5)).astype(jnp.bfloat16)
    grad_key = jnp.einsum('bcglm,blcgd->bmcd', grad_score, query_f) * (DH ** -0.5)
    grad_value = jnp.einsum('bcglm,blcgd->bmcd', prob_half.astype(jnp.float32), grad_f)
    return result, grad_query, grad_key, grad_value


def reference(queries, keys, values, upstream, rewards, response_length, block_start, move_plan):
    per_group = H // KV
    query_groups = queries.reshape(N_DP, GRP_TOK, KV, per_group, DH)
    key_groups = keys.reshape(N_DP, GRP_TOK, KV, DH)
    value_groups = values.reshape(N_DP, GRP_TOK, KV, DH)
    upstream_groups = upstream.reshape(N_DP, GRP_TOK, KV, per_group, DH)
    short_tokens = SHORTS * BLK
    short_slots = jnp.arange(SHORTS, dtype=jnp.int32)
    group_ids = jnp.arange(N_DP, dtype=jnp.int32)
    advantage = rewards - jnp.mean(rewards, axis=1, keepdims=True)

    def short_blocks(array):
        return array[:, :short_tokens].reshape((N_DP, SHORTS, BLK) + array.shape[2:])

    query_short = short_blocks(query_groups)
    key_short = short_blocks(key_groups)
    value_short = short_blocks(value_groups)

    def one_group(target):
        source = jnp.argmax(move_plan[:, :SHORTS] == target, axis=0).astype(jnp.int32)
        short_len = response_length[source, short_slots]
        short_adv = advantage[source, short_slots]
        position = jnp.arange(GRP_TOK, dtype=jnp.int32)
        long_start = (block_start[target, SHORTS:] * BLK).astype(jnp.int32)
        long_len = response_length[target, SHORTS:]
        long_adv = advantage[target, SHORTS:]
        inside = (position[None, :] >= long_start[:, None]) & (position[None, :] < long_start[:, None] + long_len[:, None])
        long_weight = jnp.sum(jnp.where(inside, long_adv[:, None], 0.0), axis=0)
        short_weight = jnp.where(jnp.arange(BLK, dtype=jnp.int32)[None, :] < short_len[:, None], short_adv[:, None], 0.0)
        weight = jnp.concatenate([short_weight.reshape(-1), long_weight[short_tokens:]])
        grad_in = (weight[:, None, None, None] * upstream_groups[target].astype(jnp.float32)).astype(jnp.bfloat16)
        query_bal = jnp.concatenate([query_short[source, short_slots].reshape((short_tokens, KV, per_group, DH)), query_groups[target, short_tokens:]])
        key_bal = jnp.concatenate([key_short[source, short_slots].reshape((short_tokens, KV, DH)), key_groups[target, short_tokens:]])
        value_bal = jnp.concatenate([value_short[source, short_slots].reshape((short_tokens, KV, DH)), value_groups[target, short_tokens:]])
        short_out, short_gq, short_gk, short_gv = rollout_attention(
            query_bal[:short_tokens].reshape(SHORTS, BLK, KV, per_group, DH),
            key_bal[:short_tokens].reshape(SHORTS, BLK, KV, DH),
            value_bal[:short_tokens].reshape(SHORTS, BLK, KV, DH),
            grad_in[:short_tokens].reshape(SHORTS, BLK, KV, per_group, DH),
            short_len)
        attn_long = jnp.zeros((GRP_TOK, KV, per_group, DH), jnp.bfloat16)
        query_long = jnp.zeros((GRP_TOK, KV, per_group, DH), jnp.bfloat16)
        key_long = jnp.zeros((GRP_TOK, KV, DH), jnp.float32)
        value_long = jnp.zeros((GRP_TOK, KV, DH), jnp.float32)
        for number in range(LONGS):
            offset = long_start[number]
            length = long_len[number]

            def window(array):
                return lax.dynamic_slice_in_dim(array, offset, LW, 0)[None]

            def accumulate(total, piece):
                return lax.dynamic_update_slice_in_dim(total, lax.dynamic_slice_in_dim(total, offset, LW, 0) + piece[0], offset, 0)

            long_out, long_gq, long_gk, long_gv = rollout_attention(window(query_bal), window(key_bal), window(value_bal), window(grad_in), length[None])
            attn_long = accumulate(attn_long, long_out)
            query_long = accumulate(query_long, long_gq)
            key_long = accumulate(key_long, long_gk)
            value_long = accumulate(value_long, long_gv)
        attn_group = jnp.concatenate([short_out.reshape((short_tokens, KV, per_group, DH)), attn_long[short_tokens:]])
        query_group = jnp.concatenate([short_gq.reshape((short_tokens, KV, per_group, DH)), query_long[short_tokens:]])
        key_group = jnp.concatenate([short_gk.reshape((short_tokens, KV, DH)), key_long[short_tokens:]]).astype(jnp.bfloat16)
        value_group = jnp.concatenate([short_gv.reshape((short_tokens, KV, DH)), value_long[short_tokens:]]).astype(jnp.bfloat16)
        return attn_group, query_group, key_group, value_group

    attn_all, query_all, key_all, value_all = lax.map(one_group, group_ids)
    return (attn_all.reshape(TOKENS, H, DH), query_all.reshape(TOKENS, H, DH),
            key_all.reshape(TOKENS, KV, DH), value_all.reshape(TOKENS, KV, DH))
```

```python
import functools

import jax
import jax.numpy as jnp
from jax import lax
from jax.experimental import pallas as pl
from jax.experimental.pallas import tpu as pltpu
from jax.sharding import PartitionSpec as P

DH = 128
BLK = 128
LONGS = 3
SHORTS = 8
NEVER = 1 << 20
SCALE = DH**-0.5
EXP_SCALE = SCALE * 1.4426950408889634
NT = (((1,), (1,)), ((), ()))
NN = (((1,), (0,)), ((), ()))


def dot(a, b, dims):
    return lax.dot_general(a, b, dims, preferred_element_type=jnp.float32)


def attend_tile(q, up, start, token, live, weight, load_k, load_v, load_kt, load_vt, add_dk, add_dv, s_ref, p_ref, chunk, chunks, key0):
    rows = q.shape[0]
    highest = jnp.full((1, rows), -1e30, jnp.float32)
    for c in range(chunks):
        s = dot(load_k(c), q, NT)
        key = key0 + c * chunk + lax.broadcasted_iota(jnp.int32, (chunk, rows), 0)
        allowed = key >= start
        if c == chunks - 1:
            allowed = allowed & (key <= token)
        s = jnp.where(allowed, s, -1e30)
        s_ref[c] = s
        highest = jnp.maximum(highest, jnp.max(s, axis=0, keepdims=True))
    shift = highest * EXP_SCALE
    total = jnp.zeros((1, rows), jnp.float32)
    out_t = jnp.zeros((DH, rows), jnp.float32)
    for c in range(chunks):
        p = jnp.exp2(s_ref[c] * EXP_SCALE - shift)
        total = total + jnp.sum(p, axis=0, keepdims=True)
        p16 = p.astype(jnp.bfloat16)
        p_ref[c] = p16
        out_t = out_t + dot(load_vt(c), p16, NN)
    inverse = live / total
    out_t = out_t * inverse
    up_t = up.astype(jnp.float32).T
    scaled = up_t * (weight / total)
    delta = jnp.sum(scaled * out_t, axis=0, keepdims=True)
    scaled16 = scaled.astype(jnp.bfloat16)
    dq_t = jnp.zeros((DH, rows), jnp.float32)
    for c in range(chunks):
        p16 = p_ref[c]
        gp = dot(load_v(c), scaled16, NN)
        ds = (p16.astype(jnp.float32) * (gp - delta)).astype(jnp.bfloat16)
        add_dv(c, dot(p16, scaled16, NT))
        add_dk(c, dot(ds, q, NN))
        dq_t = dq_t + dot(load_kt(c), ds, NN)
    return out_t.T, (dq_t * SCALE).T


def attention_kernel(chunk, q_ref, up_ref, kv_ref, kvt_ref, rows_ref, live_ref, o_ref, dq_ref, dkv_ref, s_ref, p_ref):
    i = pl.program_id(1)
    tiles = pl.num_programs(1)
    tokens = q_ref.shape[0]
    rows = tokens * q_ref.shape[2]
    window = s_ref.shape[0] * chunk
    chunks = s_ref.shape[0]
    b = i // (tiles // 2)

    @pl.when(i == 0)
    def _():
        dkv_ref[...] = jnp.zeros_like(dkv_ref)

    q = q_ref[:, 0].astype(jnp.float32).reshape(rows, DH).astype(jnp.bfloat16)
    up = up_ref[:, 0].astype(jnp.float32).reshape(rows, DH)
    start = rows_ref[0, pl.ds(i, 1), :]
    token = rows_ref[1, pl.ds(i, 1), :]
    live = live_ref[0, pl.ds(i, 1), :]
    weight = live_ref[1, pl.ds(i, 1), :]
    off = pl.multiple_of(b * BLK, BLK)

    def rows_of(c):
        return pl.ds(pl.multiple_of(off + c * chunk, BLK), chunk)

    def add(which):
        def one(c, value):
            dkv_ref[0, which, rows_of(c), :] += value

        return one

    out, dq = attend_tile(
        q, up, start, token, live, weight,
        lambda c: kv_ref[0, 0, rows_of(c), :],
        lambda c: kv_ref[0, 1, rows_of(c), :],
        lambda c: kvt_ref[0, 0, :, rows_of(c)],
        lambda c: kvt_ref[0, 1, :, rows_of(c)],
        add(0), add(1), s_ref, p_ref, chunk, chunks, off,
    )
    o_ref[:, 0] = out.reshape(tokens, -1, DH).astype(jnp.bfloat16)
    dq_ref[:, 0] = dq.reshape(tokens, -1, DH).astype(jnp.bfloat16)

    @pl.when(i == tiles - 1)
    def _():
        dkv_ref[0, 0] = dkv_ref[0, 0] * SCALE


def attention(q, up, kv, rows_i, rows_f):
    tokens, kv_count, per, _ = q.shape
    window = kv.shape[2]
    tile = 256 // per
    tiles = tokens // tile
    chunk = 256
    chunks = (window - BLK) // chunk
    kvt = kv.transpose(0, 1, 3, 2)
    return pl.pallas_call(
        functools.partial(attention_kernel, chunk),
        grid=(kv_count, tiles),
        in_specs=[
            pl.BlockSpec((tile, 1, per, DH), lambda g, i: (i, g, 0, 0)),
            pl.BlockSpec((tile, 1, per, DH), lambda g, i: (i, g, 0, 0)),
            pl.BlockSpec((1, 2, window, DH), lambda g, i: (g, 0, 0, 0)),
            pl.BlockSpec((1, 2, DH, window), lambda g, i: (g, 0, 0, 0)),
            pl.BlockSpec((2, tiles, tile * per), lambda g, i: (0, 0, 0)),
            pl.BlockSpec((2, tiles, tile * per), lambda g, i: (0, 0, 0)),
        ],
        out_specs=[
            pl.BlockSpec((tile, 1, per, DH), lambda g, i: (i, g, 0, 0)),
            pl.BlockSpec((tile, 1, per, DH), lambda g, i: (i, g, 0, 0)),
            pl.BlockSpec((1, 2, window, DH), lambda g, i: (g, 0, 0, 0)),
        ],
        out_shape=[
            jax.ShapeDtypeStruct(q.shape, jnp.bfloat16),
            jax.ShapeDtypeStruct(q.shape, jnp.bfloat16),
            jax.ShapeDtypeStruct(kv.shape, jnp.float32),
        ],
        scratch_shapes=[
            pltpu.VMEM((chunks, chunk, tile * per), jnp.float32),
            pltpu.VMEM((chunks, chunk, tile * per), jnp.bfloat16),
        ],
        compiler_params=pltpu.CompilerParams(vmem_limit_bytes=48 * 1024 * 1024),
    )(q, up, kv, kvt, rows_i, rows_f)


def row_tables(rewards, response_length, block_start, move_plan, own_group, own_seq, tokens, per):
    groups = rewards.shape[0]
    shorts = SHORTS
    advantage = rewards - jnp.mean(rewards, axis=1, keepdims=True)
    arrived = move_plan[:, :shorts] == own_group
    pick = arrived.astype(jnp.float32)
    short_len = jnp.sum(jnp.where(arrived, response_length[:, :shorts], 0), axis=0)
    short_adv = jnp.sum(jnp.where(arrived, advantage[:, :shorts], 0.0), axis=0)
    mine = (jnp.arange(groups) == own_group)[:, None]
    long_start = jnp.sum(jnp.where(mine, block_start[:, shorts:], 0), axis=0) * BLK
    long_len = jnp.sum(jnp.where(mine, response_length[:, shorts:], 0), axis=0)
    long_adv = jnp.sum(jnp.where(mine, advantage[:, shorts:], 0.0), axis=0)
    starts = jnp.concatenate([jnp.arange(shorts, dtype=jnp.int32) * BLK, long_start])
    lens = jnp.concatenate([short_len, long_len])
    advs = jnp.concatenate([short_adv, long_adv])
    position = own_seq * tokens + jnp.arange(tokens, dtype=jnp.int32)
    inside = (position[None, :] >= starts[:, None]) & (position[None, :] < (starts + lens)[:, None])
    live = jnp.any(inside, axis=0)
    start = jnp.sum(jnp.where(inside, starts[:, None], 0), axis=0)
    weight = jnp.sum(jnp.where(inside, advs[:, None], 0.0), axis=0)
    return position, live, start, weight


def shift_pairs(first, last, step):
    if step > 0:
        return [(s, s + 1) for s in range(first, last)]
    return [(s + 1, s) for s in range(first, last)]


def body(queries, keys, values, upstream, rewards, response_length, block_start, move_plan):
    groups = lax.axis_size("dp")
    seq_count = lax.axis_size("seq")
    own_group = lax.axis_index("dp")
    own_seq = lax.axis_index("seq")
    tokens, heads, _ = queries.shape
    kv_count = keys.shape[1]
    per = heads // kv_count
    here = tokens // BLK
    short_rows = SHORTS // here
    piece = BLK // groups

    packed = jnp.concatenate([queries, keys, values], axis=1)
    width = packed.shape[1]
    first = packed.reshape(here, groups, piece, width, DH).transpose(1, 0, 2, 3, 4)
    first = lax.all_to_all(first, "dp", split_axis=0, concat_axis=0, tiled=True)
    slots = jnp.minimum(own_seq * here, SHORTS - here) + jnp.arange(here)
    chosen = jnp.take(move_plan, slots, axis=1)
    every = jnp.arange(groups, dtype=jnp.int32)
    source = jnp.sum(jnp.where(chosen[:, None, :] == every[None, :, None], every[:, None, None], 0), axis=0)
    second = jnp.stack([jnp.take(first[:, n], source[:, n], axis=0) for n in range(here)], axis=1)
    second = lax.all_to_all(second, "dp", split_axis=0, concat_axis=0, tiled=True)
    moved = second.transpose(1, 0, 2, 3, 4).reshape(tokens, width, DH)
    bal = jnp.where(own_seq < short_rows, moved, packed)
    q = bal[:, :heads].reshape(tokens, kv_count, per, DH)
    up = upstream.reshape(tokens, kv_count, per, DH)
    own = bal[:, heads:].reshape(tokens, 2, kv_count, DH).transpose(2, 1, 0, 3)

    ahead = shift_pairs(short_rows, seq_count - 1, 1)
    back = shift_pairs(short_rows, seq_count - 1, -1)
    one = lax.ppermute(own, "seq", ahead)
    two = lax.ppermute(one, "seq", ahead)
    three = lax.ppermute(two, "seq", ahead)
    four = lax.ppermute(three[:, :, BLK:], "seq", ahead)
    window = jnp.concatenate([four, three, two, one, own], axis=2)

    position, live, start, weight = row_tables(
        rewards, response_length, block_start, move_plan, own_group, own_seq, tokens, per
    )
    before = window.shape[2] - tokens
    base = own_seq * tokens - before
    start_w = jnp.where(live, start - base, NEVER)
    token_w = position - base
    tiles = tokens * per // 256
    rows_i = jnp.stack([jnp.repeat(start_w, per), jnp.repeat(token_w, per)]).reshape(2, tiles, 256)
    rows_f = jnp.stack([jnp.repeat(live.astype(jnp.float32), per), jnp.repeat(weight, per)]).reshape(2, tiles, 256)
    out, dq, part = attention(q, up, window, rows_i, rows_f)

    def send(x):
        return lax.ppermute(x.astype(jnp.bfloat16), "seq", back).astype(jnp.float32)

    farthest = send(part[:, :, :BLK])
    a3 = part[:, :, BLK : 3 * BLK] + jnp.pad(farthest, ((0, 0), (0, 0), (BLK, 0), (0, 0)))
    a2 = part[:, :, 3 * BLK : 5 * BLK] + send(a3)
    a1 = part[:, :, 5 * BLK : 7 * BLK] + send(a2)
    a0 = part[:, :, 7 * BLK :] + send(a1)
    grads = a0.astype(jnp.bfloat16).transpose(1, 2, 0, 3)
    return (out.reshape(queries.shape), dq.reshape(queries.shape), grads[0], grads[1])


def solution(mesh):
    spec = P(("dp", "seq"), None, None)
    return jax.shard_map(
        body,
        mesh=mesh,
        in_specs=(spec,) * 4 + (P(),) * 4,
        out_specs=(spec,) * 4,
        check_vma=False,
    )
```

```python
import functools

import jax
import jax.numpy as jnp
from jax import lax
from jax.experimental import pallas as pl
from jax.experimental.pallas import tpu as pltpu
from jax.sharding import PartitionSpec as P

DH = 128
BLK = 128
SHORTS = 8
WINDOW = 9 * BLK
OWN = 7 * BLK
TILE = 256
CHUNK = 256
NEVER = 1 << 20
SCALE = DH**-0.5
EXP_SCALE = SCALE * 1.4426950408889634
NT = (((1,), (1,)), ((), ()))
NN = (((1,), (0,)), ((), ()))
MESH = pl.DeviceIdType.MESH


def dot(a, b, dims):
    return lax.dot_general(a, b, dims, preferred_element_type=jnp.float32)


def attend_tile(q, up, start, token, live, weight, k, v, kt, vt, add_dk, add_dv, s_ref, p_ref, key0, chunk, chunks):
    rows = q.shape[0]
    highest = jnp.full((1, rows), -1e30, jnp.float32)
    for c in range(chunks):
        s = dot(k(c), q, NT)
        key = key0 + c * chunk + lax.broadcasted_iota(jnp.int32, (chunk, rows), 0)
        allowed = key >= start
        if c == chunks - 1:
            allowed = allowed & (key <= token)
        s = jnp.where(allowed, s, -1e30)
        s_ref[c, :chunk] = s
        highest = jnp.maximum(highest, jnp.max(s, axis=0, keepdims=True))
    shift = highest * EXP_SCALE
    total = jnp.zeros((1, rows), jnp.float32)
    out_t = jnp.zeros((DH, rows), jnp.float32)
    for c in range(chunks):
        p = jnp.exp2(s_ref[c, :chunk] * EXP_SCALE - shift)
        total = total + jnp.sum(p, axis=0, keepdims=True)
        p16 = p.astype(jnp.bfloat16)
        p_ref[c, :chunk] = p16
        out_t = out_t + dot(vt(c), p16, NN)
    out_t = out_t * (live / total)
    scaled = up.astype(jnp.float32).T * (weight / total)
    delta = jnp.sum(scaled * out_t, axis=0, keepdims=True)
    scaled16 = scaled.astype(jnp.bfloat16)
    dq_t = jnp.zeros((DH, rows), jnp.float32)
    for c in range(chunks):
        p16 = p_ref[c, :chunk]
        gp = dot(v(c), scaled16, NN)
        ds = (p16.astype(jnp.float32) * (gp - delta)).astype(jnp.bfloat16)
        add_dv(c, dot(p16, scaled16, NT))
        add_dk(c, dot(ds, q, NN))
        dq_t = dq_t + dot(kt(c), ds, NN)
    return out_t.T, (dq_t * SCALE).T


def kernel(groups, seq_count, short_rows, q_hbm, up_hbm, kv_hbm, src_ref, rows_i, rows_f, o_ref, dq_ref, dkv_ref,
           q_v, up_v, kw, kt, dkv, s_ref, p_ref, sbuf, rbuf,
           r1q0, r1q1, s2q0, s2q1, r1k0, r1k1, s2k0, s2k1,
           load_sem, gather_send, gather_recv, chain_send, chain_recv, x_send, x_recv):
    seq = lax.axis_index("seq")
    dp = lax.axis_index("dp")
    tokens, kv_count, per, _ = q_v.shape
    step_tokens = TILE // per
    tiles = tokens // step_tokens
    here = tokens // BLK
    is_long = seq >= short_rows
    has_prev = seq > short_rows
    has_next = (seq >= short_rows) & (seq < seq_count - 1)

    barrier = pltpu.get_barrier_semaphore()

    @pl.when(has_prev)
    def _():
        pl.semaphore_signal(barrier, inc=1, device_id={"seq": seq - 1}, device_id_type=MESH)

    @pl.when(has_next)
    def _():
        pl.semaphore_signal(barrier, inc=1, device_id={"seq": seq + 1}, device_id_type=MESH)

    @pl.when(jnp.logical_not(is_long))
    def _():
        def greet(r, _):
            pl.semaphore_signal(barrier, inc=1, device_id={"dp": lax.rem(dp + r, groups)}, device_id_type=MESH)
            return 0

        lax.fori_loop(1, groups, greet, 0)
        pl.semaphore_wait(barrier, groups - 1)

    @pl.when(has_prev & has_next)
    def _():
        pl.semaphore_wait(barrier, 2)

    @pl.when(has_prev != has_next)
    def _():
        pl.semaphore_wait(barrier, 1)

    def tile(g, i, k, v, kt_of, vt_of, add_dk, add_dv, key0, chunk, chunks):
        spot = pl.ds(pl.multiple_of(i * step_tokens, step_tokens), step_tokens)
        q = q_v[spot, g].astype(jnp.float32).reshape(TILE, DH).astype(jnp.bfloat16)
        up = up_v[spot, g].astype(jnp.float32).reshape(TILE, DH)
        out, dq = attend_tile(
            q, up, rows_i[0, pl.ds(i, 1), :], rows_i[1, pl.ds(i, 1), :], rows_f[0, pl.ds(i, 1), :], rows_f[1, pl.ds(i, 1), :],
            k, v, kt_of, vt_of, add_dk, add_dv, s_ref, p_ref, key0, chunk, chunks,
        )
        o_ref[spot, g] = out.reshape(step_tokens, per, DH).astype(jnp.bfloat16)
        dq_ref[spot, g] = dq.reshape(step_tokens, per, DH).astype(jnp.bfloat16)

    up_load = pltpu.make_async_copy(up_hbm, up_v, load_sem.at[0])
    up_load.start()

    @pl.when(is_long)
    def _():
        q_load = pltpu.make_async_copy(q_hbm, q_v, load_sem.at[1])
        kv_load = pltpu.make_async_copy(kv_hbm, kw.at[:, :, pl.ds(OWN, tokens)], load_sem.at[2])
        kv_load.start()
        q_load.start()

        @pl.when(jnp.logical_not(has_prev))
        def _():
            kw[:, :, :OWN] = jnp.zeros((kv_count, 2, OWN, DH), kw.dtype)

        kv_load.wait()
        hop_from = (OWN, OWN - tokens, OWN - 2 * tokens, BLK * 2)
        hop_to = (OWN - tokens, OWN - 2 * tokens, OWN - 3 * tokens, 0)
        hop_rows = (tokens, tokens, tokens, BLK)

        def gather(g, k):
            return pltpu.make_async_remote_copy(
                src_ref=kw.at[g, :, pl.ds(hop_from[k], hop_rows[k])],
                dst_ref=kw.at[g, :, pl.ds(hop_to[k], hop_rows[k])],
                send_sem=gather_send.at[g, k],
                recv_sem=gather_recv.at[g, k],
                device_id={"seq": seq + 1},
                device_id_type=MESH,
            )

        def gather_arrived(g, k, when=True):
            @pl.when(has_prev & when)
            def _():
                gather(g, k).wait_recv()

        def gather_step(g, k, when=True):
            if k > 0:
                gather_arrived(g, k - 1, when)

            @pl.when(has_next & when)
            def _():
                gather(g, k).start()

        part_at = (0, BLK, 3 * BLK, 5 * BLK, 7 * BLK)
        part_rows = (BLK, tokens, tokens, tokens, tokens)

        def chain(g, k):
            return pltpu.make_async_remote_copy(
                src_ref=sbuf.at[g, k, :, pl.ds(0, part_rows[k])],
                dst_ref=rbuf.at[g, k, :, pl.ds(0, part_rows[k])],
                send_sem=chain_send.at[g, k],
                recv_sem=chain_recv.at[g, k],
                device_id={"seq": seq - 1},
                device_id_type=MESH,
            )

        def chain_step(g, k, when=True):
            if k > 0:
                @pl.when(has_next & when)
                def _():
                    chain(g, k - 1).wait_recv()
                    got = part_rows[k - 1]
                    at = pl.ds(part_at[k] + tokens - got, got)
                    dkv[g, :, at] += rbuf[g, k - 1, :, :got].astype(jnp.float32)

            if k < 4:
                @pl.when(has_prev & when)
                def _():
                    sbuf[g, k, :, : part_rows[k]] = dkv[g, :, pl.ds(part_at[k], part_rows[k])].astype(jnp.bfloat16)
                    chain(g, k).start()
            else:
                @pl.when(when)
                def _():
                    dkv_ref[g, 0] = (dkv[g, 0, pl.ds(OWN, tokens)] * SCALE).astype(jnp.bfloat16)
                    dkv_ref[g, 1] = dkv[g, 1, pl.ds(OWN, tokens)].astype(jnp.bfloat16)

        gather_step(0, 0)
        gather_step(0, 1)
        gather_step(0, 2)
        gather_step(1, 0)
        gather_step(0, 3)
        gather_step(1, 1)
        dkv[...] = jnp.zeros_like(dkv)
        q_load.wait()
        up_load.wait()
        gather_arrived(0, 3)

        def turn(t, _):
            g = t // tiles
            i = lax.rem(t, tiles)

            @pl.when(i == 0)
            def _():
                kt[0] = kw[g, 0].T
                kt[1] = kw[g, 1].T

            before, after, later = jnp.maximum(g - 1, 0), jnp.minimum(g + 1, kv_count - 1), jnp.minimum(g + 2, kv_count - 1)
            for k in range(1, 5):
                chain_step(before, k, (g > 0) & (i == 2 * k - 1))
            gather_step(after, 2, (g < kv_count - 1) & (i == 1))
            gather_step(later, 0, (g < kv_count - 2) & (i == 1))
            gather_step(after, 3, (g < kv_count - 1) & (i == 4))
            gather_step(later, 1, (g < kv_count - 2) & (i == 4))

            off = pl.multiple_of((i // (tiles // here)) * BLK, BLK)

            def at(c):
                return pl.ds(pl.multiple_of(off + c * CHUNK, BLK), CHUNK)

            def add(which):
                def one(c, value):
                    dkv[g, which, at(c)] += value

                return one

            tile(g, i, lambda c: kw[g, 0, at(c)], lambda c: kw[g, 1, at(c)], lambda c: kt[0, :, at(c)], lambda c: kt[1, :, at(c)],
                 add(0), add(1), off, CHUNK, (WINDOW - BLK) // CHUNK)

            chain_step(g, 0, i == tiles - 1)
            gather_arrived(after, 3, (g < kv_count - 1) & (i == tiles - 1))
            return 0

        lax.fori_loop(0, kv_count * tiles, turn, 0)
        for k in range(1, 5):
            chain_step(kv_count - 1, k)
        for g in range(kv_count):
            for k in range(4):
                @pl.when(has_next)
                def _():
                    gather(g, k).wait_send()

                @pl.when(has_prev)
                def _():
                    chain(g, k).wait_send()

    @pl.when(jnp.logical_not(is_long))
    def _():
        r1q, s2q, r1k, s2k = (r1q0, r1q1), (s2q0, s2q1), (r1k0, r1k1), (s2k0, s2k1)
        piece = BLK // groups
        parts = groups // (2 * kv_count)
        kv_piece = BLK // parts

        def kv_spot(ref, m, i):
            head = m // (2 * parts)
            which = lax.rem(m // parts, 2)
            return ref.at[head, which, pl.ds(pl.multiple_of(i * BLK + lax.rem(m, parts) * kv_piece, kv_piece), kv_piece)]

        def q_spot(ref, m, i):
            return ref.at[pl.ds(pl.multiple_of(i * BLK + m * piece, piece), piece)]

        def remote(src, dst, n, d):
            return pltpu.make_async_remote_copy(
                src_ref=src, dst_ref=dst, send_sem=x_send.at[n], recv_sem=x_recv.at[n], device_id={"dp": d}, device_id_type=MESH
            )

        for i in range(here):
            pltpu.make_async_copy(q_spot(q_hbm, dp, i), r1q[i].at[dp], x_recv.at[4 * i]).start()
            pltpu.make_async_copy(kv_spot(kv_hbm, dp, i), r1k[i].at[dp], x_recv.at[4 * i + 1]).start()

            def spread(r, _):
                d = lax.rem(dp + r, groups)
                remote(q_spot(q_hbm, d, i), r1q[i].at[dp], 4 * i, d).start()
                remote(kv_spot(kv_hbm, d, i), r1k[i].at[dp], 4 * i + 1, d).start()
                return 0

            lax.fori_loop(1, groups, spread, 0)

        for i in range(here):
            pltpu.make_async_copy(r1q[i], r1q[i], x_recv.at[4 * i]).wait()
            pltpu.make_async_copy(r1k[i], r1k[i], x_recv.at[4 * i + 1]).wait()

            def relay(r, _):
                d = lax.rem(dp + r, groups)
                source = src_ref[i, d]
                s2q[i][d] = r1q[i][source]
                s2k[i][d] = r1k[i][source]
                remote(s2q[i].at[d], q_spot(q_v, dp, i), 4 * i + 2, d).start()
                remote(s2k[i].at[d], kv_spot(kw, dp, i), 4 * i + 3, d).start()
                return 0

            lax.fori_loop(1, groups, relay, 0)
            source = src_ref[i, dp]
            q_v[pl.ds(pl.multiple_of(i * BLK + dp * piece, piece), piece)] = r1q[i][source]
            mine = dp // (2 * parts), lax.rem(dp // parts, 2), pl.multiple_of(i * BLK + lax.rem(dp, parts) * kv_piece, kv_piece)
            kw[mine[0], mine[1], pl.ds(mine[2], kv_piece)] = r1k[i][source]

        up_load.wait()
        most = pl.ds(0, groups - 1)
        for i in range(here):
            pltpu.make_async_copy(s2q[i].at[most], s2q[i].at[most], x_recv.at[4 * i + 2]).wait()
            pltpu.make_async_copy(s2k[i].at[most], s2k[i].at[most], x_recv.at[4 * i + 3]).wait()
            at = pl.ds(i * BLK, BLK)
            share = tiles // here

            def small(t, _):
                g = t // share
                n = i * share + lax.rem(t, share)

                @pl.when(lax.rem(t, share) == 0)
                def _():
                    kt[0, :, :BLK] = kw[g, 0, at].T
                    kt[1, :, :BLK] = kw[g, 1, at].T
                    dkv[g, :, at] = jnp.zeros((2, BLK, DH), jnp.float32)

                def add(which):
                    def one(c, value):
                        dkv[g, which, at] += value

                    return one

                tile(g, n, lambda c: kw[g, 0, at], lambda c: kw[g, 1, at], lambda c: kt[0, :, :BLK], lambda c: kt[1, :, :BLK],
                     add(0), add(1), i * BLK, BLK, 1)

                @pl.when(lax.rem(t, share) == share - 1)
                def _():
                    dkv_ref[g, 0, at] = (dkv[g, 0, at] * SCALE).astype(jnp.bfloat16)
                    dkv_ref[g, 1, at] = dkv[g, 1, at].astype(jnp.bfloat16)

                return 0

            lax.fori_loop(0, kv_count * share, small, 0)
        for i in range(here):
            for phase in range(2):
                pltpu.make_async_copy(s2q[i].at[most], s2q[i].at[most], x_send.at[4 * i + 2 * phase]).wait()
                pltpu.make_async_copy(s2k[i].at[most], s2k[i].at[most], x_send.at[4 * i + 2 * phase + 1]).wait()


def attention(q, up, kv, source, rows_i, rows_f, groups, seq_count, short_rows):
    tokens, kv_count, per, _ = q.shape
    half = jnp.bfloat16
    piece = BLK // groups
    kv_piece = BLK // (groups // (2 * kv_count))
    any_spec = pl.BlockSpec(memory_space=pl.ANY)
    vmem = pl.BlockSpec(memory_space=pltpu.VMEM)
    q_pieces = pltpu.VMEM((groups, piece, kv_count, per, DH), half)
    kv_pieces = pltpu.VMEM((groups, kv_piece, DH), half)
    chunks = (WINDOW - BLK) // CHUNK
    return pl.pallas_call(
        functools.partial(kernel, groups, seq_count, short_rows),
        in_specs=[any_spec, any_spec, any_spec, pl.BlockSpec(memory_space=pltpu.SMEM), vmem, vmem],
        out_specs=[vmem, vmem, vmem],
        out_shape=[
            jax.ShapeDtypeStruct(q.shape, half),
            jax.ShapeDtypeStruct(q.shape, half),
            jax.ShapeDtypeStruct(kv.shape, half),
        ],
        scratch_shapes=[
            pltpu.VMEM(q.shape, half),
            pltpu.VMEM(q.shape, half),
            pltpu.VMEM((kv_count, 2, WINDOW, DH), half),
            pltpu.VMEM((2, DH, WINDOW), half),
            pltpu.VMEM((kv_count, 2, WINDOW, DH), jnp.float32),
            pltpu.VMEM((chunks, CHUNK, TILE), jnp.float32),
            pltpu.VMEM((chunks, CHUNK, TILE), half),
            pltpu.VMEM((kv_count, 4, 2, tokens, DH), half),
            pltpu.VMEM((kv_count, 4, 2, tokens, DH), half),
            q_pieces, q_pieces, q_pieces, q_pieces,
            kv_pieces, kv_pieces, kv_pieces, kv_pieces,
            pltpu.SemaphoreType.DMA((3,)),
            pltpu.SemaphoreType.DMA((kv_count, 4)),
            pltpu.SemaphoreType.DMA((kv_count, 4)),
            pltpu.SemaphoreType.DMA((kv_count, 4)),
            pltpu.SemaphoreType.DMA((kv_count, 4)),
            pltpu.SemaphoreType.DMA((8,)),
            pltpu.SemaphoreType.DMA((8,)),
        ],
        compiler_params=pltpu.CompilerParams(
            collective_id=0, has_side_effects=True, vmem_limit_bytes=52 * 1024 * 1024
        ),
    )(q, up, kv, source, rows_i, rows_f)


def row_tables(rewards, response_length, block_start, move_plan, own_group, position):
    groups = rewards.shape[0]
    advantage = rewards - jnp.mean(rewards, axis=1, keepdims=True)
    every = jnp.arange(groups, dtype=jnp.int32)[:, None]
    owner = jnp.concatenate([move_plan[:, :SHORTS], jnp.broadcast_to(every, (groups, rewards.shape[1] - SHORTS))], axis=1)
    mine = owner == own_group
    starts = jnp.sum(jnp.where(mine, block_start, 0), axis=0) * BLK
    ends = starts + jnp.sum(jnp.where(mine, response_length, 0), axis=0)
    advs = jnp.sum(jnp.where(mine, advantage, 0.0), axis=0)
    inside = (position[None, :] >= starts[:, None]) & (position[None, :] < ends[:, None])
    live = jnp.sum(inside.astype(jnp.float32), axis=0)
    start = jnp.sum(jnp.where(inside, starts[:, None], 0), axis=0)
    weight = jnp.sum(jnp.where(inside, advs[:, None], 0.0), axis=0)
    return live, start, weight


def body(queries, keys, values, upstream, rewards, response_length, block_start, move_plan):
    groups = lax.axis_size("dp")
    seq_count = lax.axis_size("seq")
    own_group = lax.axis_index("dp")
    own_seq = lax.axis_index("seq")
    tokens, heads, _ = queries.shape
    kv_count = keys.shape[1]
    per = heads // kv_count
    here = tokens // BLK
    short_rows = SHORTS // here

    slots = jnp.minimum(own_seq * here, SHORTS - here)
    chosen = lax.dynamic_slice_in_dim(move_plan, slots, here, axis=1)
    every = jnp.arange(groups, dtype=jnp.int32)
    source = jnp.sum(
        jnp.where(chosen.T[:, :, None] == every[None, None, :], every[None, :, None], 0), axis=1
    )

    tiles = tokens * per // TILE
    token = jnp.arange(tokens * per, dtype=jnp.int32) // per
    position = own_seq * tokens + token
    live, start, weight = row_tables(rewards, response_length, block_start, move_plan, own_group, position)
    base = own_seq * tokens - jnp.where(own_seq < short_rows, 0, OWN)
    start_w = jnp.where(live > 0, start - base, NEVER)
    rows_i = jnp.stack([start_w, position - base]).reshape(2, tiles, TILE)
    rows_f = jnp.stack([live, weight]).reshape(2, tiles, TILE)

    q = queries.reshape(tokens, kv_count, per, DH)
    up = upstream.reshape(tokens, kv_count, per, DH)
    kv = jnp.stack([keys, values]).transpose(2, 0, 1, 3)
    out, dq, grads = attention(q, up, kv, source, rows_i, rows_f, groups, seq_count, short_rows)
    grads = grads.transpose(1, 2, 0, 3)
    return (out.reshape(queries.shape), dq.reshape(queries.shape), grads[0], grads[1])


def solution(mesh):
    spec = P(("dp", "seq"), None, None)
    return jax.shard_map(
        body,
        mesh=mesh,
        in_specs=(spec,) * 4 + (P(),) * 4,
        out_specs=(spec,) * 4,
        check_vma=False,
    )
```

```python
import functools

import jax
import jax.numpy as jnp
from jax import lax
from jax.experimental import pallas as pl
from jax.experimental.pallas import tpu as pltpu
from jax.sharding import PartitionSpec as P

DH = 128
BLK = 128
SHORTS = 8
WINDOW = 9 * BLK
OWN = 7 * BLK
CHUNK = 256
NEVER = 1 << 20
SCALE = DH**-0.5
EXP_SCALE = SCALE * 1.4426950408889634
NT = (((1,), (1,)), ((), ()))
NN = (((1,), (0,)), ((), ()))
MESH = pl.DeviceIdType.MESH


def dot(a, b, dims):
    return lax.dot_general(a, b, dims, preferred_element_type=jnp.float32)


def attend_tile(q, up, start, token, live, weight, k, v, kt, vt, add_dk, add_dv, s_ref, p_ref, key0, chunk, chunks, hook):
    rows = q.shape[0]
    hook(0)
    highest = jnp.full((1, rows), -1e30, jnp.float32)
    for c in range(chunks):
        s = dot(k(c), q, NT)
        key = key0 + c * chunk + lax.broadcasted_iota(jnp.int32, (chunk, rows), 0)
        allowed = key >= start
        if c == chunks - 1:
            allowed = allowed & (key <= token)
        s = jnp.where(allowed, s, -1e30)
        s_ref[c, :chunk] = s
        highest = jnp.maximum(highest, jnp.max(s, axis=0, keepdims=True))
    hook(1)
    shift = highest * EXP_SCALE
    total = jnp.zeros((1, rows), jnp.float32)
    out_t = jnp.zeros((DH, rows), jnp.float32)
    for c in range(chunks):
        p = jnp.exp2(s_ref[c, :chunk] * EXP_SCALE - shift)
        total = total + jnp.sum(p, axis=0, keepdims=True)
        p16 = p.astype(jnp.bfloat16)
        p_ref[c, :chunk] = p16
        out_t = out_t + dot(vt(c), p16, NN)
    hook(2)
    out_t = out_t * (live / total)
    scaled = up.astype(jnp.float32).T * (weight / total)
    delta = jnp.sum(scaled * out_t, axis=0, keepdims=True)
    scaled16 = scaled.astype(jnp.bfloat16)
    dq_t = jnp.zeros((DH, rows), jnp.float32)
    for c in range(chunks):
        p16 = p_ref[c, :chunk]
        gp = dot(v(c), scaled16, NN)
        ds = (p16.astype(jnp.float32) * (gp - delta)).astype(jnp.bfloat16)
        add_dv(c, dot(p16, scaled16, NT))
        add_dk(c, dot(ds, q, NN))
        dq_t = dq_t + dot(kt(c), ds, NN)
    return out_t.T, (dq_t * SCALE).T


def kernel(groups, seq_count, short_rows, boundary, q_hbm, up_hbm, kv_hbm, reward_ref, length_ref, block_ref, plan_ref,
           o_ref, dq_ref, dkv_ref,
           q_v, up_v, kw, relay_v, kt, dkv, s_ref, p_ref, sbuf, rbuf,
           r1q0, r1q1, s2q0, s2q1, r1k0, r1k1, s2k0, s2k1, source_ref,
           load_sem, gather_send, gather_recv, relay_recv, chain_send, chain_recv, x_send, x_recv):
    seq = lax.axis_index("seq")
    dp = lax.axis_index("dp")
    tokens, kv_count, per, _ = q_v.shape
    tile_rows = BLK * per
    here = tokens // BLK
    rolls = reward_ref.shape[1]
    last = seq_count - 1
    is_long = seq >= short_rows
    has_prev = seq > short_rows
    has_next = is_long & (seq < last)
    is_edge = seq == boundary - 1
    is_relay = seq == last
    plain_next = has_next & jnp.logical_not(is_edge)

    barrier = pltpu.get_barrier_semaphore()

    def signal(seq_to):
        pl.semaphore_signal(barrier, inc=1, device_id={"seq": seq_to}, device_id_type=MESH)

    @pl.when(has_prev)
    def _():
        signal(seq - 1)

    @pl.when(has_next)
    def _():
        signal(seq + 1)

    @pl.when(is_edge | (seq == boundary))
    def _():
        signal(last)

    @pl.when(is_relay)
    def _():
        signal(boundary - 1)
        signal(boundary)

    @pl.when(jnp.logical_not(is_long))
    def _():
        def greet(r, _):
            pl.semaphore_signal(barrier, inc=1, device_id={"dp": lax.rem(dp + r, groups)}, device_id_type=MESH)
            return 0

        lax.fori_loop(1, groups, greet, 0)
        pl.semaphore_wait(barrier, groups - 1)

    three = is_edge | (seq == boundary) | is_relay

    @pl.when(three)
    def _():
        pl.semaphore_wait(barrier, 3)

    @pl.when(has_prev & has_next & jnp.logical_not(three))
    def _():
        pl.semaphore_wait(barrier, 2)

    @pl.when(is_long & jnp.logical_not(has_prev))
    def _():
        pl.semaphore_wait(barrier, 1)

    lane_token = lax.broadcasted_iota(jnp.int32, (1, tile_rows), 1) // per

    def row_mean(group):
        total = reward_ref[group, 0]
        for r in range(1, rolls):
            total = total + reward_ref[group, r]
        return total * (1.0 / rolls)

    def tile(g, i, start, token, live, weight, k, v, kt_of, vt_of, add_dk, add_dv, key0, chunk, chunks, hook):
        spot = pl.ds(pl.multiple_of(i * BLK, BLK), BLK)
        q = q_v[spot, g].astype(jnp.float32).reshape(tile_rows, DH).astype(jnp.bfloat16)
        up = up_v[spot, g].astype(jnp.float32).reshape(tile_rows, DH)
        out, dq = attend_tile(
            q, up, start, token, live, weight, k, v, kt_of, vt_of, add_dk, add_dv, s_ref, p_ref, key0, chunk, chunks, hook
        )
        o_ref[spot, g] = out.reshape(BLK, per, DH).astype(jnp.bfloat16)
        dq_ref[spot, g] = dq.reshape(BLK, per, DH).astype(jnp.bfloat16)

    up_load = pltpu.make_async_copy(up_hbm, up_v, load_sem.at[0])

    @pl.when(is_long)
    def _():
        q_load = pltpu.make_async_copy(q_hbm, q_v, load_sem.at[1])
        kv_load = pltpu.make_async_copy(kv_hbm, kw.at[:, :, pl.ds(OWN, tokens)], load_sem.at[2])
        kv_load.start()
        kv_load.wait()
        hop_from = (OWN, OWN - tokens, OWN - 2 * tokens, BLK * 2)
        hop_to = (OWN - tokens, OWN - 2 * tokens, OWN - 3 * tokens, 0)
        hop_rows = (tokens, tokens, tokens, BLK)

        def hop(src, dst, recv, seq_to, g, k):
            return pltpu.make_async_remote_copy(
                src_ref=src, dst_ref=dst, send_sem=gather_send.at[g, k], recv_sem=recv.at[g, k],
                device_id={"seq": seq_to}, device_id_type=MESH,
            )

        def gather(g, k):
            return hop(kw.at[g, :, pl.ds(hop_from[k], hop_rows[k])], kw.at[g, :, pl.ds(hop_to[k], hop_rows[k])],
                       gather_recv, seq + 1, g, k)

        def edge(g, k):
            return hop(kw.at[g, :, pl.ds(hop_from[k], hop_rows[k])], relay_v.at[g, :, pl.ds(hop_to[k], hop_rows[k])],
                       relay_recv, last, g, k)

        def relay(g, k):
            at = pl.ds(hop_to[k], hop_rows[k])
            return hop(relay_v.at[g, :, at], kw.at[g, :, at], gather_recv, boundary, g, k)

        def gather_arrived(g, k, when=True):
            @pl.when(has_prev & when)
            def _():
                gather(g, k).wait_recv()

        def gather_step(g, k, when=True):
            if k > 0:
                gather_arrived(g, k - 1, when)

            @pl.when(plain_next & when)
            def _():
                gather(g, k).start()

            @pl.when(is_edge & when)
            def _():
                edge(g, k).start()

        def relay_step(g, k, when=True):
            @pl.when(is_relay & when)
            def _():
                edge(g, k).wait_recv()
                relay(g, k).start()

        part_at = (0, BLK, 3 * BLK, 5 * BLK, 7 * BLK)
        part_rows = (BLK, tokens, tokens, tokens, tokens)

        def chain(g, k):
            return pltpu.make_async_remote_copy(
                src_ref=sbuf.at[g, k, :, pl.ds(0, part_rows[k])],
                dst_ref=rbuf.at[g, k, :, pl.ds(0, part_rows[k])],
                send_sem=chain_send.at[g, k],
                recv_sem=chain_recv.at[g, k],
                device_id={"seq": seq - 1},
                device_id_type=MESH,
            )

        def chain_step(g, k, when=True):
            if k > 0:
                @pl.when(has_next & when)
                def _():
                    chain(g, k - 1).wait_recv()
                    got = part_rows[k - 1]
                    at = pl.ds(part_at[k] + tokens - got, got)
                    dkv[g, :, at] += rbuf[g, k - 1, :, :got].astype(jnp.float32)

            if k < 4:
                @pl.when(has_prev & when)
                def _():
                    sbuf[g, k, :, : part_rows[k]] = dkv[g, :, pl.ds(part_at[k], part_rows[k])].astype(jnp.bfloat16)
                    chain(g, k).start()
            else:
                @pl.when(when)
                def _():
                    dkv_ref[g, 0] = (dkv[g, 0, pl.ds(OWN, tokens)] * SCALE).astype(jnp.bfloat16)
                    dkv_ref[g, 1] = dkv[g, 1, pl.ds(OWN, tokens)].astype(jnp.bfloat16)

        def clear_first():
            @pl.when(jnp.logical_not(has_prev))
            def _():
                kw[:, :, :OWN] = jnp.zeros((kv_count, 2, OWN, DH), kw.dtype)

        gather_step(0, 0)
        clear_first()
        q_load.start()
        up_load.start()
        dkv[...] = jnp.zeros_like(dkv)
        relay_step(0, 0)
        gather_step(0, 1)
        relay_step(0, 1)
        gather_step(0, 2)
        gather_step(1, 0)
        relay_step(0, 2)
        relay_step(1, 0)
        gather_step(0, 3)
        gather_step(1, 1)
        relay_step(0, 3)
        relay_step(1, 1)

        mean = row_mean(dp)
        first = [block_ref[dp, j] * BLK for j in range(SHORTS, rolls)]
        stop = [f + length_ref[dp, j] for f, j in zip(first, range(SHORTS, rolls))]
        gain = [reward_ref[dp, j] - mean for j in range(SHORTS, rolls)]
        base = seq * tokens - OWN

        q_load.wait()
        up_load.wait()
        gather_arrived(0, 3)

        def turn(t, _):
            g = t // here
            i = lax.rem(t, here)
            start_head, end_head = i == 0, i == here - 1
            g1, g2 = jnp.minimum(g + 1, kv_count - 1), jnp.minimum(g + 2, kv_count - 1)
            b1, b2 = jnp.maximum(g - 1, 0), jnp.maximum(g - 2, 0)
            more1, more2, done1, done2 = g < kv_count - 1, g < kv_count - 2, g > 0, g > 1

            def hook(p):
                if p == 0:
                    for n, at in enumerate((start_head, end_head)):
                        gather_step(g1, 2 + n, more1 & at)
                        gather_step(g2, n, more2 & at)
                    chain_step(b1, 1, done1 & start_head)
                    chain_step(b2, 3, done2 & start_head)
                    chain_step(g, 0, end_head)
                    chain_step(b1, 2, done1 & end_head)
                    chain_step(b2, 4, done2 & end_head)
                if p == 2:
                    for n, at in enumerate((start_head, end_head)):
                        relay_step(g1, 2 + n, more1 & at)
                        relay_step(g2, n, more2 & at)

            @pl.when(start_head)
            def _():
                kt[0] = kw[g, 0].T
                kt[1] = kw[g, 1].T

            off = pl.multiple_of(i * BLK, BLK)

            def at(c):
                return pl.ds(pl.multiple_of(off + c * CHUNK, BLK), CHUNK)

            def add(which):
                def one(c, value):
                    dkv[g, which, at(c)] += value

                return one

            token = OWN + i * BLK + lane_token
            start = jnp.full(token.shape, NEVER, jnp.int32)
            live = jnp.zeros(token.shape, jnp.float32)
            weight = jnp.zeros(token.shape, jnp.float32)
            for f, e, w in zip(first, stop, gain):
                inside = (token >= f - base) & (token < e - base)
                start = jnp.where(inside, f - base, start)
                live = jnp.where(inside, 1.0, live)
                weight = jnp.where(inside, w, weight)

            tile(g, i, start, token, live, weight,
                 lambda c: kw[g, 0, at(c)], lambda c: kw[g, 1, at(c)], lambda c: kt[0, :, at(c)], lambda c: kt[1, :, at(c)],
                 add(0), add(1), off, CHUNK, (WINDOW - BLK) // CHUNK, hook)
            gather_arrived(g1, 3, more1 & end_head)
            return 0

        lax.fori_loop(0, kv_count * here, turn, 0)
        final = kv_count - 1
        chain_step(final, 1)
        chain_step(final - 1, 3)
        chain_step(final, 2)
        chain_step(final - 1, 4)
        chain_step(final, 3)
        chain_step(final, 4)
        for g in range(kv_count):
            for k in range(4):
                @pl.when(has_next | is_relay)
                def _():
                    gather(g, k).wait_send()

                @pl.when(has_prev)
                def _():
                    chain(g, k).wait_send()

    @pl.when(jnp.logical_not(is_long))
    def _():
        r1q, s2q, r1k, s2k = (r1q0, r1q1), (s2q0, s2q1), (r1k0, r1k1), (s2k0, s2k1)
        piece = BLK // groups
        parts = groups // (2 * kv_count)
        kv_piece = BLK // parts

        def kv_spot(ref, m, i):
            head = m // (2 * parts)
            which = lax.rem(m // parts, 2)
            return ref.at[head, which, pl.ds(pl.multiple_of(i * BLK + lax.rem(m, parts) * kv_piece, kv_piece), kv_piece)]

        def q_spot(ref, m, i):
            return ref.at[pl.ds(pl.multiple_of(i * BLK + m * piece, piece), piece)]

        def remote(src, dst, n, d):
            return pltpu.make_async_remote_copy(
                src_ref=src, dst_ref=dst, send_sem=x_send.at[n], recv_sem=x_recv.at[n], device_id={"dp": d}, device_id_type=MESH
            )

        for i in range(here):
            pltpu.make_async_copy(q_spot(q_hbm, dp, i), r1q[i].at[dp], x_recv.at[4 * i]).start()
            pltpu.make_async_copy(kv_spot(kv_hbm, dp, i), r1k[i].at[dp], x_recv.at[4 * i + 1]).start()

            def spread(r, _):
                d = lax.rem(dp + r, groups)
                remote(q_spot(q_hbm, d, i), r1q[i].at[dp], 4 * i, d).start()
                remote(kv_spot(kv_hbm, d, i), r1k[i].at[dp], 4 * i + 1, d).start()
                return 0

            lax.fori_loop(1, groups, spread, 0)
        up_load.start()

        def plan(n, _):
            i = n // groups
            d = lax.rem(n, groups)
            found = jnp.int32(0)
            for s in range(groups):
                found = jnp.where(plan_ref[s, seq * here + i] == d, jnp.int32(s), found)
            source_ref[i, d] = found
            return 0

        lax.fori_loop(0, here * groups, plan, 0)

        for i in range(here):
            pltpu.make_async_copy(r1q[i], r1q[i], x_recv.at[4 * i]).wait()
            pltpu.make_async_copy(r1k[i], r1k[i], x_recv.at[4 * i + 1]).wait()

            def send_on(r, _):
                d = lax.rem(dp + r, groups)
                source = source_ref[i, d]
                s2q[i][d] = r1q[i][source]
                s2k[i][d] = r1k[i][source]
                remote(s2q[i].at[d], q_spot(q_v, dp, i), 4 * i + 2, d).start()
                remote(s2k[i].at[d], kv_spot(kw, dp, i), 4 * i + 3, d).start()
                return 0

            lax.fori_loop(1, groups, send_on, 0)
            source = source_ref[i, dp]
            q_v[pl.ds(pl.multiple_of(i * BLK + dp * piece, piece), piece)] = r1q[i][source]
            mine = dp // (2 * parts), lax.rem(dp // parts, 2), pl.multiple_of(i * BLK + lax.rem(dp, parts) * kv_piece, kv_piece)
            kw[mine[0], mine[1], pl.ds(mine[2], kv_piece)] = r1k[i][source]

        up_load.wait()
        most = pl.ds(0, groups - 1)
        for i in range(here):
            pltpu.make_async_copy(s2q[i].at[most], s2q[i].at[most], x_recv.at[4 * i + 2]).wait()
            pltpu.make_async_copy(s2k[i].at[most], s2k[i].at[most], x_recv.at[4 * i + 3]).wait()
            at = pl.ds(i * BLK, BLK)
            source = source_ref[i, dp]
            slot = seq * here + i
            gain = reward_ref[source, slot] - row_mean(source)
            inside = lane_token < length_ref[source, slot]
            live = jnp.where(inside, 1.0, 0.0)
            weight = jnp.where(inside, gain, 0.0)
            start = jnp.where(inside, 0, NEVER)

            def small(g, _):
                kt[0, :, :BLK] = kw[g, 0, at].T
                kt[1, :, :BLK] = kw[g, 1, at].T

                def keys_out(c, value):
                    dkv_ref[g, 0, at] = (value * SCALE).astype(jnp.bfloat16)

                def values_out(c, value):
                    dkv_ref[g, 1, at] = value.astype(jnp.bfloat16)

                tile(g, i, start, lane_token, live, weight,
                     lambda c: kw[g, 0, at], lambda c: kw[g, 1, at], lambda c: kt[0, :, :BLK], lambda c: kt[1, :, :BLK],
                     keys_out, values_out, 0, BLK, 1, lambda p: None)
                return 0

            lax.fori_loop(0, kv_count, small, 0)
        for i in range(here):
            for phase in range(2):
                pltpu.make_async_copy(s2q[i].at[most], s2q[i].at[most], x_send.at[4 * i + 2 * phase]).wait()
                pltpu.make_async_copy(s2k[i].at[most], s2k[i].at[most], x_send.at[4 * i + 2 * phase + 1]).wait()


def attention(q, up, kv, plans, groups, seq_count, short_rows):
    tokens, kv_count, per, _ = q.shape
    half = jnp.bfloat16
    piece = BLK // groups
    kv_piece = BLK // (groups // (2 * kv_count))
    tile_rows = BLK * per
    any_spec = pl.BlockSpec(memory_space=pl.ANY)
    vmem = pl.BlockSpec(memory_space=pltpu.VMEM)
    smem = pl.BlockSpec(memory_space=pltpu.SMEM)
    q_pieces = pltpu.VMEM((groups, piece, kv_count, per, DH), half)
    kv_pieces = pltpu.VMEM((groups, kv_piece, DH), half)
    per_hop = pltpu.SemaphoreType.DMA((kv_count, 4))
    chunks = (WINDOW - BLK) // CHUNK
    return pl.pallas_call(
        functools.partial(kernel, groups, seq_count, short_rows, seq_count // 2),
        in_specs=[any_spec, any_spec, any_spec, smem, smem, smem, smem],
        out_specs=[vmem, vmem, vmem],
        out_shape=[
            jax.ShapeDtypeStruct(q.shape, half),
            jax.ShapeDtypeStruct(q.shape, half),
            jax.ShapeDtypeStruct(kv.shape, half),
        ],
        scratch_shapes=[
            pltpu.VMEM(q.shape, half),
            pltpu.VMEM(q.shape, half),
            pltpu.VMEM((kv_count, 2, WINDOW, DH), half),
            pltpu.VMEM((kv_count, 2, OWN, DH), half),
            pltpu.VMEM((2, DH, WINDOW), half),
            pltpu.VMEM((kv_count, 2, WINDOW, DH), jnp.float32),
            pltpu.VMEM((chunks, CHUNK, tile_rows), jnp.float32),
            pltpu.VMEM((chunks, CHUNK, tile_rows), half),
            pltpu.VMEM((kv_count, 4, 2, tokens, DH), half),
            pltpu.VMEM((kv_count, 4, 2, tokens, DH), half),
            q_pieces, q_pieces, q_pieces, q_pieces,
            kv_pieces, kv_pieces, kv_pieces, kv_pieces,
            pltpu.SMEM((tokens // BLK, groups), jnp.int32),
            pltpu.SemaphoreType.DMA((3,)),
            per_hop, per_hop, per_hop, per_hop, per_hop,
            pltpu.SemaphoreType.DMA((8,)),
            pltpu.SemaphoreType.DMA((8,)),
        ],
        compiler_params=pltpu.CompilerParams(
            collective_id=0, has_side_effects=True, vmem_limit_bytes=52 * 1024 * 1024
        ),
    )(q, up, kv, *plans)


def body(queries, keys, values, upstream, rewards, response_length, block_start, move_plan):
    groups = lax.axis_size("dp")
    seq_count = lax.axis_size("seq")
    tokens, heads, _ = queries.shape
    kv_count = keys.shape[1]
    per = heads // kv_count
    short_rows = SHORTS // (tokens // BLK)
    q = queries.reshape(tokens, kv_count, per, DH)
    up = upstream.reshape(tokens, kv_count, per, DH)
    kv = jnp.stack([keys, values]).transpose(2, 0, 1, 3)
    plans = (rewards, response_length, block_start, move_plan)
    out, dq, grads = attention(q, up, kv, plans, groups, seq_count, short_rows)
    grads = grads.transpose(1, 2, 0, 3)
    return (out.reshape(queries.shape), dq.reshape(queries.shape), grads[0], grads[1])


def solution(mesh):
    spec = P(("dp", "seq"), None, None)
    return jax.shard_map(
        body,
        mesh=mesh,
        in_specs=(spec,) * 4 + (P(),) * 4,
        out_specs=(spec,) * 4,
        check_vma=False,
    )
```

```python
import functools

import jax
import jax.numpy as jnp
from jax import lax
from jax.experimental import pallas as pl
from jax.experimental.pallas import tpu as pltpu
from jax.sharding import PartitionSpec as P

DH = 128
BLK = 128
SHORTS = 8
WINDOW = 9 * BLK
OWN = 7 * BLK
CHUNK = 256
NEVER = 1 << 20
SCALE = DH**-0.5
EXP_SCALE = SCALE * 1.4426950408889634
NT = (((1,), (1,)), ((), ()))
NN = (((1,), (0,)), ((), ()))
MESH = pl.DeviceIdType.MESH


def dot(a, b, dims):
    return lax.dot_general(a, b, dims, preferred_element_type=jnp.float32)


def attend_tile(q, up, start, token, live, weight, k, v, kt, vt, add_dk, add_dv, s_ref, p_ref, key0, chunk, chunks, hook):
    rows = q.shape[0]
    hook(0)
    highest = jnp.full((1, rows), -1e30, jnp.float32)
    for c in range(chunks):
        s = dot(k(c), q, NT)
        key = key0 + c * chunk + lax.broadcasted_iota(jnp.int32, (chunk, rows), 0)
        allowed = key >= start
        if c == chunks - 1:
            allowed = allowed & (key <= token)
        s = jnp.where(allowed, s, -1e30)
        s_ref[c, :chunk] = s
        highest = jnp.maximum(highest, jnp.max(s, axis=0, keepdims=True))
    hook(1)
    shift = highest * EXP_SCALE
    total = jnp.zeros((1, rows), jnp.float32)
    out_t = jnp.zeros((DH, rows), jnp.float32)
    for c in range(chunks):
        p = jnp.exp2(s_ref[c, :chunk] * EXP_SCALE - shift)
        total = total + jnp.sum(p, axis=0, keepdims=True)
        p16 = p.astype(jnp.bfloat16)
        p_ref[c, :chunk] = p16
        out_t = out_t + dot(vt(c), p16, NN)
    hook(2)
    out_t = out_t * (live / total)
    scaled = up.astype(jnp.float32).T * (weight / total)
    delta = jnp.sum(scaled * out_t, axis=0, keepdims=True)
    scaled16 = scaled.astype(jnp.bfloat16)
    dq_t = jnp.zeros((DH, rows), jnp.float32)
    for c in range(chunks):
        p16 = p_ref[c, :chunk]
        gp = dot(v(c), scaled16, NN)
        ds = (p16.astype(jnp.float32) * (gp - delta)).astype(jnp.bfloat16)
        add_dv(c, dot(p16, scaled16, NT))
        add_dk(c, dot(ds, q, NN))
        dq_t = dq_t + dot(kt(c), ds, NN)
        if c == 0:
            hook(3)
    return out_t.T, (dq_t * SCALE).T


def kernel(groups, seq_count, short_rows, boundary, q_hbm, up_hbm, kv_hbm, reward_ref, length_ref, block_ref, plan_ref,
           o_ref, dq_ref, dk_ref, dv_ref,
           q_v, up_v, kw, relay_v, kt, dkv, s_ref, p_ref, sbuf, rbuf,
           r1q0, r1q1, s2q0, s2q1, r1k0, r1k1, s2k0, s2k1, source_ref,
           load_sem, gather_send, gather_recv, relay_recv, chain_send, chain_recv, x_send, x_recv):
    seq = lax.axis_index("seq")
    dp = lax.axis_index("dp")
    tokens, kv_count, per, _ = q_v.shape
    tile_rows = BLK * per
    here = tokens // BLK
    rolls = reward_ref.shape[1]
    last = seq_count - 1
    is_long = seq >= short_rows
    has_prev = seq > short_rows
    has_next = is_long & (seq < last)
    is_edge = seq == boundary - 1
    is_relay = seq == last
    plain_next = has_next & jnp.logical_not(is_edge)

    barrier = pltpu.get_barrier_semaphore()

    def signal(seq_to):
        pl.semaphore_signal(barrier, inc=1, device_id={"seq": seq_to}, device_id_type=MESH)

    @pl.when(has_prev)
    def _():
        signal(seq - 1)

    @pl.when(has_next)
    def _():
        signal(seq + 1)

    @pl.when(is_edge | (seq == boundary))
    def _():
        signal(last)

    @pl.when(is_relay)
    def _():
        signal(boundary - 1)
        signal(boundary)

    @pl.when(jnp.logical_not(is_long))
    def _():
        def greet(r, _):
            pl.semaphore_signal(barrier, inc=1, device_id={"dp": lax.rem(dp + r, groups)}, device_id_type=MESH)
            return 0

        lax.fori_loop(1, groups, greet, 0)
        pl.semaphore_wait(barrier, groups - 1)

    three = is_edge | (seq == boundary) | is_relay

    @pl.when(three)
    def _():
        pl.semaphore_wait(barrier, 3)

    @pl.when(has_prev & has_next & jnp.logical_not(three))
    def _():
        pl.semaphore_wait(barrier, 2)

    @pl.when(is_long & jnp.logical_not(has_prev))
    def _():
        pl.semaphore_wait(barrier, 1)

    lane_token = lax.broadcasted_iota(jnp.int32, (1, tile_rows), 1) // per

    def row_mean(group):
        total = reward_ref[group, 0]
        for r in range(1, rolls):
            total = total + reward_ref[group, r]
        return total * (1.0 / rolls)

    def tile(g, i, start, token, live, weight, k, v, kt_of, vt_of, add_dk, add_dv, key0, chunk, chunks, hook):
        spot = pl.ds(pl.multiple_of(i * BLK, BLK), BLK)
        q = q_v[spot, g].astype(jnp.float32).reshape(tile_rows, DH).astype(jnp.bfloat16)
        up = up_v[spot, g].astype(jnp.float32).reshape(tile_rows, DH)
        out, dq = attend_tile(
            q, up, start, token, live, weight, k, v, kt_of, vt_of, add_dk, add_dv, s_ref, p_ref, key0, chunk, chunks, hook
        )
        o_ref[spot, g] = out.reshape(BLK, per, DH).astype(jnp.bfloat16)
        dq_ref[spot, g] = dq.reshape(BLK, per, DH).astype(jnp.bfloat16)

    up_load = pltpu.make_async_copy(up_hbm, up_v, load_sem.at[0])

    @pl.when(is_long)
    def _():
        q_load = pltpu.make_async_copy(q_hbm, q_v, load_sem.at[1])
        kv_load = pltpu.make_async_copy(kv_hbm, kw.at[:, :, pl.ds(OWN, tokens)], load_sem.at[2])
        kv_load.start()
        kv_load.wait()
        hop_from = (OWN, OWN - tokens, OWN - 2 * tokens, BLK * 2)
        hop_to = (OWN - tokens, OWN - 2 * tokens, OWN - 3 * tokens, 0)
        hop_rows = (tokens, tokens, tokens, BLK)

        def hop(src, dst, recv, seq_to, g, k, w):
            return pltpu.make_async_remote_copy(
                src_ref=src, dst_ref=dst, send_sem=gather_send.at[g, 2 * k + w], recv_sem=recv.at[g, 2 * k + w],
                device_id={"seq": seq_to}, device_id_type=MESH,
            )

        def gather(g, k, w):
            return hop(kw.at[g, w, pl.ds(hop_from[k], hop_rows[k])], kw.at[g, w, pl.ds(hop_to[k], hop_rows[k])],
                       gather_recv, seq + 1, g, k, w)

        def edge(g, k, w):
            return hop(kw.at[g, w, pl.ds(hop_from[k], hop_rows[k])], relay_v.at[g, w, pl.ds(hop_to[k], hop_rows[k])],
                       relay_recv, last, g, k, w)

        def relay(g, k, w):
            at = pl.ds(hop_to[k], hop_rows[k])
            return hop(relay_v.at[g, w, at], kw.at[g, w, at], gather_recv, boundary, g, k, w)

        def gather_arrived(g, k, w, when=True):
            @pl.when(has_prev & when)
            def _():
                gather(g, k, w).wait_recv()

        def gather_step(g, k, when=True):
            for w in range(2):
                if k > 0:
                    gather_arrived(g, k - 1, w, when)

                @pl.when(plain_next & when)
                def _():
                    gather(g, k, w).start()

                @pl.when(is_edge & when)
                def _():
                    edge(g, k, w).start()

        def relay_step(g, k, when=True):
            @pl.when(is_relay & when)
            def _():
                for w in range(2):
                    edge(g, k, w).wait_recv()
                    relay(g, k, w).start()

        part_at = (0, BLK, 3 * BLK, 5 * BLK, 7 * BLK)
        part_rows = (BLK, tokens, tokens, tokens, tokens)

        def chain(g, k, w):
            return pltpu.make_async_remote_copy(
                src_ref=sbuf.at[g, k, w, pl.ds(0, part_rows[k])],
                dst_ref=rbuf.at[g, k, w, pl.ds(0, part_rows[k])],
                send_sem=chain_send.at[g, 2 * k + w],
                recv_sem=chain_recv.at[g, 2 * k + w],
                device_id={"seq": seq - 1},
                device_id_type=MESH,
            )

        def chain_step(g, k, when=True):
            for w in range(2):
                if k > 0:
                    @pl.when(has_next & when)
                    def _():
                        chain(g, k - 1, w).wait_recv()
                        got = part_rows[k - 1]
                        at = pl.ds(part_at[k] + tokens - got, got)
                        dkv[g, w, at] += rbuf[g, k - 1, w, :got].astype(jnp.float32)

                if k < 4:
                    @pl.when(has_prev & when)
                    def _():
                        sbuf[g, k, w, : part_rows[k]] = dkv[g, w, pl.ds(part_at[k], part_rows[k])].astype(jnp.bfloat16)
                        chain(g, k, w).start()
                else:
                    @pl.when(when)
                    def _():
                        lanes = pl.ds(pl.multiple_of(g * DH, DH), DH)
                        total = dkv[g, w, pl.ds(OWN, tokens)]
                        if w == 0:
                            dk_ref[:, lanes] = (total * SCALE).astype(jnp.bfloat16)
                        else:
                            dv_ref[:, lanes] = total.astype(jnp.bfloat16)

        def clear_first():
            @pl.when(jnp.logical_not(has_prev))
            def _():
                kw[:, :, :OWN] = jnp.zeros((kv_count, 2, OWN, DH), kw.dtype)

        gather_step(0, 0)
        clear_first()
        q_load.start()
        up_load.start()
        dkv[...] = jnp.zeros_like(dkv)
        relay_step(0, 0)
        gather_step(0, 1)
        relay_step(0, 1)
        gather_step(0, 2)
        gather_step(1, 0)
        relay_step(0, 2)
        relay_step(1, 0)
        gather_step(0, 3)
        gather_step(1, 1)
        relay_step(0, 3)
        relay_step(1, 1)

        mean = row_mean(dp)
        first = [block_ref[dp, j] * BLK for j in range(SHORTS, rolls)]
        stop = [f + length_ref[dp, j] for f, j in zip(first, range(SHORTS, rolls))]
        gain = [reward_ref[dp, j] - mean for j in range(SHORTS, rolls)]
        base = seq * tokens - OWN

        q_load.wait()
        up_load.wait()
        gather_arrived(0, 3, 0)
        gather_arrived(0, 3, 1)

        def turn(t, _):
            g = t // here
            i = lax.rem(t, here)
            start_head, end_head = i == 0, i == here - 1
            g1, g2 = jnp.minimum(g + 1, kv_count - 1), jnp.minimum(g + 2, kv_count - 1)
            b1, b2 = jnp.maximum(g - 1, 0), jnp.maximum(g - 2, 0)
            more1, more2, done1, done2 = g < kv_count - 1, g < kv_count - 2, g > 0, g > 1

            def hook(p):
                if p == 0:
                    for n, at in enumerate((start_head, end_head)):
                        gather_step(g1, 2 + n, more1 & at)
                    relay_step(g2, 0, more2 & end_head)
                    chain_step(b2, 4, done2 & start_head)
                    chain_step(g, 0, end_head)
                if p == 1:
                    for n, at in enumerate((start_head, end_head)):
                        gather_step(g2, n, more2 & at)
                    chain_step(b1, 2, done1 & start_head)
                    chain_step(b1, 3, done1 & end_head)
                if p == 2:
                    for n, at in enumerate((start_head, end_head)):
                        relay_step(g1, 2 + n, more1 & at)
                if p == 3:
                    relay_step(g2, 1, more2 & end_head)
                    chain_step(g, 1, end_head)

            @pl.when(start_head)
            def _():
                kt[0] = kw[g, 0].T
                kt[1] = kw[g, 1].T

            off = pl.multiple_of(i * BLK, BLK)

            def at(c):
                return pl.ds(pl.multiple_of(off + c * CHUNK, BLK), CHUNK)

            def add(which):
                def one(c, value):
                    dkv[g, which, at(c)] += value

                return one

            token = OWN + i * BLK + lane_token
            start = jnp.full(token.shape, NEVER, jnp.int32)
            live = jnp.zeros(token.shape, jnp.float32)
            weight = jnp.zeros(token.shape, jnp.float32)
            for f, e, w in zip(first, stop, gain):
                inside = (token >= f - base) & (token < e - base)
                start = jnp.where(inside, f - base, start)
                live = jnp.where(inside, 1.0, live)
                weight = jnp.where(inside, w, weight)

            tile(g, i, start, token, live, weight,
                 lambda c: kw[g, 0, at(c)], lambda c: kw[g, 1, at(c)], lambda c: kt[0, :, at(c)], lambda c: kt[1, :, at(c)],
                 add(0), add(1), off, CHUNK, (WINDOW - BLK) // CHUNK, hook)
            gather_arrived(g1, 3, 0, more1 & end_head)
            gather_arrived(g1, 3, 1, more1 & end_head)
            return 0

        lax.fori_loop(0, kv_count * here, turn, 0)
        final = kv_count - 1
        chain_step(final, 2)
        chain_step(final - 1, 4)
        chain_step(final, 3)
        chain_step(final, 4)
        for g in range(kv_count):
            for k in range(4):
                for w in range(2):
                    @pl.when(has_next | is_relay)
                    def _():
                        gather(g, k, w).wait_send()

                    @pl.when(has_prev)
                    def _():
                        chain(g, k, w).wait_send()

    @pl.when(jnp.logical_not(is_long))
    def _():
        r1q, s2q, r1k, s2k = (r1q0, r1q1), (s2q0, s2q1), (r1k0, r1k1), (s2k0, s2k1)
        piece = BLK // groups
        parts = groups // (2 * kv_count)
        kv_piece = BLK // parts

        def kv_spot(ref, m, i):
            head = m // (2 * parts)
            which = lax.rem(m // parts, 2)
            return ref.at[head, which, pl.ds(pl.multiple_of(i * BLK + lax.rem(m, parts) * kv_piece, kv_piece), kv_piece)]

        def q_spot(ref, m, i):
            return ref.at[pl.ds(pl.multiple_of(i * BLK + m * piece, piece), piece)]

        def remote(src, dst, n, d):
            return pltpu.make_async_remote_copy(
                src_ref=src, dst_ref=dst, send_sem=x_send.at[n], recv_sem=x_recv.at[n], device_id={"dp": d}, device_id_type=MESH
            )

        for i in range(here):
            pltpu.make_async_copy(q_spot(q_hbm, dp, i), r1q[i].at[dp], x_recv.at[4 * i]).start()
            pltpu.make_async_copy(kv_spot(kv_hbm, dp, i), r1k[i].at[dp], x_recv.at[4 * i + 1]).start()

            def spread(r, _):
                d = lax.rem(dp + r, groups)
                remote(q_spot(q_hbm, d, i), r1q[i].at[dp], 4 * i, d).start()
                remote(kv_spot(kv_hbm, d, i), r1k[i].at[dp], 4 * i + 1, d).start()
                return 0

            lax.fori_loop(1, groups, spread, 0)
        up_load.start()

        def plan(n, _):
            i = n // groups
            d = lax.rem(n, groups)
            found = jnp.int32(0)
            for s in range(groups):
                found = jnp.where(plan_ref[s, seq * here + i] == d, jnp.int32(s), found)
            source_ref[i, d] = found
            return 0

        lax.fori_loop(0, here * groups, plan, 0)

        for i in range(here):
            pltpu.make_async_copy(r1q[i], r1q[i], x_recv.at[4 * i]).wait()
            pltpu.make_async_copy(r1k[i], r1k[i], x_recv.at[4 * i + 1]).wait()

            def send_on(r, _):
                d = lax.rem(dp + r, groups)
                source = source_ref[i, d]
                s2q[i][d] = r1q[i][source]
                s2k[i][d] = r1k[i][source]
                remote(s2q[i].at[d], q_spot(q_v, dp, i), 4 * i + 2, d).start()
                remote(s2k[i].at[d], kv_spot(kw, dp, i), 4 * i + 3, d).start()
                return 0

            lax.fori_loop(1, groups, send_on, 0)
            source = source_ref[i, dp]
            q_v[pl.ds(pl.multiple_of(i * BLK + dp * piece, piece), piece)] = r1q[i][source]
            mine = dp // (2 * parts), lax.rem(dp // parts, 2), pl.multiple_of(i * BLK + lax.rem(dp, parts) * kv_piece, kv_piece)
            kw[mine[0], mine[1], pl.ds(mine[2], kv_piece)] = r1k[i][source]

        up_load.wait()
        most = pl.ds(0, groups - 1)
        for i in range(here):
            pltpu.make_async_copy(s2q[i].at[most], s2q[i].at[most], x_recv.at[4 * i + 2]).wait()
            pltpu.make_async_copy(s2k[i].at[most], s2k[i].at[most], x_recv.at[4 * i + 3]).wait()
            at = pl.ds(i * BLK, BLK)
            source = source_ref[i, dp]
            slot = seq * here + i
            gain = reward_ref[source, slot] - row_mean(source)
            inside = lane_token < length_ref[source, slot]
            live = jnp.where(inside, 1.0, 0.0)
            weight = jnp.where(inside, gain, 0.0)
            start = jnp.where(inside, 0, NEVER)

            def small(g, _):
                kt[0, :, :BLK] = kw[g, 0, at].T
                kt[1, :, :BLK] = kw[g, 1, at].T
                lanes = pl.ds(pl.multiple_of(g * DH, DH), DH)

                def keys_out(c, value):
                    dk_ref[at, lanes] = (value * SCALE).astype(jnp.bfloat16)

                def values_out(c, value):
                    dv_ref[at, lanes] = value.astype(jnp.bfloat16)

                tile(g, i, start, lane_token, live, weight,
                     lambda c: kw[g, 0, at], lambda c: kw[g, 1, at], lambda c: kt[0, :, :BLK], lambda c: kt[1, :, :BLK],
                     keys_out, values_out, 0, BLK, 1, lambda p: None)
                return 0

            lax.fori_loop(0, kv_count, small, 0)
        for i in range(here):
            for phase in range(2):
                pltpu.make_async_copy(s2q[i].at[most], s2q[i].at[most], x_send.at[4 * i + 2 * phase]).wait()
                pltpu.make_async_copy(s2k[i].at[most], s2k[i].at[most], x_send.at[4 * i + 2 * phase + 1]).wait()


def attention(q, up, kv, plans, groups, seq_count, short_rows):
    tokens, kv_count, per, _ = q.shape
    half = jnp.bfloat16
    piece = BLK // groups
    kv_piece = BLK // (groups // (2 * kv_count))
    tile_rows = BLK * per
    any_spec = pl.BlockSpec(memory_space=pl.ANY)
    vmem = pl.BlockSpec(memory_space=pltpu.VMEM)
    smem = pl.BlockSpec(memory_space=pltpu.SMEM)
    q_pieces = pltpu.VMEM((groups, piece, kv_count, per, DH), half)
    kv_pieces = pltpu.VMEM((groups, kv_piece, DH), half)
    per_hop = pltpu.SemaphoreType.DMA((kv_count, 8))
    chunks = (WINDOW - BLK) // CHUNK
    return pl.pallas_call(
        functools.partial(kernel, groups, seq_count, short_rows, seq_count // 2),
        in_specs=[any_spec, any_spec, any_spec, smem, smem, smem, smem],
        out_specs=[vmem, vmem, vmem, vmem],
        out_shape=[
            jax.ShapeDtypeStruct(q.shape, half),
            jax.ShapeDtypeStruct(q.shape, half),
            jax.ShapeDtypeStruct((tokens, kv_count * DH), half),
            jax.ShapeDtypeStruct((tokens, kv_count * DH), half),
        ],
        scratch_shapes=[
            pltpu.VMEM(q.shape, half),
            pltpu.VMEM(q.shape, half),
            pltpu.VMEM((kv_count, 2, WINDOW, DH), half),
            pltpu.VMEM((kv_count, 2, OWN, DH), half),
            pltpu.VMEM((2, DH, WINDOW), half),
            pltpu.VMEM((kv_count, 2, WINDOW, DH), jnp.float32),
            pltpu.VMEM((chunks, CHUNK, tile_rows), jnp.float32),
            pltpu.VMEM((chunks, CHUNK, tile_rows), half),
            pltpu.VMEM((kv_count, 4, 2, tokens, DH), half),
            pltpu.VMEM((kv_count, 4, 2, tokens, DH), half),
            q_pieces, q_pieces, q_pieces, q_pieces,
            kv_pieces, kv_pieces, kv_pieces, kv_pieces,
            pltpu.SMEM((tokens // BLK, groups), jnp.int32),
            pltpu.SemaphoreType.DMA((3,)),
            per_hop, per_hop, per_hop, per_hop, per_hop,
            pltpu.SemaphoreType.DMA((8,)),
            pltpu.SemaphoreType.DMA((8,)),
        ],
        compiler_params=pltpu.CompilerParams(
            collective_id=0, has_side_effects=True, vmem_limit_bytes=52 * 1024 * 1024
        ),
    )(q, up, kv, *plans)


def body(queries, keys, values, upstream, rewards, response_length, block_start, move_plan):
    groups = lax.axis_size("dp")
    seq_count = lax.axis_size("seq")
    tokens, heads, _ = queries.shape
    kv_count = keys.shape[1]
    per = heads // kv_count
    short_rows = SHORTS // (tokens // BLK)
    q = queries.reshape(tokens, kv_count, per, DH)
    up = upstream.reshape(tokens, kv_count, per, DH)
    kv = jnp.stack([keys, values]).transpose(2, 0, 1, 3)
    plans = (rewards, response_length, block_start, move_plan)
    out, dq, dk, dv = attention(q, up, kv, plans, groups, seq_count, short_rows)
    return (out.reshape(queries.shape), dq.reshape(queries.shape), dk.reshape(keys.shape), dv.reshape(values.shape))


def solution(mesh):
    spec = P(("dp", "seq"), None, None)
    return jax.shard_map(
        body,
        mesh=mesh,
        in_specs=(spec,) * 4 + (P(),) * 4,
        out_specs=(spec,) * 4,
        check_vma=False,
    )
```

```python
import functools

import jax
import jax.numpy as jnp
from jax import lax
from jax.experimental import pallas as pl
from jax.experimental.pallas import tpu as pltpu
from jax.sharding import PartitionSpec as P

DH = 128
BLK = 128
SHORTS = 8
WINDOW = 9 * BLK
OWN = 7 * BLK
CHUNK = 256
NEVER = 1 << 20
SCALE = DH**-0.5
EXP_SCALE = SCALE * 1.4426950408889634
NT = (((1,), (1,)), ((), ()))
NN = (((1,), (0,)), ((), ()))
MESH = pl.DeviceIdType.MESH


def dot(a, b, dims):
    return lax.dot_general(a, b, dims, preferred_element_type=jnp.float32)


def attend_tile(q, up, start, token, live, weight, k, v, kt, vt, add_dk, add_dv, s_ref, p_ref, key0, chunk, chunks, hook):
    rows = q.shape[0]
    hook(0)
    highest = jnp.full((1, rows), -1e30, jnp.float32)
    for c in range(chunks):
        s = dot(k(c), q, NT)
        key = key0 + c * chunk + lax.broadcasted_iota(jnp.int32, (chunk, rows), 0)
        allowed = key >= start
        if c == chunks - 1:
            allowed = allowed & (key <= token)
        s = jnp.where(allowed, s, -1e30)
        s_ref[c, :chunk] = s
        highest = jnp.maximum(highest, jnp.max(s, axis=0, keepdims=True))
    hook(1)
    shift = highest * EXP_SCALE
    total = jnp.zeros((1, rows), jnp.float32)
    out_t = jnp.zeros((DH, rows), jnp.float32)
    for c in range(chunks):
        p = jnp.exp2(s_ref[c, :chunk] * EXP_SCALE - shift)
        total = total + jnp.sum(p, axis=0, keepdims=True)
        p16 = p.astype(jnp.bfloat16)
        p_ref[c, :chunk] = p16
        out_t = out_t + dot(vt(c), p16, NN)
    hook(2)
    out_t = out_t * (live / total)
    scaled = up.astype(jnp.float32).T * (weight / total)
    delta = jnp.sum(scaled * out_t, axis=0, keepdims=True)
    scaled16 = scaled.astype(jnp.bfloat16)
    dq_t = jnp.zeros((DH, rows), jnp.float32)
    for c in range(chunks):
        p16 = p_ref[c, :chunk]
        gp = dot(v(c), scaled16, NN)
        ds = (p16.astype(jnp.float32) * (gp - delta)).astype(jnp.bfloat16)
        add_dv(c, dot(p16, scaled16, NT))
        add_dk(c, dot(ds, q, NN))
        dq_t = dq_t + dot(kt(c), ds, NN)
        if c == 0:
            hook(3)
    return out_t.T, (dq_t * SCALE).T


def kernel(groups, seq_count, short_rows, boundary, q_hbm, up_hbm, kv_hbm, reward_ref, length_ref, block_ref, plan_ref,
           o_ref, dq_ref, dk_ref, dv_ref,
           q_v, up_v, kw, relay_v, kt, dkv, s_ref, p_ref, sbuf, rbuf,
           r1q0, r1q1, s2q0, s2q1, r1k0, r1k1, s2k0, s2k1, source_ref,
           load_sem, gather_send, gather_recv, relay_send, relay_recv, chain_send, chain_recv, x_send, x_recv):
    seq = lax.axis_index("seq")
    dp = lax.axis_index("dp")
    tokens, kv_count, per, _ = q_v.shape
    tile_rows = BLK * per
    here = tokens // BLK
    rolls = reward_ref.shape[1]
    last = seq_count - 1
    is_long = seq >= short_rows
    has_prev = seq > short_rows
    has_next = is_long & (seq < last)
    is_edge = seq == boundary - 1
    is_relay = seq == boundary
    twin = dp + 2 - 4 * lax.rem(dp // 2, 2)
    plain_next = has_next & jnp.logical_not(is_edge)

    barrier = pltpu.get_barrier_semaphore()

    def signal(seq_to):
        pl.semaphore_signal(barrier, inc=1, device_id={"seq": seq_to}, device_id_type=MESH)

    @pl.when(has_prev)
    def _():
        signal(seq - 1)

    @pl.when(has_next)
    def _():
        signal(seq + 1)

    def signal_twin(seq_to):
        pl.semaphore_signal(barrier, inc=1, device_id={"dp": twin, "seq": seq_to}, device_id_type=MESH)

    @pl.when(is_edge)
    def _():
        signal_twin(boundary)

    @pl.when(is_relay)
    def _():
        signal_twin(boundary - 1)
        signal_twin(boundary)

    @pl.when(jnp.logical_not(is_long))
    def _():
        def greet(r, _):
            pl.semaphore_signal(barrier, inc=1, device_id={"dp": lax.rem(dp + r, groups)}, device_id_type=MESH)
            return 0

        lax.fori_loop(1, groups, greet, 0)
        pl.semaphore_wait(barrier, groups - 1)

    @pl.when(is_relay)
    def _():
        pl.semaphore_wait(barrier, 4)

    @pl.when(is_edge)
    def _():
        pl.semaphore_wait(barrier, 3)

    @pl.when(has_prev & has_next & jnp.logical_not(is_edge | is_relay))
    def _():
        pl.semaphore_wait(barrier, 2)

    @pl.when(has_prev != has_next)
    def _():
        pl.semaphore_wait(barrier, 1)

    lane_token = lax.broadcasted_iota(jnp.int32, (1, tile_rows), 1) // per

    def row_mean(group):
        total = reward_ref[group, 0]
        for r in range(1, rolls):
            total = total + reward_ref[group, r]
        return total * (1.0 / rolls)

    def tile(g, i, start, token, live, weight, k, v, kt_of, vt_of, add_dk, add_dv, key0, chunk, chunks, hook):
        spot = pl.ds(pl.multiple_of(i * BLK, BLK), BLK)
        q = q_v[spot, g].astype(jnp.float32).reshape(tile_rows, DH).astype(jnp.bfloat16)
        up = up_v[spot, g].astype(jnp.float32).reshape(tile_rows, DH)
        out, dq = attend_tile(
            q, up, start, token, live, weight, k, v, kt_of, vt_of, add_dk, add_dv, s_ref, p_ref, key0, chunk, chunks, hook
        )
        o_ref[spot, g] = out.reshape(BLK, per, DH).astype(jnp.bfloat16)
        dq_ref[spot, g] = dq.reshape(BLK, per, DH).astype(jnp.bfloat16)

    up_load = pltpu.make_async_copy(up_hbm, up_v, load_sem.at[0])

    @pl.when(is_long)
    def _():
        q_load = pltpu.make_async_copy(q_hbm, q_v, load_sem.at[1])
        kv_load = pltpu.make_async_copy(kv_hbm, kw.at[:, :, pl.ds(OWN, tokens)], load_sem.at[2])
        kv_load.start()
        kv_load.wait()
        hop_from = (OWN, OWN - tokens, OWN - 2 * tokens, BLK * 2)
        hop_to = (OWN - tokens, OWN - 2 * tokens, OWN - 3 * tokens, 0)
        hop_rows = (tokens, tokens, tokens, BLK)

        def hop(src, dst, send, recv, device, g, k, w):
            return pltpu.make_async_remote_copy(
                src_ref=src, dst_ref=dst, send_sem=send.at[g, 2 * k + w], recv_sem=recv.at[g, 2 * k + w],
                device_id=device, device_id_type=MESH,
            )

        def gather(g, k, w):
            return hop(kw.at[g, w, pl.ds(hop_from[k], hop_rows[k])], kw.at[g, w, pl.ds(hop_to[k], hop_rows[k])],
                       gather_send, gather_recv, {"seq": seq + 1}, g, k, w)

        def edge(g, k, w):
            return hop(kw.at[g, w, pl.ds(hop_from[k], hop_rows[k])], relay_v.at[g, w, pl.ds(hop_to[k], hop_rows[k])],
                       gather_send, relay_recv, {"dp": twin, "seq": boundary}, g, k, w)

        def relay(g, k, w):
            at = pl.ds(hop_to[k], hop_rows[k])
            return hop(relay_v.at[g, w, at], kw.at[g, w, at], relay_send, gather_recv, {"dp": twin, "seq": boundary}, g, k, w)

        def gather_arrived(g, k, w, when=True):
            @pl.when(has_prev & when)
            def _():
                gather(g, k, w).wait_recv()

        def gather_step(g, k, when=True):
            for w in range(2):
                if k > 0:
                    gather_arrived(g, k - 1, w, when)

                @pl.when(plain_next & when)
                def _():
                    gather(g, k, w).start()

                @pl.when(is_edge & when)
                def _():
                    edge(g, k, w).start()

        def relay_step(g, k, when=True):
            @pl.when(is_relay & when)
            def _():
                for w in range(2):
                    edge(g, k, w).wait_recv()
                    relay(g, k, w).start()

        part_at = (0, BLK, 3 * BLK, 5 * BLK, 7 * BLK)
        part_rows = (BLK, tokens, tokens, tokens, tokens)

        def chain(g, k, w):
            return pltpu.make_async_remote_copy(
                src_ref=sbuf.at[g, k, w, pl.ds(0, part_rows[k])],
                dst_ref=rbuf.at[g, k, w, pl.ds(0, part_rows[k])],
                send_sem=chain_send.at[g, 2 * k + w],
                recv_sem=chain_recv.at[g, 2 * k + w],
                device_id={"seq": seq - 1},
                device_id_type=MESH,
            )

        def chain_step(g, k, when=True):
            for w in range(2):
                if k > 0:
                    @pl.when(has_next & when)
                    def _():
                        chain(g, k - 1, w).wait_recv()
                        got = part_rows[k - 1]
                        at = pl.ds(part_at[k] + tokens - got, got)
                        dkv[g, w, at] += rbuf[g, k - 1, w, :got].astype(jnp.float32)

                if k < 4:
                    @pl.when(has_prev & when)
                    def _():
                        sbuf[g, k, w, : part_rows[k]] = dkv[g, w, pl.ds(part_at[k], part_rows[k])].astype(jnp.bfloat16)
                        chain(g, k, w).start()
                else:
                    @pl.when(when)
                    def _():
                        total = dkv[g, w, pl.ds(OWN, tokens)]
                        if w == 0:
                            dk_ref[:, pl.ds(g, 1)] = (total * SCALE)[:, None]
                        else:
                            dv_ref[:, pl.ds(g, 1)] = total[:, None]

        def clear_first():
            @pl.when(jnp.logical_not(has_prev))
            def _():
                kw[:, :, :OWN] = jnp.zeros((kv_count, 2, OWN, DH), kw.dtype)

        gather_step(0, 0)
        clear_first()
        q_load.start()
        up_load.start()
        dkv[...] = jnp.zeros_like(dkv)
        relay_step(0, 0)
        gather_step(0, 1)
        relay_step(0, 1)
        gather_step(0, 2)
        gather_step(1, 0)
        relay_step(0, 2)
        relay_step(1, 0)
        gather_step(0, 3)
        gather_step(1, 1)
        relay_step(0, 3)
        relay_step(1, 1)

        mean = row_mean(dp)
        first = [block_ref[dp, j] * BLK for j in range(SHORTS, rolls)]
        stop = [f + length_ref[dp, j] for f, j in zip(first, range(SHORTS, rolls))]
        gain = [reward_ref[dp, j] - mean for j in range(SHORTS, rolls)]
        base = seq * tokens - OWN

        q_load.wait()
        up_load.wait()
        gather_arrived(0, 3, 0)
        gather_arrived(0, 3, 1)

        def turn(t, _):
            g = t // here
            i = lax.rem(t, here)
            start_head, end_head = i == 0, i == here - 1
            g1, g2 = jnp.minimum(g + 1, kv_count - 1), jnp.minimum(g + 2, kv_count - 1)
            b1, b2 = jnp.maximum(g - 1, 0), jnp.maximum(g - 2, 0)
            more1, more2, done1, done2 = g < kv_count - 1, g < kv_count - 2, g > 0, g > 1

            def hook(p):
                if p == 0:
                    for n, at in enumerate((start_head, end_head)):
                        gather_step(g1, 2 + n, more1 & at)
                    relay_step(g2, 0, more2 & end_head)
                    chain_step(b2, 4, done2 & start_head)
                    chain_step(g, 0, end_head)
                if p == 1:
                    for n, at in enumerate((start_head, end_head)):
                        gather_step(g2, n, more2 & at)
                    chain_step(b1, 2, done1 & start_head)
                    chain_step(b1, 3, done1 & end_head)
                if p == 2:
                    for n, at in enumerate((start_head, end_head)):
                        relay_step(g1, 2 + n, more1 & at)
                if p == 3:
                    relay_step(g2, 1, more2 & end_head)
                    chain_step(g, 1, end_head)

            @pl.when(start_head)
            def _():
                kt[0] = kw[g, 0].T
                kt[1] = kw[g, 1].T

            off = pl.multiple_of(i * BLK, BLK)

            def at(c):
                return pl.ds(pl.multiple_of(off + c * CHUNK, BLK), CHUNK)

            def add(which):
                def one(c, value):
                    dkv[g, which, at(c)] += value

                return one

            token = OWN + i * BLK + lane_token
            start = jnp.full(token.shape, NEVER, jnp.int32)
            live = jnp.zeros(token.shape, jnp.float32)
            weight = jnp.zeros(token.shape, jnp.float32)
            for f, e, w in zip(first, stop, gain):
                inside = (token >= f - base) & (token < e - base)
                start = jnp.where(inside, f - base, start)
                live = jnp.where(inside, 1.0, live)
                weight = jnp.where(inside, w, weight)

            tile(g, i, start, token, live, weight,
                 lambda c: kw[g, 0, at(c)], lambda c: kw[g, 1, at(c)], lambda c: kt[0, :, at(c)], lambda c: kt[1, :, at(c)],
                 add(0), add(1), off, CHUNK, (WINDOW - BLK) // CHUNK, hook)
            gather_arrived(g1, 3, 0, more1 & end_head)
            gather_arrived(g1, 3, 1, more1 & end_head)
            return 0

        lax.fori_loop(0, kv_count * here, turn, 0)
        final = kv_count - 1
        chain_step(final, 2)
        chain_step(final - 1, 4)
        chain_step(final, 3)
        chain_step(final, 4)
        for g in range(kv_count):
            for k in range(4):
                for w in range(2):
                    @pl.when(has_next)
                    def _():
                        gather(g, k, w).wait_send()

                    @pl.when(is_relay)
                    def _():
                        relay(g, k, w).wait_send()

                    @pl.when(has_prev)
                    def _():
                        chain(g, k, w).wait_send()

    @pl.when(jnp.logical_not(is_long))
    def _():
        r1q, s2q, r1k, s2k = (r1q0, r1q1), (s2q0, s2q1), (r1k0, r1k1), (s2k0, s2k1)
        piece = BLK // groups
        parts = groups // (2 * kv_count)
        kv_piece = BLK // parts

        def kv_spot(ref, m, i):
            head = m // (2 * parts)
            which = lax.rem(m // parts, 2)
            return ref.at[head, which, pl.ds(pl.multiple_of(i * BLK + lax.rem(m, parts) * kv_piece, kv_piece), kv_piece)]

        def q_spot(ref, m, i):
            return ref.at[pl.ds(pl.multiple_of(i * BLK + m * piece, piece), piece)]

        def remote(src, dst, n, d):
            return pltpu.make_async_remote_copy(
                src_ref=src, dst_ref=dst, send_sem=x_send.at[n], recv_sem=x_recv.at[n], device_id={"dp": d}, device_id_type=MESH
            )

        for i in range(here):
            pltpu.make_async_copy(q_spot(q_hbm, dp, i), r1q[i].at[dp], x_recv.at[4 * i]).start()
            pltpu.make_async_copy(kv_spot(kv_hbm, dp, i), r1k[i].at[dp], x_recv.at[4 * i + 1]).start()

            def spread(r, _):
                d = lax.rem(dp + r, groups)
                remote(q_spot(q_hbm, d, i), r1q[i].at[dp], 4 * i, d).start()
                remote(kv_spot(kv_hbm, d, i), r1k[i].at[dp], 4 * i + 1, d).start()
                return 0

            lax.fori_loop(1, groups, spread, 0)
        up_load.start()

        def plan(n, _):
            i = n // groups
            d = lax.rem(n, groups)
            found = jnp.int32(0)
            for s in range(groups):
                found = jnp.where(plan_ref[s, seq * here + i] == d, jnp.int32(s), found)
            source_ref[i, d] = found
            return 0

        lax.fori_loop(0, here * groups, plan, 0)

        for i in range(here):
            pltpu.make_async_copy(r1q[i], r1q[i], x_recv.at[4 * i]).wait()
            pltpu.make_async_copy(r1k[i], r1k[i], x_recv.at[4 * i + 1]).wait()

            def send_on(r, _):
                d = lax.rem(dp + r, groups)
                source = source_ref[i, d]
                s2q[i][d] = r1q[i][source]
                s2k[i][d] = r1k[i][source]
                remote(s2q[i].at[d], q_spot(q_v, dp, i), 4 * i + 2, d).start()
                remote(s2k[i].at[d], kv_spot(kw, dp, i), 4 * i + 3, d).start()
                return 0

            lax.fori_loop(1, groups, send_on, 0)
            source = source_ref[i, dp]
            q_v[pl.ds(pl.multiple_of(i * BLK + dp * piece, piece), piece)] = r1q[i][source]
            mine = dp // (2 * parts), lax.rem(dp // parts, 2), pl.multiple_of(i * BLK + lax.rem(dp, parts) * kv_piece, kv_piece)
            kw[mine[0], mine[1], pl.ds(mine[2], kv_piece)] = r1k[i][source]

        up_load.wait()
        most = pl.ds(0, groups - 1)
        for i in range(here):
            pltpu.make_async_copy(s2q[i].at[most], s2q[i].at[most], x_recv.at[4 * i + 2]).wait()
            pltpu.make_async_copy(s2k[i].at[most], s2k[i].at[most], x_recv.at[4 * i + 3]).wait()
            at = pl.ds(i * BLK, BLK)
            source = source_ref[i, dp]
            slot = seq * here + i
            gain = reward_ref[source, slot] - row_mean(source)
            inside = lane_token < length_ref[source, slot]
            live = jnp.where(inside, 1.0, 0.0)
            weight = jnp.where(inside, gain, 0.0)
            start = jnp.where(inside, 0, NEVER)

            def small(g, _):
                kt[0, :, :BLK] = kw[g, 0, at].T
                kt[1, :, :BLK] = kw[g, 1, at].T

                def keys_out(c, value):
                    dk_ref[at, pl.ds(g, 1)] = (value * SCALE)[:, None]

                def values_out(c, value):
                    dv_ref[at, pl.ds(g, 1)] = value[:, None]

                tile(g, i, start, lane_token, live, weight,
                     lambda c: kw[g, 0, at], lambda c: kw[g, 1, at], lambda c: kt[0, :, :BLK], lambda c: kt[1, :, :BLK],
                     keys_out, values_out, 0, BLK, 1, lambda p: None)
                return 0

            lax.fori_loop(0, kv_count, small, 0)
        for i in range(here):
            for phase in range(2):
                pltpu.make_async_copy(s2q[i].at[most], s2q[i].at[most], x_send.at[4 * i + 2 * phase]).wait()
                pltpu.make_async_copy(s2k[i].at[most], s2k[i].at[most], x_send.at[4 * i + 2 * phase + 1]).wait()


def attention(q, up, kv, plans, groups, seq_count, short_rows):
    tokens, kv_count, per, _ = q.shape
    half = jnp.bfloat16
    piece = BLK // groups
    kv_piece = BLK // (groups // (2 * kv_count))
    tile_rows = BLK * per
    any_spec = pl.BlockSpec(memory_space=pl.ANY)
    vmem = pl.BlockSpec(memory_space=pltpu.VMEM)
    smem = pl.BlockSpec(memory_space=pltpu.SMEM)
    q_pieces = pltpu.VMEM((groups, piece, kv_count, per, DH), half)
    kv_pieces = pltpu.VMEM((groups, kv_piece, DH), half)
    per_hop = pltpu.SemaphoreType.DMA((kv_count, 8))
    chunks = (WINDOW - BLK) // CHUNK
    return pl.pallas_call(
        functools.partial(kernel, groups, seq_count, short_rows, seq_count // 2),
        in_specs=[any_spec, any_spec, any_spec, smem, smem, smem, smem],
        out_specs=[vmem, vmem, vmem, vmem],
        out_shape=[
            jax.ShapeDtypeStruct(q.shape, half),
            jax.ShapeDtypeStruct(q.shape, half),
            jax.ShapeDtypeStruct((tokens, kv_count, DH), jnp.float32),
            jax.ShapeDtypeStruct((tokens, kv_count, DH), jnp.float32),
        ],
        scratch_shapes=[
            pltpu.VMEM(q.shape, half),
            pltpu.VMEM(q.shape, half),
            pltpu.VMEM((kv_count, 2, WINDOW, DH), half),
            pltpu.VMEM((kv_count, 2, OWN, DH), half),
            pltpu.VMEM((2, DH, WINDOW), half),
            pltpu.VMEM((kv_count, 2, WINDOW, DH), jnp.float32),
            pltpu.VMEM((chunks, CHUNK, tile_rows), jnp.float32),
            pltpu.VMEM((chunks, CHUNK, tile_rows), half),
            pltpu.VMEM((kv_count, 4, 2, tokens, DH), half),
            pltpu.VMEM((kv_count, 4, 2, tokens, DH), half),
            q_pieces, q_pieces, q_pieces, q_pieces,
            kv_pieces, kv_pieces, kv_pieces, kv_pieces,
            pltpu.SMEM((tokens // BLK, groups), jnp.int32),
            pltpu.SemaphoreType.DMA((3,)),
            per_hop, per_hop, per_hop, per_hop, per_hop, per_hop,
            pltpu.SemaphoreType.DMA((8,)),
            pltpu.SemaphoreType.DMA((8,)),
        ],
        compiler_params=pltpu.CompilerParams(
            collective_id=0, has_side_effects=True, vmem_limit_bytes=52 * 1024 * 1024
        ),
    )(q, up, kv, *plans)


def body(queries, keys, values, upstream, rewards, response_length, block_start, move_plan):
    groups = lax.axis_size("dp")
    seq_count = lax.axis_size("seq")
    tokens, heads, _ = queries.shape
    kv_count = keys.shape[1]
    per = heads // kv_count
    short_rows = SHORTS // (tokens // BLK)
    q = queries.reshape(tokens, kv_count, per, DH)
    up = upstream.reshape(tokens, kv_count, per, DH)
    kv = jnp.stack([keys, values]).transpose(2, 0, 1, 3)
    plans = (rewards, response_length, block_start, move_plan)
    out, dq, dk, dv = attention(q, up, kv, plans, groups, seq_count, short_rows)
    return (out.reshape(queries.shape), dq.reshape(queries.shape), dk.astype(keys.dtype), dv.astype(values.dtype))


def solution(mesh):
    spec = P(("dp", "seq"), None, None)
    return jax.shard_map(
        body,
        mesh=mesh,
        in_specs=(spec,) * 4 + (P(),) * 4,
        out_specs=(spec,) * 4,
        check_vma=False,
    )
```

```python
import functools

import jax
import jax.numpy as jnp
from jax import lax
from jax.experimental import pallas as pl
from jax.experimental.pallas import tpu as pltpu
from jax.sharding import PartitionSpec as P

DH = 128
BLK = 128
SHORTS = 8
WINDOW = 9 * BLK
OWN = 7 * BLK
CHUNK = 256
NEVER = 1 << 20
SCALE = DH**-0.5
EXP_SCALE = SCALE * 1.4426950408889634
NT = (((1,), (1,)), ((), ()))
NN = (((1,), (0,)), ((), ()))
MESH = pl.DeviceIdType.MESH


def dot(a, b, dims):
    return lax.dot_general(a, b, dims, preferred_element_type=jnp.float32)


def attend_tile(q, up, start, token, live, weight, k, v, kt, vt, add_dk, add_dv, s_ref, p_ref, key0, chunk, chunks, hook):
    rows = q.shape[0]
    hook(0)
    highest = jnp.full((1, rows), -1e30, jnp.float32)
    for c in range(chunks):
        s = dot(k(c), q, NT)
        key = key0 + c * chunk + lax.broadcasted_iota(jnp.int32, (chunk, rows), 0)
        allowed = key >= start
        if c == chunks - 1:
            allowed = allowed & (key <= token)
        s = jnp.where(allowed, s, -1e30)
        s_ref[c, :chunk] = s
        highest = jnp.maximum(highest, jnp.max(s, axis=0, keepdims=True))
    hook(1)
    shift = highest * EXP_SCALE
    total = jnp.zeros((1, rows), jnp.float32)
    out_t = jnp.zeros((DH, rows), jnp.float32)
    for c in range(chunks):
        p = jnp.exp2(s_ref[c, :chunk] * EXP_SCALE - shift)
        total = total + jnp.sum(p, axis=0, keepdims=True)
        p16 = p.astype(jnp.bfloat16)
        p_ref[c, :chunk] = p16
        out_t = out_t + dot(vt(c), p16, NN)
    hook(2)
    out_t = out_t * (live / total)
    scaled = up.astype(jnp.float32).T * (weight / total)
    delta = jnp.sum(scaled * out_t, axis=0, keepdims=True)
    scaled16 = scaled.astype(jnp.bfloat16)
    dq_t = jnp.zeros((DH, rows), jnp.float32)
    for c in range(chunks):
        p16 = p_ref[c, :chunk]
        gp = dot(v(c), scaled16, NN)
        ds = (p16.astype(jnp.float32) * (gp - delta)).astype(jnp.bfloat16)
        add_dv(c, dot(p16, scaled16, NT))
        add_dk(c, dot(ds, q, NN))
        dq_t = dq_t + dot(kt(c), ds, NN)
        if c == 0:
            hook(3)
    return out_t.T, (dq_t * SCALE).T


def kernel(groups, seq_count, short_rows, boundary, q_hbm, up_hbm, kv_hbm, reward_ref, length_ref, block_ref, plan_ref,
           o_ref, dq_ref, dkv_ref,
           q_v, up_v, kw, relay_v, kt, dkv, s_ref, p_ref, sbuf, rbuf,
           r1q0, r1q1, s2q0, s2q1, r1k0, r1k1, s2k0, s2k1, source_ref,
           load_sem, gather_send, gather_recv, relay_send, relay_recv, chain_send, chain_recv, x_send, x_recv):
    seq = lax.axis_index("seq")
    dp = lax.axis_index("dp")
    tokens, kv_count, per, _ = q_v.shape
    tile_rows = BLK * per
    here = tokens // BLK
    rolls = reward_ref.shape[1]
    last = seq_count - 1
    is_long = seq >= short_rows
    has_prev = seq > short_rows
    has_next = is_long & (seq < last)
    is_edge = seq == boundary - 1
    is_relay = seq == boundary
    twin = dp + 2 - 4 * lax.rem(dp // 2, 2)
    plain_next = has_next & jnp.logical_not(is_edge)

    barrier = pltpu.get_barrier_semaphore()

    def signal(seq_to):
        pl.semaphore_signal(barrier, inc=1, device_id={"seq": seq_to}, device_id_type=MESH)

    @pl.when(has_prev)
    def _():
        signal(seq - 1)

    @pl.when(has_next)
    def _():
        signal(seq + 1)

    def signal_twin(seq_to):
        pl.semaphore_signal(barrier, inc=1, device_id={"dp": twin, "seq": seq_to}, device_id_type=MESH)

    @pl.when(is_edge)
    def _():
        signal_twin(boundary)

    @pl.when(is_relay)
    def _():
        signal_twin(boundary - 1)
        signal_twin(boundary)

    @pl.when(jnp.logical_not(is_long))
    def _():
        def greet(r, _):
            pl.semaphore_signal(barrier, inc=1, device_id={"dp": lax.rem(dp + r, groups)}, device_id_type=MESH)
            return 0

        lax.fori_loop(1, groups, greet, 0)
        pl.semaphore_wait(barrier, groups - 1)

    @pl.when(is_relay)
    def _():
        pl.semaphore_wait(barrier, 4)

    @pl.when(is_edge)
    def _():
        pl.semaphore_wait(barrier, 3)

    @pl.when(has_prev & has_next & jnp.logical_not(is_edge | is_relay))
    def _():
        pl.semaphore_wait(barrier, 2)

    @pl.when(has_prev != has_next)
    def _():
        pl.semaphore_wait(barrier, 1)

    lane_token = lax.broadcasted_iota(jnp.int32, (1, tile_rows), 1) // per

    def row_mean(group):
        total = reward_ref[group, 0]
        for r in range(1, rolls):
            total = total + reward_ref[group, r]
        return total * (1.0 / rolls)

    def tile(g, i, start, token, live, weight, k, v, kt_of, vt_of, add_dk, add_dv, key0, chunk, chunks, hook):
        spot = pl.ds(pl.multiple_of(i * BLK, BLK), BLK)
        q = q_v[spot, g].astype(jnp.float32).reshape(tile_rows, DH).astype(jnp.bfloat16)
        up = up_v[spot, g].astype(jnp.float32).reshape(tile_rows, DH)
        out, dq = attend_tile(
            q, up, start, token, live, weight, k, v, kt_of, vt_of, add_dk, add_dv, s_ref, p_ref, key0, chunk, chunks, hook
        )
        o_ref[spot, g] = out.reshape(BLK, per, DH).astype(jnp.bfloat16)
        dq_ref[spot, g] = dq.reshape(BLK, per, DH).astype(jnp.bfloat16)

    up_load = pltpu.make_async_copy(up_hbm, up_v, load_sem.at[0])

    @pl.when(is_long)
    def _():
        q_load = pltpu.make_async_copy(q_hbm, q_v, load_sem.at[1])
        kv_load = pltpu.make_async_copy(kv_hbm, kw.at[:, :, pl.ds(OWN, tokens)], load_sem.at[2])
        kv_load.start()
        kv_load.wait()
        hop_from = (OWN, OWN - tokens, OWN - 2 * tokens, BLK * 2)
        hop_to = (OWN - tokens, OWN - 2 * tokens, OWN - 3 * tokens, 0)
        hop_rows = (tokens, tokens, tokens, BLK)

        def hop(src, dst, send, recv, device, g, k, w):
            return pltpu.make_async_remote_copy(
                src_ref=src, dst_ref=dst, send_sem=send.at[g, 2 * k + w], recv_sem=recv.at[g, 2 * k + w],
                device_id=device, device_id_type=MESH,
            )

        def gather(g, k, w):
            return hop(kw.at[g, w, pl.ds(hop_from[k], hop_rows[k])], kw.at[g, w, pl.ds(hop_to[k], hop_rows[k])],
                       gather_send, gather_recv, {"seq": seq + 1}, g, k, w)

        def edge(g, k, w):
            return hop(kw.at[g, w, pl.ds(hop_from[k], hop_rows[k])], relay_v.at[g, w, pl.ds(hop_to[k], hop_rows[k])],
                       gather_send, relay_recv, {"dp": twin, "seq": boundary}, g, k, w)

        def relay(g, k, w):
            at = pl.ds(hop_to[k], hop_rows[k])
            return hop(relay_v.at[g, w, at], kw.at[g, w, at], relay_send, gather_recv, {"dp": twin, "seq": boundary}, g, k, w)

        def gather_arrived(g, k, w, when=True):
            @pl.when(has_prev & when)
            def _():
                gather(g, k, w).wait_recv()

        def gather_step(g, k, when=True):
            for w in range(2):
                if k > 0:
                    gather_arrived(g, k - 1, w, when)

                @pl.when(plain_next & when)
                def _():
                    gather(g, k, w).start()

                @pl.when(is_edge & when)
                def _():
                    edge(g, k, w).start()

        def relay_step(g, k, when=True):
            @pl.when(is_relay & when)
            def _():
                for w in range(2):
                    edge(g, k, w).wait_recv()
                    relay(g, k, w).start()

        part_at = (0, BLK, 3 * BLK, 5 * BLK, 7 * BLK)
        part_rows = (BLK, tokens, tokens, tokens, tokens)

        def chain(g, k, w):
            return pltpu.make_async_remote_copy(
                src_ref=sbuf.at[g, k, w, pl.ds(0, part_rows[k])],
                dst_ref=rbuf.at[g, k, w, pl.ds(0, part_rows[k])],
                send_sem=chain_send.at[g, 2 * k + w],
                recv_sem=chain_recv.at[g, 2 * k + w],
                device_id={"seq": seq - 1},
                device_id_type=MESH,
            )

        def chain_step(g, k, when=True):
            for w in range(2):
                if k > 0:
                    @pl.when(has_next & when)
                    def _():
                        chain(g, k - 1, w).wait_recv()
                        got = part_rows[k - 1]
                        at = pl.ds(part_at[k] + tokens - got, got)
                        dkv[g, w, at] += rbuf[g, k - 1, w, :got].astype(jnp.float32)

                if k < 4:
                    @pl.when(has_prev & when)
                    def _():
                        sbuf[g, k, w, : part_rows[k]] = dkv[g, w, pl.ds(part_at[k], part_rows[k])].astype(jnp.bfloat16)
                        chain(g, k, w).start()
                else:
                    @pl.when(when)
                    def _():
                        total = dkv[g, w, pl.ds(OWN, tokens)]
                        if w == 0:
                            dkv_ref[g, 0] = (total * SCALE).astype(jnp.bfloat16)
                        else:
                            dkv_ref[g, 1] = total.astype(jnp.bfloat16)

        def clear_first():
            @pl.when(jnp.logical_not(has_prev))
            def _():
                kw[:, :, :OWN] = jnp.zeros((kv_count, 2, OWN, DH), kw.dtype)

        gather_step(0, 0)
        clear_first()
        q_load.start()
        up_load.start()
        dkv[...] = jnp.zeros_like(dkv)
        relay_step(0, 0)
        gather_step(0, 1)
        relay_step(0, 1)
        gather_step(0, 2)
        gather_step(1, 0)
        relay_step(0, 2)
        relay_step(1, 0)
        gather_step(0, 3)
        gather_step(1, 1)
        relay_step(0, 3)
        relay_step(1, 1)

        mean = row_mean(dp)
        first = [block_ref[dp, j] * BLK for j in range(SHORTS, rolls)]
        stop = [f + length_ref[dp, j] for f, j in zip(first, range(SHORTS, rolls))]
        gain = [reward_ref[dp, j] - mean for j in range(SHORTS, rolls)]
        base = seq * tokens - OWN

        q_load.wait()
        up_load.wait()
        gather_arrived(0, 3, 0)
        gather_arrived(0, 3, 1)

        def turn(t, _):
            g = t // here
            i = lax.rem(t, here)
            start_head, end_head = i == 0, i == here - 1
            g1, g2 = jnp.minimum(g + 1, kv_count - 1), jnp.minimum(g + 2, kv_count - 1)
            b1, b2 = jnp.maximum(g - 1, 0), jnp.maximum(g - 2, 0)
            more1, more2, done1, done2 = g < kv_count - 1, g < kv_count - 2, g > 0, g > 1

            def hook(p):
                if p == 0:
                    for n, at in enumerate((start_head, end_head)):
                        gather_step(g1, 2 + n, more1 & at)
                        relay_step(g1, 2 + n, more1 & at)
                    chain_step(b2, 4, done2 & start_head)
                    chain_step(g, 0, end_head)
                if p == 1:
                    for n, at in enumerate((start_head, end_head)):
                        gather_step(g2, n, more2 & at)
                        relay_step(g2, n, more2 & at)
                    chain_step(b1, 2, done1 & start_head)
                    chain_step(b1, 3, done1 & end_head)
                if p == 3:
                    chain_step(g, 1, end_head)

            @pl.when(start_head)
            def _():
                kt[0] = kw[g, 0].T
                kt[1] = kw[g, 1].T

            off = pl.multiple_of(i * BLK, BLK)

            def at(c):
                return pl.ds(pl.multiple_of(off + c * CHUNK, BLK), CHUNK)

            def add(which):
                def one(c, value):
                    dkv[g, which, at(c)] += value

                return one

            token = OWN + i * BLK + lane_token
            start = jnp.full(token.shape, NEVER, jnp.int32)
            live = jnp.zeros(token.shape, jnp.float32)
            weight = jnp.zeros(token.shape, jnp.float32)
            for f, e, w in zip(first, stop, gain):
                inside = (token >= f - base) & (token < e - base)
                start = jnp.where(inside, f - base, start)
                live = jnp.where(inside, 1.0, live)
                weight = jnp.where(inside, w, weight)

            tile(g, i, start, token, live, weight,
                 lambda c: kw[g, 0, at(c)], lambda c: kw[g, 1, at(c)], lambda c: kt[0, :, at(c)], lambda c: kt[1, :, at(c)],
                 add(0), add(1), off, CHUNK, (WINDOW - BLK) // CHUNK, hook)
            gather_arrived(g1, 3, 0, more1 & end_head)
            gather_arrived(g1, 3, 1, more1 & end_head)
            return 0

        lax.fori_loop(0, kv_count * here, turn, 0)
        final = kv_count - 1
        chain_step(final, 2)
        chain_step(final - 1, 4)
        chain_step(final, 3)
        chain_step(final, 4)
        for g in range(kv_count):
            for k in range(4):
                for w in range(2):
                    @pl.when(has_next)
                    def _():
                        gather(g, k, w).wait_send()

                    @pl.when(is_relay)
                    def _():
                        relay(g, k, w).wait_send()

                    @pl.when(has_prev)
                    def _():
                        chain(g, k, w).wait_send()

    @pl.when(jnp.logical_not(is_long))
    def _():
        r1q, s2q, r1k, s2k = (r1q0, r1q1), (s2q0, s2q1), (r1k0, r1k1), (s2k0, s2k1)
        piece = BLK // groups
        parts = groups // (2 * kv_count)
        kv_piece = BLK // parts

        def kv_spot(ref, m, i):
            head = m // (2 * parts)
            which = lax.rem(m // parts, 2)
            return ref.at[head, which, pl.ds(pl.multiple_of(i * BLK + lax.rem(m, parts) * kv_piece, kv_piece), kv_piece)]

        def q_spot(ref, m, i):
            return ref.at[pl.ds(pl.multiple_of(i * BLK + m * piece, piece), piece)]

        def remote(src, dst, n, d):
            return pltpu.make_async_remote_copy(
                src_ref=src, dst_ref=dst, send_sem=x_send.at[n], recv_sem=x_recv.at[n], device_id={"dp": d}, device_id_type=MESH
            )

        for i in range(here):
            pltpu.make_async_copy(q_spot(q_hbm, dp, i), r1q[i].at[dp], x_recv.at[4 * i]).start()
            pltpu.make_async_copy(kv_spot(kv_hbm, dp, i), r1k[i].at[dp], x_recv.at[4 * i + 1]).start()

            def spread(r, _):
                d = lax.rem(dp + r, groups)
                remote(q_spot(q_hbm, d, i), r1q[i].at[dp], 4 * i, d).start()
                remote(kv_spot(kv_hbm, d, i), r1k[i].at[dp], 4 * i + 1, d).start()
                return 0

            lax.fori_loop(1, groups, spread, 0)
        up_load.start()

        def plan(n, _):
            i = n // groups
            d = lax.rem(n, groups)
            found = jnp.int32(0)
            for s in range(groups):
                found = jnp.where(plan_ref[s, seq * here + i] == d, jnp.int32(s), found)
            source_ref[i, d] = found
            return 0

        lax.fori_loop(0, here * groups, plan, 0)

        for i in range(here):
            pltpu.make_async_copy(r1q[i], r1q[i], x_recv.at[4 * i]).wait()
            pltpu.make_async_copy(r1k[i], r1k[i], x_recv.at[4 * i + 1]).wait()

            def send_on(r, _):
                d = lax.rem(dp + r, groups)
                source = source_ref[i, d]
                s2q[i][d] = r1q[i][source]
                s2k[i][d] = r1k[i][source]
                remote(s2q[i].at[d], q_spot(q_v, dp, i), 4 * i + 2, d).start()
                remote(s2k[i].at[d], kv_spot(kw, dp, i), 4 * i + 3, d).start()
                return 0

            lax.fori_loop(1, groups, send_on, 0)
            source = source_ref[i, dp]
            q_v[pl.ds(pl.multiple_of(i * BLK + dp * piece, piece), piece)] = r1q[i][source]
            mine = dp // (2 * parts), lax.rem(dp // parts, 2), pl.multiple_of(i * BLK + lax.rem(dp, parts) * kv_piece, kv_piece)
            kw[mine[0], mine[1], pl.ds(mine[2], kv_piece)] = r1k[i][source]

        up_load.wait()
        most = pl.ds(0, groups - 1)
        for i in range(here):
            pltpu.make_async_copy(s2q[i].at[most], s2q[i].at[most], x_recv.at[4 * i + 2]).wait()
            pltpu.make_async_copy(s2k[i].at[most], s2k[i].at[most], x_recv.at[4 * i + 3]).wait()
            at = pl.ds(i * BLK, BLK)
            source = source_ref[i, dp]
            slot = seq * here + i
            gain = reward_ref[source, slot] - row_mean(source)
            inside = lane_token < length_ref[source, slot]
            live = jnp.where(inside, 1.0, 0.0)
            weight = jnp.where(inside, gain, 0.0)
            start = jnp.where(inside, 0, NEVER)

            def small(g, _):
                kt[0, :, :BLK] = kw[g, 0, at].T
                kt[1, :, :BLK] = kw[g, 1, at].T

                def keys_out(c, value):
                    dkv_ref[g, 0, at] = (value * SCALE).astype(jnp.bfloat16)

                def values_out(c, value):
                    dkv_ref[g, 1, at] = value.astype(jnp.bfloat16)

                tile(g, i, start, lane_token, live, weight,
                     lambda c: kw[g, 0, at], lambda c: kw[g, 1, at], lambda c: kt[0, :, :BLK], lambda c: kt[1, :, :BLK],
                     keys_out, values_out, 0, BLK, 1, lambda p: None)
                return 0

            lax.fori_loop(0, kv_count, small, 0)
        for i in range(here):
            for phase in range(2):
                pltpu.make_async_copy(s2q[i].at[most], s2q[i].at[most], x_send.at[4 * i + 2 * phase]).wait()
                pltpu.make_async_copy(s2k[i].at[most], s2k[i].at[most], x_send.at[4 * i + 2 * phase + 1]).wait()


def attention(q, up, kv, plans, groups, seq_count, short_rows):
    tokens, kv_count, per, _ = q.shape
    half = jnp.bfloat16
    piece = BLK // groups
    kv_piece = BLK // (groups // (2 * kv_count))
    tile_rows = BLK * per
    any_spec = pl.BlockSpec(memory_space=pl.ANY)
    vmem = pl.BlockSpec(memory_space=pltpu.VMEM)
    smem = pl.BlockSpec(memory_space=pltpu.SMEM)
    q_pieces = pltpu.VMEM((groups, piece, kv_count, per, DH), half)
    kv_pieces = pltpu.VMEM((groups, kv_piece, DH), half)
    per_hop = pltpu.SemaphoreType.DMA((kv_count, 8))
    chunks = (WINDOW - BLK) // CHUNK
    return pl.pallas_call(
        functools.partial(kernel, groups, seq_count, short_rows, seq_count // 2),
        in_specs=[any_spec, any_spec, any_spec, smem, smem, smem, smem],
        out_specs=[vmem, vmem, vmem],
        out_shape=[
            jax.ShapeDtypeStruct(q.shape, half),
            jax.ShapeDtypeStruct(q.shape, half),
            jax.ShapeDtypeStruct(kv.shape, half),
        ],
        scratch_shapes=[
            pltpu.VMEM(q.shape, half),
            pltpu.VMEM(q.shape, half),
            pltpu.VMEM((kv_count, 2, WINDOW, DH), half),
            pltpu.VMEM((kv_count, 2, OWN, DH), half),
            pltpu.VMEM((2, DH, WINDOW), half),
            pltpu.VMEM((kv_count, 2, WINDOW, DH), jnp.float32),
            pltpu.VMEM((chunks, CHUNK, tile_rows), jnp.float32),
            pltpu.VMEM((chunks, CHUNK, tile_rows), half),
            pltpu.VMEM((kv_count, 4, 2, tokens, DH), half),
            pltpu.VMEM((kv_count, 4, 2, tokens, DH), half),
            q_pieces, q_pieces, q_pieces, q_pieces,
            kv_pieces, kv_pieces, kv_pieces, kv_pieces,
            pltpu.SMEM((tokens // BLK, groups), jnp.int32),
            pltpu.SemaphoreType.DMA((3,)),
            per_hop, per_hop, per_hop, per_hop, per_hop, per_hop,
            pltpu.SemaphoreType.DMA((8,)),
            pltpu.SemaphoreType.DMA((8,)),
        ],
        compiler_params=pltpu.CompilerParams(
            collective_id=0, has_side_effects=True, vmem_limit_bytes=52 * 1024 * 1024
        ),
    )(q, up, kv, *plans)


def body(queries, keys, values, upstream, rewards, response_length, block_start, move_plan):
    groups = lax.axis_size("dp")
    seq_count = lax.axis_size("seq")
    tokens, heads, _ = queries.shape
    kv_count = keys.shape[1]
    per = heads // kv_count
    short_rows = SHORTS // (tokens // BLK)
    q = queries.reshape(tokens, kv_count, per, DH)
    up = upstream.reshape(tokens, kv_count, per, DH)
    kv = jnp.stack([keys, values]).transpose(2, 0, 1, 3)
    plans = (rewards, response_length, block_start, move_plan)
    out, dq, grads = attention(q, up, kv, plans, groups, seq_count, short_rows)
    grads = grads.transpose(1, 2, 0, 3)
    return (out.reshape(queries.shape), dq.reshape(queries.shape), grads[0], grads[1])


def solution(mesh):
    spec = P(("dp", "seq"), None, None)
    return jax.shard_map(
        body,
        mesh=mesh,
        in_specs=(spec,) * 4 + (P(),) * 4,
        out_specs=(spec,) * 4,
        check_vma=False,
    )
```

```python
import functools

import jax
import jax.numpy as jnp
from jax import lax
from jax.experimental import pallas as pl
from jax.experimental.pallas import tpu as pltpu
from jax.sharding import PartitionSpec as P

DH = 128
BLK = 128
SHORTS = 8
WINDOW = 9 * BLK
OWN = 7 * BLK
CHUNK = 256
NEVER = 1 << 20
SCALE = DH**-0.5
EXP_SCALE = SCALE * 1.4426950408889634
NT = (((1,), (1,)), ((), ()))
NN = (((1,), (0,)), ((), ()))
MESH = pl.DeviceIdType.MESH


def dot(a, b, dims):
    return lax.dot_general(a, b, dims, preferred_element_type=jnp.float32)


def attend_tile(q, up, start, token, live, weight, k, v, kt, vt, add_dk, add_dv, s_ref, p_ref, key0, chunk, chunks, hook):
    rows = q.shape[0]
    hook(0)
    highest = jnp.full((1, rows), -1e30, jnp.float32)
    for c in range(chunks):
        s = dot(k(c), q, NT)
        key = key0 + c * chunk + lax.broadcasted_iota(jnp.int32, (chunk, rows), 0)
        allowed = key >= start
        if c == chunks - 1:
            allowed = allowed & (key <= token)
        s = jnp.where(allowed, s, -1e30)
        s_ref[c, :chunk] = s
        highest = jnp.maximum(highest, jnp.max(s, axis=0, keepdims=True))
    hook(1)
    shift = highest * EXP_SCALE
    total = jnp.zeros((1, rows), jnp.float32)
    out_t = jnp.zeros((DH, rows), jnp.float32)
    for c in range(chunks):
        p = jnp.exp2(s_ref[c, :chunk] * EXP_SCALE - shift)
        total = total + jnp.sum(p, axis=0, keepdims=True)
        p16 = p.astype(jnp.bfloat16)
        p_ref[c, :chunk] = p16
        out_t = out_t + dot(vt(c), p16, NN)
    hook(2)
    out_t = out_t * (live / total)
    scaled = up.astype(jnp.float32).T * (weight / total)
    delta = jnp.sum(scaled * out_t, axis=0, keepdims=True)
    scaled16 = scaled.astype(jnp.bfloat16)
    dq_t = jnp.zeros((DH, rows), jnp.float32)
    for c in range(chunks):
        p16 = p_ref[c, :chunk]
        gp = dot(v(c), scaled16, NN)
        ds = (p16.astype(jnp.float32) * (gp - delta)).astype(jnp.bfloat16)
        add_dv(c, dot(p16, scaled16, NT))
        add_dk(c, dot(ds, q, NN))
        dq_t = dq_t + dot(kt(c), ds, NN)
        if c == 0:
            hook(3)
    return out_t.T, (dq_t * SCALE).T


def kernel(groups, seq_count, short_rows, boundary, q_hbm, up_hbm, kv_hbm, reward_ref, length_ref, block_ref, plan_ref,
           o_ref, dq_ref, dkv_ref,
           q_v, up_v, kw, relay_v, kt, dkv, s_ref, p_ref, sbuf, rbuf,
           r1q0, r1q1, s2q0, s2q1, r1k0, r1k1, s2k0, s2k1, source_ref,
           load_sem, gather_send, gather_recv, relay_send, relay_recv, chain_send, chain_recv, x_send, x_recv):
    seq = lax.axis_index("seq")
    dp = lax.axis_index("dp")
    tokens, kv_count, per, _ = q_v.shape
    tile_rows = BLK * per
    here = tokens // BLK
    rolls = reward_ref.shape[1]
    last = seq_count - 1
    is_long = seq >= short_rows
    has_prev = seq > short_rows
    has_next = is_long & (seq < last)
    is_edge = seq == boundary - 1
    is_relay = seq == boundary
    twin = dp + 2 - 4 * lax.rem(dp // 2, 2)
    late = seq < boundary
    early = seq >= boundary
    plain_next = has_next & jnp.logical_not(is_edge)

    barrier = pltpu.get_barrier_semaphore()

    def signal(seq_to):
        pl.semaphore_signal(barrier, inc=1, device_id={"seq": seq_to}, device_id_type=MESH)

    @pl.when(has_prev)
    def _():
        signal(seq - 1)

    @pl.when(has_next)
    def _():
        signal(seq + 1)

    def signal_twin(seq_to):
        pl.semaphore_signal(barrier, inc=1, device_id={"dp": twin, "seq": seq_to}, device_id_type=MESH)

    @pl.when(is_edge)
    def _():
        signal_twin(boundary)

    @pl.when(is_relay)
    def _():
        signal_twin(boundary - 1)
        signal_twin(boundary)

    @pl.when(jnp.logical_not(is_long))
    def _():
        def greet(r, _):
            pl.semaphore_signal(barrier, inc=1, device_id={"dp": lax.rem(dp + r, groups)}, device_id_type=MESH)
            return 0

        lax.fori_loop(1, groups, greet, 0)
        pl.semaphore_wait(barrier, groups - 1)

    @pl.when(is_relay)
    def _():
        pl.semaphore_wait(barrier, 4)

    @pl.when(is_edge)
    def _():
        pl.semaphore_wait(barrier, 3)

    @pl.when(has_prev & has_next & jnp.logical_not(is_edge | is_relay))
    def _():
        pl.semaphore_wait(barrier, 2)

    @pl.when(has_prev != has_next)
    def _():
        pl.semaphore_wait(barrier, 1)

    lane_token = lax.broadcasted_iota(jnp.int32, (1, tile_rows), 1) // per

    def row_mean(group):
        total = reward_ref[group, 0]
        for r in range(1, rolls):
            total = total + reward_ref[group, r]
        return total * (1.0 / rolls)

    def tile(g, i, start, token, live, weight, k, v, kt_of, vt_of, add_dk, add_dv, key0, chunk, chunks, hook):
        spot = pl.ds(pl.multiple_of(i * BLK, BLK), BLK)
        q = q_v[spot, g].astype(jnp.float32).reshape(tile_rows, DH).astype(jnp.bfloat16)
        up = up_v[spot, g].astype(jnp.float32).reshape(tile_rows, DH)
        out, dq = attend_tile(
            q, up, start, token, live, weight, k, v, kt_of, vt_of, add_dk, add_dv, s_ref, p_ref, key0, chunk, chunks, hook
        )
        o_ref[spot, g] = out.reshape(BLK, per, DH).astype(jnp.bfloat16)
        dq_ref[spot, g] = dq.reshape(BLK, per, DH).astype(jnp.bfloat16)

    up_load = pltpu.make_async_copy(up_hbm, up_v, load_sem.at[0])

    @pl.when(is_long)
    def _():
        q_load = pltpu.make_async_copy(q_hbm, q_v, load_sem.at[1])
        kv_load = pltpu.make_async_copy(kv_hbm, kw.at[:, :, pl.ds(OWN, tokens)], load_sem.at[2])
        kv_load.start()
        kv_load.wait()
        hop_from = (OWN, OWN - tokens, OWN - 2 * tokens, BLK * 2)
        hop_to = (OWN - tokens, OWN - 2 * tokens, OWN - 3 * tokens, 0)
        hop_rows = (tokens, tokens, tokens, BLK)

        def hop(src, dst, send, recv, device, g, k, w):
            return pltpu.make_async_remote_copy(
                src_ref=src, dst_ref=dst, send_sem=send.at[g, 2 * k + w], recv_sem=recv.at[g, 2 * k + w],
                device_id=device, device_id_type=MESH,
            )

        def gather(g, k, w):
            return hop(kw.at[g, w, pl.ds(hop_from[k], hop_rows[k])], kw.at[g, w, pl.ds(hop_to[k], hop_rows[k])],
                       gather_send, gather_recv, {"seq": seq + 1}, g, k, w)

        def edge(g, k, w):
            return hop(kw.at[g, w, pl.ds(hop_from[k], hop_rows[k])], relay_v.at[g, w, pl.ds(hop_to[k], hop_rows[k])],
                       gather_send, relay_recv, {"dp": twin, "seq": boundary}, g, k, w)

        def relay(g, k, w):
            at = pl.ds(hop_to[k], hop_rows[k])
            return hop(relay_v.at[g, w, at], kw.at[g, w, at], relay_send, gather_recv, {"dp": twin, "seq": boundary}, g, k, w)

        def gather_arrived(g, k, w, when=True):
            @pl.when(has_prev & when)
            def _():
                gather(g, k, w).wait_recv()

        def gather_step(g, k, when=True):
            for w in range(2):
                if k > 0:
                    gather_arrived(g, k - 1, w, when)

                @pl.when(plain_next & when)
                def _():
                    gather(g, k, w).start()

                @pl.when(is_edge & when)
                def _():
                    edge(g, k, w).start()

        def relay_step(g, k, when=True):
            @pl.when(is_relay & when)
            def _():
                for w in range(2):
                    edge(g, k, w).wait_recv()
                    relay(g, k, w).start()

        part_at = (0, BLK, 3 * BLK, 5 * BLK, 7 * BLK)
        part_rows = (BLK, tokens, tokens, tokens, tokens)

        def chain(g, k, w):
            return pltpu.make_async_remote_copy(
                src_ref=sbuf.at[g, k, w, pl.ds(0, part_rows[k])],
                dst_ref=rbuf.at[g, k, w, pl.ds(0, part_rows[k])],
                send_sem=chain_send.at[g, 2 * k + w],
                recv_sem=chain_recv.at[g, 2 * k + w],
                device_id={"seq": seq - 1},
                device_id_type=MESH,
            )

        def chain_step(g, k, when=True):
            for w in range(2):
                if k > 0:
                    @pl.when(has_next & when)
                    def _():
                        chain(g, k - 1, w).wait_recv()
                        got = part_rows[k - 1]
                        at = pl.ds(part_at[k] + tokens - got, got)
                        dkv[g, w, at] += rbuf[g, k - 1, w, :got].astype(jnp.float32)

                if k < 4:
                    @pl.when(has_prev & when)
                    def _():
                        sbuf[g, k, w, : part_rows[k]] = dkv[g, w, pl.ds(part_at[k], part_rows[k])].astype(jnp.bfloat16)
                        chain(g, k, w).start()
                else:
                    @pl.when(when)
                    def _():
                        total = dkv[g, w, pl.ds(OWN, tokens)]
                        if w == 0:
                            dkv_ref[g, 0] = (total * SCALE).astype(jnp.bfloat16)
                        else:
                            dkv_ref[g, 1] = total.astype(jnp.bfloat16)

        def clear_first():
            @pl.when(jnp.logical_not(has_prev))
            def _():
                kw[:, :, :OWN] = jnp.zeros((kv_count, 2, OWN, DH), kw.dtype)

        gather_step(0, 0)
        clear_first()
        q_load.start()
        up_load.start()
        dkv[...] = jnp.zeros_like(dkv)
        relay_step(0, 0)
        gather_step(0, 1)
        relay_step(0, 1)
        gather_step(0, 2)
        gather_step(1, 0)
        relay_step(0, 2)
        relay_step(1, 0)
        gather_step(0, 3)
        gather_step(1, 1)
        relay_step(0, 3)
        relay_step(1, 1)

        mean = row_mean(dp)
        first = [block_ref[dp, j] * BLK for j in range(SHORTS, rolls)]
        stop = [f + length_ref[dp, j] for f, j in zip(first, range(SHORTS, rolls))]
        gain = [reward_ref[dp, j] - mean for j in range(SHORTS, rolls)]
        base = seq * tokens - OWN

        q_load.wait()
        up_load.wait()
        gather_arrived(0, 3, 0)
        gather_arrived(0, 3, 1)

        def turn(t, _):
            g = t // here
            i = lax.rem(t, here)
            start_head, end_head = i == 0, i == here - 1
            g1, g2 = jnp.minimum(g + 1, kv_count - 1), jnp.minimum(g + 2, kv_count - 1)
            b1, b2 = jnp.maximum(g - 1, 0), jnp.maximum(g - 2, 0)
            more1, more2, done1, done2 = g < kv_count - 1, g < kv_count - 2, g > 0, g > 1

            def hook(p):
                if p == 0:
                    for n, at in enumerate((start_head, end_head)):
                        gather_step(g1, 2 + n, more1 & at)
                        relay_step(g1, 2 + n, more1 & at)
                    chain_step(b2, 4, done2 & start_head & early)
                    chain_step(0, 2, (g == kv_count - 1) & start_head & late)
                    chain_step(g, 0, end_head)
                if p == 1:
                    for n, at in enumerate((start_head, end_head)):
                        gather_step(g2, n, more2 & at)
                        relay_step(g2, n, more2 & at)
                    chain_step(b1, 2, done1 & start_head & early)
                    chain_step(b1, 3, done1 & end_head & early)
                    chain_step(0, 1, (g == kv_count - 2) & end_head & late)
                    chain_step(0, 3, (g == kv_count - 1) & start_head & late)
                    chain_step(0, 4, (g == kv_count - 1) & end_head & late)
                    chain_step(1, 1, (g == kv_count - 1) & end_head & late)
                if p == 3:
                    chain_step(g, 1, end_head & early)

            @pl.when(start_head)
            def _():
                kt[0] = kw[g, 0].T
                kt[1] = kw[g, 1].T

            off = pl.multiple_of(i * BLK, BLK)

            def at(c):
                return pl.ds(pl.multiple_of(off + c * CHUNK, BLK), CHUNK)

            def add(which):
                def one(c, value):
                    dkv[g, which, at(c)] += value

                return one

            token = OWN + i * BLK + lane_token
            start = jnp.full(token.shape, NEVER, jnp.int32)
            live = jnp.zeros(token.shape, jnp.float32)
            weight = jnp.zeros(token.shape, jnp.float32)
            for f, e, w in zip(first, stop, gain):
                inside = (token >= f - base) & (token < e - base)
                start = jnp.where(inside, f - base, start)
                live = jnp.where(inside, 1.0, live)
                weight = jnp.where(inside, w, weight)

            tile(g, i, start, token, live, weight,
                 lambda c: kw[g, 0, at(c)], lambda c: kw[g, 1, at(c)], lambda c: kt[0, :, at(c)], lambda c: kt[1, :, at(c)],
                 add(0), add(1), off, CHUNK, (WINDOW - BLK) // CHUNK, hook)
            gather_arrived(g1, 3, 0, more1 & end_head)
            gather_arrived(g1, 3, 1, more1 & end_head)
            return 0

        lax.fori_loop(0, kv_count * here, turn, 0)
        final = kv_count - 1

        @pl.when(early)
        def _():
            chain_step(final, 2)
            chain_step(final - 1, 4)
            chain_step(final, 3)
            chain_step(final, 4)

        @pl.when(late)
        def _():
            for total in range(3, final + 5):
                for g in range(1, kv_count):
                    k = total - g
                    if 1 <= k <= 4 and (g, k) != (1, 1):
                        chain_step(g, k)

        for g in range(kv_count):
            for k in range(4):
                for w in range(2):
                    @pl.when(has_next)
                    def _():
                        gather(g, k, w).wait_send()

                    @pl.when(is_relay)
                    def _():
                        relay(g, k, w).wait_send()

                    @pl.when(has_prev)
                    def _():
                        chain(g, k, w).wait_send()

    @pl.when(jnp.logical_not(is_long))
    def _():
        r1q, s2q, r1k, s2k = (r1q0, r1q1), (s2q0, s2q1), (r1k0, r1k1), (s2k0, s2k1)
        piece = BLK // groups
        parts = groups // (2 * kv_count)
        kv_piece = BLK // parts

        def kv_spot(ref, m, i):
            head = m // (2 * parts)
            which = lax.rem(m // parts, 2)
            return ref.at[head, which, pl.ds(pl.multiple_of(i * BLK + lax.rem(m, parts) * kv_piece, kv_piece), kv_piece)]

        def q_spot(ref, m, i):
            return ref.at[pl.ds(pl.multiple_of(i * BLK + m * piece, piece), piece)]

        def remote(src, dst, n, d):
            return pltpu.make_async_remote_copy(
                src_ref=src, dst_ref=dst, send_sem=x_send.at[n], recv_sem=x_recv.at[n], device_id={"dp": d}, device_id_type=MESH
            )

        for i in range(here):
            pltpu.make_async_copy(q_spot(q_hbm, dp, i), r1q[i].at[dp], x_recv.at[4 * i]).start()
            pltpu.make_async_copy(kv_spot(kv_hbm, dp, i), r1k[i].at[dp], x_recv.at[4 * i + 1]).start()

            def spread(r, _):
                d = lax.rem(dp + r, groups)
                remote(q_spot(q_hbm, d, i), r1q[i].at[dp], 4 * i, d).start()
                remote(kv_spot(kv_hbm, d, i), r1k[i].at[dp], 4 * i + 1, d).start()
                return 0

            lax.fori_loop(1, groups, spread, 0)
        up_load.start()

        def plan(n, _):
            i = n // groups
            d = lax.rem(n, groups)
            found = jnp.int32(0)
            for s in range(groups):
                found = jnp.where(plan_ref[s, seq * here + i] == d, jnp.int32(s), found)
            source_ref[i, d] = found
            return 0

        lax.fori_loop(0, here * groups, plan, 0)

        for i in range(here):
            pltpu.make_async_copy(r1q[i], r1q[i], x_recv.at[4 * i]).wait()
            pltpu.make_async_copy(r1k[i], r1k[i], x_recv.at[4 * i + 1]).wait()

            def send_on(r, _):
                d = lax.rem(dp + r, groups)
                source = source_ref[i, d]
                s2q[i][d] = r1q[i][source]
                s2k[i][d] = r1k[i][source]
                remote(s2q[i].at[d], q_spot(q_v, dp, i), 4 * i + 2, d).start()
                remote(s2k[i].at[d], kv_spot(kw, dp, i), 4 * i + 3, d).start()
                return 0

            lax.fori_loop(1, groups, send_on, 0)
            source = source_ref[i, dp]
            q_v[pl.ds(pl.multiple_of(i * BLK + dp * piece, piece), piece)] = r1q[i][source]
            mine = dp // (2 * parts), lax.rem(dp // parts, 2), pl.multiple_of(i * BLK + lax.rem(dp, parts) * kv_piece, kv_piece)
            kw[mine[0], mine[1], pl.ds(mine[2], kv_piece)] = r1k[i][source]

        up_load.wait()
        most = pl.ds(0, groups - 1)
        for i in range(here):
            pltpu.make_async_copy(s2q[i].at[most], s2q[i].at[most], x_recv.at[4 * i + 2]).wait()
            pltpu.make_async_copy(s2k[i].at[most], s2k[i].at[most], x_recv.at[4 * i + 3]).wait()
            at = pl.ds(i * BLK, BLK)
            source = source_ref[i, dp]
            slot = seq * here + i
            gain = reward_ref[source, slot] - row_mean(source)
            inside = lane_token < length_ref[source, slot]
            live = jnp.where(inside, 1.0, 0.0)
            weight = jnp.where(inside, gain, 0.0)
            start = jnp.where(inside, 0, NEVER)

            def small(g, _):
                kt[0, :, :BLK] = kw[g, 0, at].T
                kt[1, :, :BLK] = kw[g, 1, at].T

                def keys_out(c, value):
                    dkv_ref[g, 0, at] = (value * SCALE).astype(jnp.bfloat16)

                def values_out(c, value):
                    dkv_ref[g, 1, at] = value.astype(jnp.bfloat16)

                tile(g, i, start, lane_token, live, weight,
                     lambda c: kw[g, 0, at], lambda c: kw[g, 1, at], lambda c: kt[0, :, :BLK], lambda c: kt[1, :, :BLK],
                     keys_out, values_out, 0, BLK, 1, lambda p: None)
                return 0

            lax.fori_loop(0, kv_count, small, 0)
        for i in range(here):
            for phase in range(2):
                pltpu.make_async_copy(s2q[i].at[most], s2q[i].at[most], x_send.at[4 * i + 2 * phase]).wait()
                pltpu.make_async_copy(s2k[i].at[most], s2k[i].at[most], x_send.at[4 * i + 2 * phase + 1]).wait()


def attention(q, up, kv, plans, groups, seq_count, short_rows):
    tokens, kv_count, per, _ = q.shape
    half = jnp.bfloat16
    piece = BLK // groups
    kv_piece = BLK // (groups // (2 * kv_count))
    tile_rows = BLK * per
    any_spec = pl.BlockSpec(memory_space=pl.ANY)
    vmem = pl.BlockSpec(memory_space=pltpu.VMEM)
    smem = pl.BlockSpec(memory_space=pltpu.SMEM)
    q_pieces = pltpu.VMEM((groups, piece, kv_count, per, DH), half)
    kv_pieces = pltpu.VMEM((groups, kv_piece, DH), half)
    per_hop = pltpu.SemaphoreType.DMA((kv_count, 8))
    chunks = (WINDOW - BLK) // CHUNK
    return pl.pallas_call(
        functools.partial(kernel, groups, seq_count, short_rows, seq_count // 2),
        in_specs=[any_spec, any_spec, any_spec, smem, smem, smem, smem],
        out_specs=[vmem, vmem, vmem],
        out_shape=[
            jax.ShapeDtypeStruct(q.shape, half),
            jax.ShapeDtypeStruct(q.shape, half),
            jax.ShapeDtypeStruct(kv.shape, half),
        ],
        scratch_shapes=[
            pltpu.VMEM(q.shape, half),
            pltpu.VMEM(q.shape, half),
            pltpu.VMEM((kv_count, 2, WINDOW, DH), half),
            pltpu.VMEM((kv_count, 2, OWN, DH), half),
            pltpu.VMEM((2, DH, WINDOW), half),
            pltpu.VMEM((kv_count, 2, WINDOW, DH), jnp.float32),
            pltpu.VMEM((chunks, CHUNK, tile_rows), jnp.float32),
            pltpu.VMEM((chunks, CHUNK, tile_rows), half),
            pltpu.VMEM((kv_count, 4, 2, tokens, DH), half),
            pltpu.VMEM((kv_count, 4, 2, tokens, DH), half),
            q_pieces, q_pieces, q_pieces, q_pieces,
            kv_pieces, kv_pieces, kv_pieces, kv_pieces,
            pltpu.SMEM((tokens // BLK, groups), jnp.int32),
            pltpu.SemaphoreType.DMA((3,)),
            per_hop, per_hop, per_hop, per_hop, per_hop, per_hop,
            pltpu.SemaphoreType.DMA((8,)),
            pltpu.SemaphoreType.DMA((8,)),
        ],
        compiler_params=pltpu.CompilerParams(
            collective_id=0, has_side_effects=True, vmem_limit_bytes=52 * 1024 * 1024
        ),
    )(q, up, kv, *plans)


def body(queries, keys, values, upstream, rewards, response_length, block_start, move_plan):
    groups = lax.axis_size("dp")
    seq_count = lax.axis_size("seq")
    tokens, heads, _ = queries.shape
    kv_count = keys.shape[1]
    per = heads // kv_count
    short_rows = SHORTS // (tokens // BLK)
    q = queries.reshape(tokens, kv_count, per, DH)
    up = upstream.reshape(tokens, kv_count, per, DH)
    kv = jnp.stack([keys, values]).transpose(2, 0, 1, 3)
    plans = (rewards, response_length, block_start, move_plan)
    out, dq, grads = attention(q, up, kv, plans, groups, seq_count, short_rows)
    grads = grads.transpose(1, 2, 0, 3)
    return (out.reshape(queries.shape), dq.reshape(queries.shape), grads[0], grads[1])


def solution(mesh):
    spec = P(("dp", "seq"), None, None)
    return jax.shard_map(
        body,
        mesh=mesh,
        in_specs=(spec,) * 4 + (P(),) * 4,
        out_specs=(spec,) * 4,
        check_vma=False,
    )
```

```python
import functools

import jax
import jax.numpy as jnp
from jax import lax
from jax.experimental import pallas as pl
from jax.experimental.pallas import tpu as pltpu
from jax.sharding import PartitionSpec as P

DH = 128
BLK = 128
SHORTS = 8
WINDOW = 9 * BLK
OWN = 7 * BLK
CHUNK = 256
NEVER = 1 << 20
SCALE = DH**-0.5
EXP_SCALE = SCALE * 1.4426950408889634
NT = (((1,), (1,)), ((), ()))
NN = (((1,), (0,)), ((), ()))
MESH = pl.DeviceIdType.MESH


def dot(a, b, dims):
    return lax.dot_general(a, b, dims, preferred_element_type=jnp.float32)


def attend_tile(q, up, start, token, live, weight, k, v, kt, vt, add_dk, add_dv, s_ref, p_ref, key0, chunk, chunks, hook):
    rows = q.shape[0]
    hook(0)
    highest = jnp.full((1, rows), -1e30, jnp.float32)
    for c in range(chunks):
        s = dot(k(c), q, NT)
        key = key0 + c * chunk + lax.broadcasted_iota(jnp.int32, (chunk, rows), 0)
        allowed = key >= start
        if c == chunks - 1:
            allowed = allowed & (key <= token)
        s = jnp.where(allowed, s, -1e30)
        s_ref[c, :chunk] = s
        highest = jnp.maximum(highest, jnp.max(s, axis=0, keepdims=True))
    hook(1)
    shift = highest * EXP_SCALE
    total = jnp.zeros((1, rows), jnp.float32)
    out_t = jnp.zeros((DH, rows), jnp.float32)
    for c in range(chunks):
        p = jnp.exp2(s_ref[c, :chunk] * EXP_SCALE - shift)
        total = total + jnp.sum(p, axis=0, keepdims=True)
        p16 = p.astype(jnp.bfloat16)
        p_ref[c, :chunk] = p16
        out_t = out_t + dot(vt(c), p16, NN)
    hook(2)
    out_t = out_t * (live / total)
    scaled = up.astype(jnp.float32).T * (weight / total)
    delta = jnp.sum(scaled * out_t, axis=0, keepdims=True)
    scaled16 = scaled.astype(jnp.bfloat16)
    dq_t = jnp.zeros((DH, rows), jnp.float32)
    for c in range(chunks):
        p16 = p_ref[c, :chunk]
        gp = dot(v(c), scaled16, NN)
        ds = (p16.astype(jnp.float32) * (gp - delta)).astype(jnp.bfloat16)
        add_dv(c, dot(p16, scaled16, NT))
        add_dk(c, dot(ds, q, NN))
        dq_t = dq_t + dot(kt(c), ds, NN)
        if c == 0:
            hook(3)
    return out_t.T, (dq_t * SCALE).T


def kernel(groups, seq_count, short_rows, boundary, q_hbm, up_hbm, kv_hbm, reward_ref, length_ref, block_ref, plan_ref,
           o_ref, dq_ref, dkv_ref,
           q_v, up_v, kw, relay_v, kt, dkv, s_ref, p_ref, sbuf, rbuf,
           r1q0, r1q1, s2q0, s2q1, r1k0, r1k1, s2k0, s2k1, source_ref,
           load_sem, gather_send, gather_recv, relay_send, relay_recv, chain_send, chain_recv, x_send, x_recv):
    seq = lax.axis_index("seq")
    dp = lax.axis_index("dp")
    tokens, kv_count, per, _ = q_v.shape
    tile_rows = BLK * per
    here = tokens // BLK
    rolls = reward_ref.shape[1]
    last = seq_count - 1
    is_long = seq >= short_rows
    has_prev = seq > short_rows
    has_next = is_long & (seq < last)
    is_edge = seq == boundary - 1
    is_relay = seq == boundary
    twin = dp + 2 - 4 * lax.rem(dp // 2, 2)
    late = seq < boundary
    early = seq >= boundary
    plain_next = has_next & jnp.logical_not(is_edge)

    barrier = pltpu.get_barrier_semaphore()

    def signal(seq_to):
        pl.semaphore_signal(barrier, inc=1, device_id={"seq": seq_to}, device_id_type=MESH)

    @pl.when(has_prev)
    def _():
        signal(seq - 1)

    @pl.when(has_next)
    def _():
        signal(seq + 1)

    def signal_twin(seq_to):
        pl.semaphore_signal(barrier, inc=1, device_id={"dp": twin, "seq": seq_to}, device_id_type=MESH)

    @pl.when(is_edge)
    def _():
        signal_twin(boundary)

    @pl.when(is_relay)
    def _():
        signal_twin(boundary - 1)
        signal_twin(boundary)

    @pl.when(jnp.logical_not(is_long))
    def _():
        def greet(r, _):
            pl.semaphore_signal(barrier, inc=1, device_id={"dp": lax.rem(dp + r, groups)}, device_id_type=MESH)
            return 0

        lax.fori_loop(1, groups, greet, 0)
        pl.semaphore_wait(barrier, groups - 1)

    @pl.when(is_relay)
    def _():
        pl.semaphore_wait(barrier, 4)

    @pl.when(is_edge)
    def _():
        pl.semaphore_wait(barrier, 3)

    @pl.when(has_prev & has_next & jnp.logical_not(is_edge | is_relay))
    def _():
        pl.semaphore_wait(barrier, 2)

    @pl.when(has_prev != has_next)
    def _():
        pl.semaphore_wait(barrier, 1)

    lane_token = lax.broadcasted_iota(jnp.int32, (1, tile_rows), 1) // per

    def row_mean(group):
        total = reward_ref[group, 0]
        for r in range(1, rolls):
            total = total + reward_ref[group, r]
        return total * (1.0 / rolls)

    def tile(g, i, start, token, live, weight, k, v, kt_of, vt_of, add_dk, add_dv, key0, chunk, chunks, hook):
        spot = pl.ds(pl.multiple_of(i * BLK, BLK), BLK)
        q = q_v[spot, g].astype(jnp.float32).reshape(tile_rows, DH).astype(jnp.bfloat16)
        up = up_v[spot, g].astype(jnp.float32).reshape(tile_rows, DH)
        out, dq = attend_tile(
            q, up, start, token, live, weight, k, v, kt_of, vt_of, add_dk, add_dv, s_ref, p_ref, key0, chunk, chunks, hook
        )
        o_ref[spot, g] = out.reshape(BLK, per, DH).astype(jnp.bfloat16)
        dq_ref[spot, g] = dq.reshape(BLK, per, DH).astype(jnp.bfloat16)

    up_load = pltpu.make_async_copy(up_hbm, up_v, load_sem.at[0])

    @pl.when(is_long)
    def _():
        q_load = pltpu.make_async_copy(q_hbm, q_v, load_sem.at[1])
        kv_load = pltpu.make_async_copy(kv_hbm, kw.at[:, :, pl.ds(OWN, tokens)], load_sem.at[2])
        kv_load.start()
        kv_load.wait()
        hop_from = (OWN, OWN - tokens, OWN - 2 * tokens, BLK * 2)
        hop_to = (OWN - tokens, OWN - 2 * tokens, OWN - 3 * tokens, 0)
        hop_rows = (tokens, tokens, tokens, BLK)

        def hop(src, dst, send, recv, device, g, k, w):
            return pltpu.make_async_remote_copy(
                src_ref=src, dst_ref=dst, send_sem=send.at[g, 2 * k + w], recv_sem=recv.at[g, 2 * k + w],
                device_id=device, device_id_type=MESH,
            )

        def gather(g, k, w):
            return hop(kw.at[g, w, pl.ds(hop_from[k], hop_rows[k])], kw.at[g, w, pl.ds(hop_to[k], hop_rows[k])],
                       gather_send, gather_recv, {"seq": seq + 1}, g, k, w)

        def edge(g, k, w):
            return hop(kw.at[g, w, pl.ds(hop_from[k], hop_rows[k])], relay_v.at[g, w, pl.ds(hop_to[k], hop_rows[k])],
                       gather_send, relay_recv, {"dp": twin, "seq": boundary}, g, k, w)

        def relay(g, k, w):
            at = pl.ds(hop_to[k], hop_rows[k])
            return hop(relay_v.at[g, w, at], kw.at[g, w, at], relay_send, gather_recv, {"dp": twin, "seq": boundary}, g, k, w)

        def gather_arrived(g, k, w, when=True):
            @pl.when((seq > short_rows + k) & when)
            def _():
                gather(g, k, w).wait_recv()

        def gather_step(g, k, when=True):
            for w in range(2):
                if k > 0:
                    gather_arrived(g, k - 1, w, when)

                @pl.when(plain_next & (seq >= short_rows + k) & when)
                def _():
                    gather(g, k, w).start()

                @pl.when(is_edge & when)
                def _():
                    edge(g, k, w).start()

        def relay_step(g, k, when=True):
            @pl.when(is_relay & when)
            def _():
                for w in range(2):
                    edge(g, k, w).wait_recv()
                    relay(g, k, w).start()

        part_at = (0, BLK, 3 * BLK, 5 * BLK, 7 * BLK)
        part_rows = (BLK, tokens, tokens, tokens, tokens)

        def chain(g, k, w):
            return pltpu.make_async_remote_copy(
                src_ref=sbuf.at[g, k, w, pl.ds(0, part_rows[k])],
                dst_ref=rbuf.at[g, k, w, pl.ds(0, part_rows[k])],
                send_sem=chain_send.at[g, 2 * k + w],
                recv_sem=chain_recv.at[g, 2 * k + w],
                device_id={"seq": seq - 1},
                device_id_type=MESH,
            )

        def chain_step(g, k, when=True):
            for w in range(2):
                if k > 0:
                    @pl.when(has_next & (seq >= short_rows + 4 - k) & when)
                    def _():
                        chain(g, k - 1, w).wait_recv()
                        got = part_rows[k - 1]
                        at = pl.ds(part_at[k] + tokens - got, got)
                        dkv[g, w, at] += rbuf[g, k - 1, w, :got].astype(jnp.float32)

                if k < 4:
                    @pl.when(has_prev & (seq >= short_rows + 4 - k) & when)
                    def _():
                        sbuf[g, k, w, : part_rows[k]] = dkv[g, w, pl.ds(part_at[k], part_rows[k])].astype(jnp.bfloat16)
                        chain(g, k, w).start()
                else:
                    @pl.when(when)
                    def _():
                        total = dkv[g, w, pl.ds(OWN, tokens)]
                        if w == 0:
                            dkv_ref[g, 0] = (total * SCALE).astype(jnp.bfloat16)
                        else:
                            dkv_ref[g, 1] = total.astype(jnp.bfloat16)

        def clear_first():
            for n in range(4):
                @pl.when(seq == short_rows + n)
                def _():
                    empty = OWN - n * tokens
                    kw[:, :, :empty] = jnp.zeros((kv_count, 2, empty, DH), kw.dtype)

        gather_step(0, 0)
        clear_first()
        q_load.start()
        up_load.start()
        dkv[...] = jnp.zeros_like(dkv)
        relay_step(0, 0)
        gather_step(0, 1)
        relay_step(0, 1)
        gather_step(0, 2)
        gather_step(1, 0)
        relay_step(0, 2)
        relay_step(1, 0)
        gather_step(0, 3)
        gather_step(1, 1)
        relay_step(0, 3)
        relay_step(1, 1)

        mean = row_mean(dp)
        first = [block_ref[dp, j] * BLK for j in range(SHORTS, rolls)]
        stop = [f + length_ref[dp, j] for f, j in zip(first, range(SHORTS, rolls))]
        gain = [reward_ref[dp, j] - mean for j in range(SHORTS, rolls)]
        base = seq * tokens - OWN

        q_load.wait()
        up_load.wait()
        gather_arrived(0, 3, 0)
        gather_arrived(0, 3, 1)

        def turn(t, _):
            g = t // here
            i = lax.rem(t, here)
            start_head, end_head = i == 0, i == here - 1
            g1, g2 = jnp.minimum(g + 1, kv_count - 1), jnp.minimum(g + 2, kv_count - 1)
            b1, b2 = jnp.maximum(g - 1, 0), jnp.maximum(g - 2, 0)
            more1, more2, done1, done2 = g < kv_count - 1, g < kv_count - 2, g > 0, g > 1

            def hook(p):
                if p == 0:
                    for n, at in enumerate((start_head, end_head)):
                        gather_step(g1, 2 + n, more1 & at)
                        relay_step(g1, 2 + n, more1 & at)
                    chain_step(b2, 4, done2 & start_head & early)
                    chain_step(0, 2, (g == kv_count - 1) & start_head & late)
                    chain_step(g, 0, end_head)
                if p == 1:
                    for n, at in enumerate((start_head, end_head)):
                        gather_step(g2, n, more2 & at)
                        relay_step(g2, n, more2 & at)
                    chain_step(b1, 2, done1 & start_head & early)
                    chain_step(b1, 3, done1 & end_head & early)
                    chain_step(0, 1, (g == kv_count - 2) & end_head & late)
                    chain_step(0, 3, (g == kv_count - 1) & start_head & late)
                    chain_step(0, 4, (g == kv_count - 1) & end_head & late)
                    chain_step(1, 1, (g == kv_count - 1) & end_head & late)
                if p == 3:
                    chain_step(g, 1, end_head & early)

            @pl.when(start_head)
            def _():
                kt[0] = kw[g, 0].T
                kt[1] = kw[g, 1].T

            off = pl.multiple_of(i * BLK, BLK)

            def at(c):
                return pl.ds(pl.multiple_of(off + c * CHUNK, BLK), CHUNK)

            def add(which):
                def one(c, value):
                    dkv[g, which, at(c)] += value

                return one

            token = OWN + i * BLK + lane_token
            start = jnp.full(token.shape, NEVER, jnp.int32)
            live = jnp.zeros(token.shape, jnp.float32)
            weight = jnp.zeros(token.shape, jnp.float32)
            for f, e, w in zip(first, stop, gain):
                inside = (token >= f - base) & (token < e - base)
                start = jnp.where(inside, f - base, start)
                live = jnp.where(inside, 1.0, live)
                weight = jnp.where(inside, w, weight)

            tile(g, i, start, token, live, weight,
                 lambda c: kw[g, 0, at(c)], lambda c: kw[g, 1, at(c)], lambda c: kt[0, :, at(c)], lambda c: kt[1, :, at(c)],
                 add(0), add(1), off, CHUNK, (WINDOW - BLK) // CHUNK, hook)
            gather_arrived(g1, 3, 0, more1 & end_head)
            gather_arrived(g1, 3, 1, more1 & end_head)
            return 0

        lax.fori_loop(0, kv_count * here, turn, 0)
        final = kv_count - 1

        @pl.when(early)
        def _():
            chain_step(final, 2)
            chain_step(final - 1, 4)
            chain_step(final, 3)
            chain_step(final, 4)

        @pl.when(late)
        def _():
            for total in range(3, final + 5):
                for g in range(1, kv_count):
                    k = total - g
                    if 1 <= k <= 4 and (g, k) != (1, 1):
                        chain_step(g, k)

        for g in range(kv_count):
            for k in range(4):
                for w in range(2):
                    @pl.when(has_next & (seq >= short_rows + k))
                    def _():
                        gather(g, k, w).wait_send()

                    @pl.when(is_relay)
                    def _():
                        relay(g, k, w).wait_send()

                    @pl.when(has_prev & (seq >= short_rows + 4 - k))
                    def _():
                        chain(g, k, w).wait_send()

    @pl.when(jnp.logical_not(is_long))
    def _():
        r1q, s2q, r1k, s2k = (r1q0, r1q1), (s2q0, s2q1), (r1k0, r1k1), (s2k0, s2k1)
        piece = BLK // groups
        parts = groups // (2 * kv_count)
        kv_piece = BLK // parts

        def kv_spot(ref, m, i):
            head = m // (2 * parts)
            which = lax.rem(m // parts, 2)
            return ref.at[head, which, pl.ds(pl.multiple_of(i * BLK + lax.rem(m, parts) * kv_piece, kv_piece), kv_piece)]

        def q_spot(ref, m, i):
            return ref.at[pl.ds(pl.multiple_of(i * BLK + m * piece, piece), piece)]

        def remote(src, dst, n, d):
            return pltpu.make_async_remote_copy(
                src_ref=src, dst_ref=dst, send_sem=x_send.at[n], recv_sem=x_recv.at[n], device_id={"dp": d}, device_id_type=MESH
            )

        for i in range(here):
            pltpu.make_async_copy(q_spot(q_hbm, dp, i), r1q[i].at[dp], x_recv.at[4 * i]).start()
            pltpu.make_async_copy(kv_spot(kv_hbm, dp, i), r1k[i].at[dp], x_recv.at[4 * i + 1]).start()

            def spread(r, _):
                d = lax.rem(dp + r, groups)
                remote(q_spot(q_hbm, d, i), r1q[i].at[dp], 4 * i, d).start()
                remote(kv_spot(kv_hbm, d, i), r1k[i].at[dp], 4 * i + 1, d).start()
                return 0

            lax.fori_loop(1, groups, spread, 0)
        up_load.start()

        def plan(n, _):
            i = n // groups
            d = lax.rem(n, groups)
            found = jnp.int32(0)
            for s in range(groups):
                found = jnp.where(plan_ref[s, seq * here + i] == d, jnp.int32(s), found)
            source_ref[i, d] = found
            return 0

        lax.fori_loop(0, here * groups, plan, 0)

        for i in range(here):
            pltpu.make_async_copy(r1q[i], r1q[i], x_recv.at[4 * i]).wait()
            pltpu.make_async_copy(r1k[i], r1k[i], x_recv.at[4 * i + 1]).wait()

            def send_on(r, _):
                d = lax.rem(dp + r, groups)
                source = source_ref[i, d]
                s2q[i][d] = r1q[i][source]
                s2k[i][d] = r1k[i][source]
                remote(s2q[i].at[d], q_spot(q_v, dp, i), 4 * i + 2, d).start()
                remote(s2k[i].at[d], kv_spot(kw, dp, i), 4 * i + 3, d).start()
                return 0

            lax.fori_loop(1, groups, send_on, 0)
            source = source_ref[i, dp]
            q_v[pl.ds(pl.multiple_of(i * BLK + dp * piece, piece), piece)] = r1q[i][source]
            mine = dp // (2 * parts), lax.rem(dp // parts, 2), pl.multiple_of(i * BLK + lax.rem(dp, parts) * kv_piece, kv_piece)
            kw[mine[0], mine[1], pl.ds(mine[2], kv_piece)] = r1k[i][source]

        up_load.wait()
        most = pl.ds(0, groups - 1)
        for i in range(here):
            pltpu.make_async_copy(s2q[i].at[most], s2q[i].at[most], x_recv.at[4 * i + 2]).wait()
            pltpu.make_async_copy(s2k[i].at[most], s2k[i].at[most], x_recv.at[4 * i + 3]).wait()
            at = pl.ds(i * BLK, BLK)
            source = source_ref[i, dp]
            slot = seq * here + i
            gain = reward_ref[source, slot] - row_mean(source)
            inside = lane_token < length_ref[source, slot]
            live = jnp.where(inside, 1.0, 0.0)
            weight = jnp.where(inside, gain, 0.0)
            start = jnp.where(inside, 0, NEVER)

            def small(g, _):
                kt[0, :, :BLK] = kw[g, 0, at].T
                kt[1, :, :BLK] = kw[g, 1, at].T

                def keys_out(c, value):
                    dkv_ref[g, 0, at] = (value * SCALE).astype(jnp.bfloat16)

                def values_out(c, value):
                    dkv_ref[g, 1, at] = value.astype(jnp.bfloat16)

                tile(g, i, start, lane_token, live, weight,
                     lambda c: kw[g, 0, at], lambda c: kw[g, 1, at], lambda c: kt[0, :, :BLK], lambda c: kt[1, :, :BLK],
                     keys_out, values_out, 0, BLK, 1, lambda p: None)
                return 0

            lax.fori_loop(0, kv_count, small, 0)
        for i in range(here):
            for phase in range(2):
                pltpu.make_async_copy(s2q[i].at[most], s2q[i].at[most], x_send.at[4 * i + 2 * phase]).wait()
                pltpu.make_async_copy(s2k[i].at[most], s2k[i].at[most], x_send.at[4 * i + 2 * phase + 1]).wait()


def attention(q, up, kv, plans, groups, seq_count, short_rows):
    tokens, kv_count, per, _ = q.shape
    half = jnp.bfloat16
    piece = BLK // groups
    kv_piece = BLK // (groups // (2 * kv_count))
    tile_rows = BLK * per
    any_spec = pl.BlockSpec(memory_space=pl.ANY)
    vmem = pl.BlockSpec(memory_space=pltpu.VMEM)
    smem = pl.BlockSpec(memory_space=pltpu.SMEM)
    q_pieces = pltpu.VMEM((groups, piece, kv_count, per, DH), half)
    kv_pieces = pltpu.VMEM((groups, kv_piece, DH), half)
    per_hop = pltpu.SemaphoreType.DMA((kv_count, 8))
    chunks = (WINDOW - BLK) // CHUNK
    return pl.pallas_call(
        functools.partial(kernel, groups, seq_count, short_rows, seq_count // 2),
        in_specs=[any_spec, any_spec, any_spec, smem, smem, smem, smem],
        out_specs=[vmem, vmem, vmem],
        out_shape=[
            jax.ShapeDtypeStruct(q.shape, half),
            jax.ShapeDtypeStruct(q.shape, half),
            jax.ShapeDtypeStruct(kv.shape, half),
        ],
        scratch_shapes=[
            pltpu.VMEM(q.shape, half),
            pltpu.VMEM(q.shape, half),
            pltpu.VMEM((kv_count, 2, WINDOW, DH), half),
            pltpu.VMEM((kv_count, 2, OWN, DH), half),
            pltpu.VMEM((2, DH, WINDOW), half),
            pltpu.VMEM((kv_count, 2, WINDOW, DH), jnp.float32),
            pltpu.VMEM((chunks, CHUNK, tile_rows), jnp.float32),
            pltpu.VMEM((chunks, CHUNK, tile_rows), half),
            pltpu.VMEM((kv_count, 4, 2, tokens, DH), half),
            pltpu.VMEM((kv_count, 4, 2, tokens, DH), half),
            q_pieces, q_pieces, q_pieces, q_pieces,
            kv_pieces, kv_pieces, kv_pieces, kv_pieces,
            pltpu.SMEM((tokens // BLK, groups), jnp.int32),
            pltpu.SemaphoreType.DMA((3,)),
            per_hop, per_hop, per_hop, per_hop, per_hop, per_hop,
            pltpu.SemaphoreType.DMA((8,)),
            pltpu.SemaphoreType.DMA((8,)),
        ],
        compiler_params=pltpu.CompilerParams(
            collective_id=0, has_side_effects=True, vmem_limit_bytes=52 * 1024 * 1024
        ),
    )(q, up, kv, *plans)


def body(queries, keys, values, upstream, rewards, response_length, block_start, move_plan):
    groups = lax.axis_size("dp")
    seq_count = lax.axis_size("seq")
    tokens, heads, _ = queries.shape
    kv_count = keys.shape[1]
    per = heads // kv_count
    short_rows = SHORTS // (tokens // BLK)
    q = queries.reshape(tokens, kv_count, per, DH)
    up = upstream.reshape(tokens, kv_count, per, DH)
    kv = jnp.stack([keys, values]).transpose(2, 0, 1, 3)
    plans = (rewards, response_length, block_start, move_plan)
    out, dq, grads = attention(q, up, kv, plans, groups, seq_count, short_rows)
    grads = grads.transpose(1, 2, 0, 3)
    return (out.reshape(queries.shape), dq.reshape(queries.shape), grads[0], grads[1])


def solution(mesh):
    spec = P(("dp", "seq"), None, None)
    return jax.shard_map(
        body,
        mesh=mesh,
        in_specs=(spec,) * 4 + (P(),) * 4,
        out_specs=(spec,) * 4,
        check_vma=False,
    )
```

```python
import functools

import jax
import jax.numpy as jnp
from jax import lax
from jax.experimental import pallas as pl
from jax.experimental.pallas import tpu as pltpu
from jax.sharding import PartitionSpec as P

DH = 128
BLK = 128
SHORTS = 8
WINDOW = 9 * BLK
OWN = 7 * BLK
CHUNK = 256
NEVER = 1 << 20
SCALE = DH**-0.5
EXP_SCALE = SCALE * 1.4426950408889634
NT = (((1,), (1,)), ((), ()))
NN = (((1,), (0,)), ((), ()))
MESH = pl.DeviceIdType.MESH


def dot(a, b, dims):
    return lax.dot_general(a, b, dims, preferred_element_type=jnp.float32)


def attend_tile(q, up, start, token, live, weight, k, v, kt, vt, add_dk, add_dv, s_ref, p_ref, key0, chunk, chunks, hook):
    rows = q.shape[0]
    hook(0)
    highest = jnp.full((1, rows), -1e30, jnp.float32)
    for c in range(chunks):
        s = dot(k(c), q, NT)
        key = key0 + c * chunk + lax.broadcasted_iota(jnp.int32, (chunk, rows), 0)
        allowed = key >= start
        if c == chunks - 1:
            allowed = allowed & (key <= token)
        s = jnp.where(allowed, s, -1e30)
        s_ref[c, :chunk] = s
        highest = jnp.maximum(highest, jnp.max(s, axis=0, keepdims=True))
    hook(1)
    shift = highest * EXP_SCALE
    total = jnp.zeros((1, rows), jnp.float32)
    out_t = jnp.zeros((DH, rows), jnp.float32)
    for c in range(chunks):
        p = jnp.exp2(s_ref[c, :chunk] * EXP_SCALE - shift)
        total = total + jnp.sum(p, axis=0, keepdims=True)
        p16 = p.astype(jnp.bfloat16)
        p_ref[c, :chunk] = p16
        out_t = out_t + dot(vt(c), p16, NN)
    hook(2)
    out_t = out_t * (live / total)
    scaled = up.astype(jnp.float32).T * (weight / total)
    delta = jnp.sum(scaled * out_t, axis=0, keepdims=True)
    scaled16 = scaled.astype(jnp.bfloat16)
    dq_t = jnp.zeros((DH, rows), jnp.float32)
    for c in range(chunks):
        p16 = p_ref[c, :chunk]
        gp = dot(v(c), scaled16, NN)
        ds = (p16.astype(jnp.float32) * (gp - delta)).astype(jnp.bfloat16)
        add_dv(c, dot(p16, scaled16, NT))
        add_dk(c, dot(ds, q, NN))
        dq_t = dq_t + dot(kt(c), ds, NN)
        if c == 0:
            hook(3)
    return out_t.T, (dq_t * SCALE).T


def kernel(groups, seq_count, short_rows, boundary, q_hbm, up_hbm, kv_hbm, reward_ref, length_ref, block_ref, plan_ref,
           o_hbm, dq_hbm, dkv_ref,
           o_ref, dq_ref, q_v, up_v, kw, relay_v, kt, dkv, s_ref, p_ref, sbuf, rbuf,
           r1q0, r1q1, s2q0, s2q1, r1k0, r1k1, s2k0, s2k1, source_ref,
           load_sem, gather_send, gather_recv, relay_send, relay_recv, chain_send, chain_recv, x_send, x_recv):
    seq = lax.axis_index("seq")
    dp = lax.axis_index("dp")
    tokens, kv_count, per, _ = q_v.shape
    tile_rows = BLK * per
    here = tokens // BLK
    rolls = reward_ref.shape[1]
    last = seq_count - 1
    is_long = seq >= short_rows
    has_prev = seq > short_rows
    has_next = is_long & (seq < last)
    is_edge = seq == boundary - 1
    is_relay = seq == boundary
    twin = dp + 2 - 4 * lax.rem(dp // 2, 2)
    late = seq < boundary
    early = seq >= boundary
    plain_next = has_next & jnp.logical_not(is_edge)

    barrier = pltpu.get_barrier_semaphore()

    def signal(seq_to):
        pl.semaphore_signal(barrier, inc=1, device_id={"seq": seq_to}, device_id_type=MESH)

    @pl.when(has_prev)
    def _():
        signal(seq - 1)

    @pl.when(has_next)
    def _():
        signal(seq + 1)

    def signal_twin(seq_to):
        pl.semaphore_signal(barrier, inc=1, device_id={"dp": twin, "seq": seq_to}, device_id_type=MESH)

    @pl.when(is_edge)
    def _():
        signal_twin(boundary)

    @pl.when(is_relay)
    def _():
        signal_twin(boundary - 1)
        signal_twin(boundary)

    @pl.when(jnp.logical_not(is_long))
    def _():
        def greet(r, _):
            pl.semaphore_signal(barrier, inc=1, device_id={"dp": lax.rem(dp + r, groups)}, device_id_type=MESH)
            return 0

        lax.fori_loop(1, groups, greet, 0)
        pl.semaphore_wait(barrier, groups - 1)

    @pl.when(is_relay)
    def _():
        pl.semaphore_wait(barrier, 4)

    @pl.when(is_edge)
    def _():
        pl.semaphore_wait(barrier, 3)

    @pl.when(has_prev & has_next & jnp.logical_not(is_edge | is_relay))
    def _():
        pl.semaphore_wait(barrier, 2)

    @pl.when(has_prev != has_next)
    def _():
        pl.semaphore_wait(barrier, 1)

    lane_token = lax.broadcasted_iota(jnp.int32, (1, tile_rows), 1) // per

    def row_mean(group):
        total = reward_ref[group, 0]
        for r in range(1, rolls):
            total = total + reward_ref[group, r]
        return total * (1.0 / rolls)

    def tile(g, i, start, token, live, weight, k, v, kt_of, vt_of, add_dk, add_dv, key0, chunk, chunks, hook):
        spot = pl.ds(pl.multiple_of(i * BLK, BLK), BLK)
        q = q_v[spot, g].astype(jnp.float32).reshape(tile_rows, DH).astype(jnp.bfloat16)
        up = up_v[spot, g].astype(jnp.float32).reshape(tile_rows, DH)
        out, dq = attend_tile(
            q, up, start, token, live, weight, k, v, kt_of, vt_of, add_dk, add_dv, s_ref, p_ref, key0, chunk, chunks, hook
        )
        o_ref[spot, g] = out.reshape(BLK, per, DH).astype(jnp.bfloat16)
        dq_ref[spot, g] = dq.reshape(BLK, per, DH).astype(jnp.bfloat16)
        pltpu.make_async_copy(o_ref.at[spot, g], o_hbm.at[spot, g], load_sem.at[3]).start()
        pltpu.make_async_copy(dq_ref.at[spot, g], dq_hbm.at[spot, g], load_sem.at[4]).start()

    up_load = pltpu.make_async_copy(up_hbm, up_v, load_sem.at[0])

    @pl.when(is_long)
    def _():
        q_load = pltpu.make_async_copy(q_hbm, q_v, load_sem.at[1])
        kv_load = pltpu.make_async_copy(kv_hbm, kw.at[:, :, pl.ds(OWN, tokens)], load_sem.at[2])
        kv_load.start()
        kv_load.wait()
        hop_from = (OWN, OWN - tokens, OWN - 2 * tokens, BLK * 2)
        hop_to = (OWN - tokens, OWN - 2 * tokens, OWN - 3 * tokens, 0)
        hop_rows = (tokens, tokens, tokens, BLK)

        def hop(src, dst, send, recv, device, g, k, w):
            return pltpu.make_async_remote_copy(
                src_ref=src, dst_ref=dst, send_sem=send.at[g, 2 * k + w], recv_sem=recv.at[g, 2 * k + w],
                device_id=device, device_id_type=MESH,
            )

        def gather(g, k, w):
            return hop(kw.at[g, w, pl.ds(hop_from[k], hop_rows[k])], kw.at[g, w, pl.ds(hop_to[k], hop_rows[k])],
                       gather_send, gather_recv, {"seq": seq + 1}, g, k, w)

        def edge(g, k, w):
            return hop(kw.at[g, w, pl.ds(hop_from[k], hop_rows[k])], relay_v.at[g, w, pl.ds(hop_to[k], hop_rows[k])],
                       gather_send, relay_recv, {"dp": twin, "seq": boundary}, g, k, w)

        def relay(g, k, w):
            at = pl.ds(hop_to[k], hop_rows[k])
            return hop(relay_v.at[g, w, at], kw.at[g, w, at], relay_send, gather_recv, {"dp": twin, "seq": boundary}, g, k, w)

        def gather_arrived(g, k, w, when=True):
            @pl.when((seq > short_rows + k) & when)
            def _():
                gather(g, k, w).wait_recv()

        def gather_step(g, k, when=True):
            for w in range(2):
                if k > 0:
                    gather_arrived(g, k - 1, w, when)

                @pl.when(plain_next & (seq >= short_rows + k) & when)
                def _():
                    gather(g, k, w).start()

                @pl.when(is_edge & when)
                def _():
                    edge(g, k, w).start()

        def relay_step(g, k, when=True):
            @pl.when(is_relay & when)
            def _():
                for w in range(2):
                    edge(g, k, w).wait_recv()
                    relay(g, k, w).start()

        part_at = (0, BLK, 3 * BLK, 5 * BLK, 7 * BLK)
        part_rows = (BLK, tokens, tokens, tokens, tokens)

        def chain(g, k, w):
            return pltpu.make_async_remote_copy(
                src_ref=sbuf.at[g, k, w, pl.ds(0, part_rows[k])],
                dst_ref=rbuf.at[g, k, w, pl.ds(0, part_rows[k])],
                send_sem=chain_send.at[g, 2 * k + w],
                recv_sem=chain_recv.at[g, 2 * k + w],
                device_id={"seq": seq - 1},
                device_id_type=MESH,
            )

        def chain_step(g, k, when=True):
            for w in range(2):
                if k > 0:
                    @pl.when(has_next & (seq >= short_rows + 4 - k) & when)
                    def _():
                        chain(g, k - 1, w).wait_recv()
                        got = part_rows[k - 1]
                        at = pl.ds(part_at[k] + tokens - got, got)
                        dkv[g, w, at] += rbuf[g, k - 1, w, :got].astype(jnp.float32)

                if k < 4:
                    @pl.when(has_prev & (seq >= short_rows + 4 - k) & when)
                    def _():
                        sbuf[g, k, w, : part_rows[k]] = dkv[g, w, pl.ds(part_at[k], part_rows[k])].astype(jnp.bfloat16)
                        chain(g, k, w).start()
                else:
                    @pl.when(when)
                    def _():
                        total = dkv[g, w, pl.ds(OWN, tokens)]
                        if w == 0:
                            dkv_ref[g, 0] = (total * SCALE).astype(jnp.bfloat16)
                        else:
                            dkv_ref[g, 1] = total.astype(jnp.bfloat16)

        def clear_first():
            for n in range(4):
                @pl.when(seq == short_rows + n)
                def _():
                    empty = OWN - n * tokens
                    kw[:, :, :empty] = jnp.zeros((kv_count, 2, empty, DH), kw.dtype)

        gather_step(0, 0)
        clear_first()
        q_load.start()
        up_load.start()
        dkv[...] = jnp.zeros_like(dkv)
        relay_step(0, 0)
        gather_step(0, 1)
        relay_step(0, 1)
        gather_step(0, 2)
        relay_step(0, 2)
        gather_step(1, 0)
        relay_step(1, 0)
        relay_step(0, 3)
        gather_step(0, 3)
        gather_step(1, 1)
        relay_step(1, 1)

        mean = row_mean(dp)
        first = [block_ref[dp, j] * BLK for j in range(SHORTS, rolls)]
        stop = [f + length_ref[dp, j] for f, j in zip(first, range(SHORTS, rolls))]
        gain = [reward_ref[dp, j] - mean for j in range(SHORTS, rolls)]
        base = seq * tokens - OWN

        q_load.wait()
        up_load.wait()
        gather_arrived(0, 3, 0)
        gather_arrived(0, 3, 1)

        def turn(t, _):
            g = t // here
            i = lax.rem(t, here)
            start_head, end_head = i == 0, i == here - 1
            g1, g2 = jnp.minimum(g + 1, kv_count - 1), jnp.minimum(g + 2, kv_count - 1)
            b1, b2 = jnp.maximum(g - 1, 0), jnp.maximum(g - 2, 0)
            more1, more2, done1, done2 = g < kv_count - 1, g < kv_count - 2, g > 0, g > 1

            def hook(p):
                if p == 0:
                    for n, at in enumerate((start_head, end_head)):
                        relay_step(g1, 2 + n, more1 & at)
                        gather_step(g1, 2 + n, more1 & at)
                    chain_step(b2, 4, done2 & start_head & early)
                    chain_step(0, 2, (g == kv_count - 1) & start_head & late)
                    chain_step(g, 0, end_head)
                if p == 1:
                    for n, at in enumerate((start_head, end_head)):
                        relay_step(g2, n, more2 & at)
                        gather_step(g2, n, more2 & at)
                    chain_step(b1, 2, done1 & start_head & early)
                    chain_step(b1, 3, done1 & end_head & early)
                    chain_step(0, 1, (g == kv_count - 2) & end_head & late)
                    chain_step(0, 3, (g == kv_count - 1) & start_head & late)
                    chain_step(0, 4, (g == kv_count - 1) & end_head & late)
                    chain_step(1, 1, (g == kv_count - 1) & end_head & late)
                if p == 3:
                    chain_step(g, 1, end_head & early)

            @pl.when(start_head)
            def _():
                kt[0] = kw[g, 0].T
                kt[1] = kw[g, 1].T

            off = pl.multiple_of(i * BLK, BLK)

            def at(c):
                return pl.ds(pl.multiple_of(off + c * CHUNK, BLK), CHUNK)

            def add(which):
                def one(c, value):
                    dkv[g, which, at(c)] += value

                return one

            token = OWN + i * BLK + lane_token
            start = jnp.full(token.shape, NEVER, jnp.int32)
            live = jnp.zeros(token.shape, jnp.float32)
            weight = jnp.zeros(token.shape, jnp.float32)
            for f, e, w in zip(first, stop, gain):
                inside = (token >= f - base) & (token < e - base)
                start = jnp.where(inside, f - base, start)
                live = jnp.where(inside, 1.0, live)
                weight = jnp.where(inside, w, weight)

            tile(g, i, start, token, live, weight,
                 lambda c: kw[g, 0, at(c)], lambda c: kw[g, 1, at(c)], lambda c: kt[0, :, at(c)], lambda c: kt[1, :, at(c)],
                 add(0), add(1), off, CHUNK, (WINDOW - BLK) // CHUNK, hook)
            gather_arrived(g1, 3, 0, more1 & end_head)
            gather_arrived(g1, 3, 1, more1 & end_head)
            return 0

        lax.fori_loop(0, kv_count * here, turn, 0)
        final = kv_count - 1

        @pl.when(early)
        def _():
            chain_step(final, 2)
            chain_step(final - 1, 4)
            chain_step(final, 3)
            chain_step(final, 4)

        @pl.when(late)
        def _():
            for total in range(3, final + 5):
                for g in range(1, kv_count):
                    k = total - g
                    if 1 <= k <= 4 and (g, k) != (1, 1):
                        chain_step(g, k)

        for g in range(kv_count):
            for k in range(4):
                for w in range(2):
                    @pl.when(has_next & (seq >= short_rows + k))
                    def _():
                        gather(g, k, w).wait_send()

                    @pl.when(is_relay)
                    def _():
                        relay(g, k, w).wait_send()

                    @pl.when(has_prev & (seq >= short_rows + 4 - k))
                    def _():
                        chain(g, k, w).wait_send()

    @pl.when(jnp.logical_not(is_long))
    def _():
        r1q, s2q, r1k, s2k = (r1q0, r1q1), (s2q0, s2q1), (r1k0, r1k1), (s2k0, s2k1)
        piece = BLK // groups
        parts = groups // (2 * kv_count)
        kv_piece = BLK // parts

        def kv_spot(ref, m, i):
            head = m // (2 * parts)
            which = lax.rem(m // parts, 2)
            return ref.at[head, which, pl.ds(pl.multiple_of(i * BLK + lax.rem(m, parts) * kv_piece, kv_piece), kv_piece)]

        def q_spot(ref, m, i):
            return ref.at[pl.ds(pl.multiple_of(i * BLK + m * piece, piece), piece)]

        def remote(src, dst, n, d):
            return pltpu.make_async_remote_copy(
                src_ref=src, dst_ref=dst, send_sem=x_send.at[n], recv_sem=x_recv.at[n], device_id={"dp": d}, device_id_type=MESH
            )

        for i in range(here):
            pltpu.make_async_copy(q_spot(q_hbm, dp, i), r1q[i].at[dp], x_recv.at[4 * i]).start()
            pltpu.make_async_copy(kv_spot(kv_hbm, dp, i), r1k[i].at[dp], x_recv.at[4 * i + 1]).start()

            def spread(r, _):
                d = lax.rem(dp + r, groups)
                remote(q_spot(q_hbm, d, i), r1q[i].at[dp], 4 * i, d).start()
                remote(kv_spot(kv_hbm, d, i), r1k[i].at[dp], 4 * i + 1, d).start()
                return 0

            lax.fori_loop(1, groups, spread, 0)
        up_load.start()

        def plan(n, _):
            i = n // groups
            d = lax.rem(n, groups)
            found = jnp.int32(0)
            for s in range(groups):
                found = jnp.where(plan_ref[s, seq * here + i] == d, jnp.int32(s), found)
            source_ref[i, d] = found
            return 0

        lax.fori_loop(0, here * groups, plan, 0)

        for i in range(here):
            pltpu.make_async_copy(r1q[i], r1q[i], x_recv.at[4 * i]).wait()
            pltpu.make_async_copy(r1k[i], r1k[i], x_recv.at[4 * i + 1]).wait()

            def send_on(r, _):
                d = lax.rem(dp + r, groups)
                source = source_ref[i, d]
                s2q[i][d] = r1q[i][source]
                s2k[i][d] = r1k[i][source]
                remote(s2q[i].at[d], q_spot(q_v, dp, i), 4 * i + 2, d).start()
                remote(s2k[i].at[d], kv_spot(kw, dp, i), 4 * i + 3, d).start()
                return 0

            lax.fori_loop(1, groups, send_on, 0)
            source = source_ref[i, dp]
            q_v[pl.ds(pl.multiple_of(i * BLK + dp * piece, piece), piece)] = r1q[i][source]
            mine = dp // (2 * parts), lax.rem(dp // parts, 2), pl.multiple_of(i * BLK + lax.rem(dp, parts) * kv_piece, kv_piece)
            kw[mine[0], mine[1], pl.ds(mine[2], kv_piece)] = r1k[i][source]

        up_load.wait()
        most = pl.ds(0, groups - 1)
        for i in range(here):
            pltpu.make_async_copy(s2q[i].at[most], s2q[i].at[most], x_recv.at[4 * i + 2]).wait()
            pltpu.make_async_copy(s2k[i].at[most], s2k[i].at[most], x_recv.at[4 * i + 3]).wait()
            at = pl.ds(i * BLK, BLK)
            source = source_ref[i, dp]
            slot = seq * here + i
            gain = reward_ref[source, slot] - row_mean(source)
            inside = lane_token < length_ref[source, slot]
            live = jnp.where(inside, 1.0, 0.0)
            weight = jnp.where(inside, gain, 0.0)
            start = jnp.where(inside, 0, NEVER)

            def small(g, _):
                kt[0, :, :BLK] = kw[g, 0, at].T
                kt[1, :, :BLK] = kw[g, 1, at].T

                def keys_out(c, value):
                    dkv_ref[g, 0, at] = (value * SCALE).astype(jnp.bfloat16)

                def values_out(c, value):
                    dkv_ref[g, 1, at] = value.astype(jnp.bfloat16)

                tile(g, i, start, lane_token, live, weight,
                     lambda c: kw[g, 0, at], lambda c: kw[g, 1, at], lambda c: kt[0, :, :BLK], lambda c: kt[1, :, :BLK],
                     keys_out, values_out, 0, BLK, 1, lambda p: None)
                return 0

            lax.fori_loop(0, kv_count, small, 0)
        for i in range(here):
            for phase in range(2):
                pltpu.make_async_copy(s2q[i].at[most], s2q[i].at[most], x_send.at[4 * i + 2 * phase]).wait()
                pltpu.make_async_copy(s2k[i].at[most], s2k[i].at[most], x_send.at[4 * i + 2 * phase + 1]).wait()

    pltpu.make_async_copy(o_ref, o_hbm, load_sem.at[3]).wait()
    pltpu.make_async_copy(dq_ref, dq_hbm, load_sem.at[4]).wait()


def attention(q, up, kv, plans, groups, seq_count, short_rows):
    tokens, kv_count, per, _ = q.shape
    half = jnp.bfloat16
    piece = BLK // groups
    kv_piece = BLK // (groups // (2 * kv_count))
    tile_rows = BLK * per
    any_spec = pl.BlockSpec(memory_space=pl.ANY)
    vmem = pl.BlockSpec(memory_space=pltpu.VMEM)
    smem = pl.BlockSpec(memory_space=pltpu.SMEM)
    q_pieces = pltpu.VMEM((groups, piece, kv_count, per, DH), half)
    kv_pieces = pltpu.VMEM((groups, kv_piece, DH), half)
    per_hop = pltpu.SemaphoreType.DMA((kv_count, 8))
    chunks = (WINDOW - BLK) // CHUNK
    return pl.pallas_call(
        functools.partial(kernel, groups, seq_count, short_rows, seq_count // 2),
        in_specs=[any_spec, any_spec, any_spec, smem, smem, smem, smem],
        out_specs=[any_spec, any_spec, vmem],
        out_shape=[
            jax.ShapeDtypeStruct(q.shape, half),
            jax.ShapeDtypeStruct(q.shape, half),
            jax.ShapeDtypeStruct(kv.shape, half),
        ],
        scratch_shapes=[
            pltpu.VMEM(q.shape, half),
            pltpu.VMEM(q.shape, half),
            pltpu.VMEM(q.shape, half),
            pltpu.VMEM(q.shape, half),
            pltpu.VMEM((kv_count, 2, WINDOW, DH), half),
            pltpu.VMEM((kv_count, 2, OWN, DH), half),
            pltpu.VMEM((2, DH, WINDOW), half),
            pltpu.VMEM((kv_count, 2, WINDOW, DH), jnp.float32),
            pltpu.VMEM((chunks, CHUNK, tile_rows), jnp.float32),
            pltpu.VMEM((chunks, CHUNK, tile_rows), half),
            pltpu.VMEM((kv_count, 4, 2, tokens, DH), half),
            pltpu.VMEM((kv_count, 4, 2, tokens, DH), half),
            q_pieces, q_pieces, q_pieces, q_pieces,
            kv_pieces, kv_pieces, kv_pieces, kv_pieces,
            pltpu.SMEM((tokens // BLK, groups), jnp.int32),
            pltpu.SemaphoreType.DMA((5,)),
            per_hop, per_hop, per_hop, per_hop, per_hop, per_hop,
            pltpu.SemaphoreType.DMA((8,)),
            pltpu.SemaphoreType.DMA((8,)),
        ],
        compiler_params=pltpu.CompilerParams(
            collective_id=0, has_side_effects=True, vmem_limit_bytes=52 * 1024 * 1024
        ),
    )(q, up, kv, *plans)


def body(queries, keys, values, upstream, rewards, response_length, block_start, move_plan):
    groups = lax.axis_size("dp")
    seq_count = lax.axis_size("seq")
    tokens, heads, _ = queries.shape
    kv_count = keys.shape[1]
    per = heads // kv_count
    short_rows = SHORTS // (tokens // BLK)
    q = queries.reshape(tokens, kv_count, per, DH)
    up = upstream.reshape(tokens, kv_count, per, DH)
    kv = jnp.stack([keys, values]).transpose(2, 0, 1, 3)
    plans = (rewards, response_length, block_start, move_plan)
    out, dq, grads = attention(q, up, kv, plans, groups, seq_count, short_rows)
    grads = grads.transpose(1, 2, 0, 3)
    return (out.reshape(queries.shape), dq.reshape(queries.shape), grads[0], grads[1])


def solution(mesh):
    spec = P(("dp", "seq"), None, None)
    return jax.shard_map(
        body,
        mesh=mesh,
        in_specs=(spec,) * 4 + (P(),) * 4,
        out_specs=(spec,) * 4,
        check_vma=False,
    )
```

```python
import functools

import jax
import jax.numpy as jnp
from jax import lax
from jax.experimental import pallas as pl
from jax.experimental.pallas import tpu as pltpu
from jax.sharding import PartitionSpec as P

DH = 128
BLK = 128
SHORTS = 8
WINDOW = 9 * BLK
OWN = 7 * BLK
CHUNK = 256
NEVER = 1 << 20
SCALE = DH**-0.5
EXP_SCALE = SCALE * 1.4426950408889634
NT = (((1,), (1,)), ((), ()))
NN = (((1,), (0,)), ((), ()))
MESH = pl.DeviceIdType.MESH


def dot(a, b, dims):
    return lax.dot_general(a, b, dims, preferred_element_type=jnp.float32)


def attend_tile(q, up, start, token, live, weight, k, v, kt, vt, add_dk, add_dv, s_ref, p_ref, key0, chunk, chunks, hook):
    rows = q.shape[0]
    hook(0)
    highest = jnp.full((1, rows), -1e30, jnp.float32)
    for c in range(chunks):
        s = dot(k(c), q, NT)
        key = key0 + c * chunk + lax.broadcasted_iota(jnp.int32, (chunk, rows), 0)
        allowed = key >= start
        if c == chunks - 1:
            allowed = allowed & (key <= token)
        s = jnp.where(allowed, s, -1e30)
        s_ref[c, :chunk] = s
        highest = jnp.maximum(highest, jnp.max(s, axis=0, keepdims=True))
    hook(1)
    shift = highest * EXP_SCALE
    total = jnp.zeros((1, rows), jnp.float32)
    out_t = jnp.zeros((DH, rows), jnp.float32)
    for c in range(chunks):
        p = jnp.exp2(s_ref[c, :chunk] * EXP_SCALE - shift)
        total = total + jnp.sum(p, axis=0, keepdims=True)
        p16 = p.astype(jnp.bfloat16)
        p_ref[c, :chunk] = p16
        out_t = out_t + dot(vt(c), p16, NN)
    hook(2)
    out_t = out_t * (live / total)
    scaled = up.astype(jnp.float32).T * (weight / total)
    delta = jnp.sum(scaled * out_t, axis=0, keepdims=True)
    scaled16 = scaled.astype(jnp.bfloat16)
    dq_t = jnp.zeros((DH, rows), jnp.float32)
    for c in range(chunks):
        p16 = p_ref[c, :chunk]
        gp = dot(v(c), scaled16, NN)
        ds = (p16.astype(jnp.float32) * (gp - delta)).astype(jnp.bfloat16)
        add_dv(c, dot(p16, scaled16, NT))
        add_dk(c, dot(ds, q, NN))
        dq_t = dq_t + dot(kt(c), ds, NN)
        if c == 0:
            hook(3)
    return out_t.T, (dq_t * SCALE).T


def kernel(groups, seq_count, short_rows, boundary, q_hbm, up_hbm, kv_hbm, reward_ref, length_ref, block_ref, plan_ref,
           o_hbm, dq_hbm, dkv_ref,
           o_ref, dq_ref, q_v, up_v, kw, relay_v, kt, dkv, s_ref, p_ref, sbuf, rbuf,
           r1q0, r1q1, s2q0, s2q1, r1k0, r1k1, s2k0, s2k1, source_ref,
           load_sem, gather_send, gather_recv, relay_send, relay_recv, chain_send, chain_recv, x_send, x_recv):
    seq = lax.axis_index("seq")
    dp = lax.axis_index("dp")
    tokens, kv_count, per, _ = q_v.shape
    tile_rows = BLK * per
    here = tokens // BLK
    rolls = reward_ref.shape[1]
    last = seq_count - 1
    is_long = seq >= short_rows
    has_prev = seq > short_rows
    has_next = is_long & (seq < last)
    is_edge = seq == boundary - 1
    is_relay = seq == boundary
    twin = dp + 2 - 4 * lax.rem(dp // 2, 2)
    late = seq < boundary
    early = seq >= boundary
    plain_next = has_next & jnp.logical_not(is_edge)

    barrier = pltpu.get_barrier_semaphore()

    def signal(seq_to):
        pl.semaphore_signal(barrier, inc=1, device_id={"seq": seq_to}, device_id_type=MESH)

    @pl.when(has_prev)
    def _():
        signal(seq - 1)

    @pl.when(has_next)
    def _():
        signal(seq + 1)

    def signal_twin(seq_to):
        pl.semaphore_signal(barrier, inc=1, device_id={"dp": twin, "seq": seq_to}, device_id_type=MESH)

    @pl.when(is_edge)
    def _():
        signal_twin(boundary)

    @pl.when(is_relay)
    def _():
        signal_twin(boundary - 1)
        signal_twin(boundary)

    @pl.when(jnp.logical_not(is_long))
    def _():
        def greet(r, _):
            pl.semaphore_signal(barrier, inc=1, device_id={"dp": lax.rem(dp + r, groups)}, device_id_type=MESH)
            return 0

        lax.fori_loop(1, groups, greet, 0)
        pl.semaphore_wait(barrier, groups - 1)

    @pl.when(is_relay)
    def _():
        pl.semaphore_wait(barrier, 4)

    @pl.when(is_edge)
    def _():
        pl.semaphore_wait(barrier, 3)

    @pl.when(has_prev & has_next & jnp.logical_not(is_edge | is_relay))
    def _():
        pl.semaphore_wait(barrier, 2)

    @pl.when(has_prev != has_next)
    def _():
        pl.semaphore_wait(barrier, 1)

    lane_token = lax.broadcasted_iota(jnp.int32, (1, tile_rows), 1) // per

    def row_mean(group):
        total = reward_ref[group, 0]
        for r in range(1, rolls):
            total = total + reward_ref[group, r]
        return total * (1.0 / rolls)

    def tile(g, i, start, token, live, weight, k, v, kt_of, vt_of, add_dk, add_dv, key0, chunk, chunks, hook):
        spot = pl.ds(pl.multiple_of(i * BLK, BLK), BLK)
        q = q_v[spot, g].astype(jnp.float32).reshape(tile_rows, DH).astype(jnp.bfloat16)
        up = up_v[spot, g].astype(jnp.float32).reshape(tile_rows, DH)
        out, dq = attend_tile(
            q, up, start, token, live, weight, k, v, kt_of, vt_of, add_dk, add_dv, s_ref, p_ref, key0, chunk, chunks, hook
        )
        o_ref[spot, g] = out.reshape(BLK, per, DH).astype(jnp.bfloat16)
        dq_ref[spot, g] = dq.reshape(BLK, per, DH).astype(jnp.bfloat16)
        pltpu.make_async_copy(o_ref.at[spot, g], o_hbm.at[spot, g], load_sem.at[3]).start()
        pltpu.make_async_copy(dq_ref.at[spot, g], dq_hbm.at[spot, g], load_sem.at[4]).start()

    up_load = pltpu.make_async_copy(up_hbm, up_v, load_sem.at[0])

    @pl.when(is_long)
    def _():
        q_load = pltpu.make_async_copy(q_hbm, q_v, load_sem.at[1])
        kv_load = pltpu.make_async_copy(kv_hbm, kw.at[:, :, pl.ds(OWN, tokens)], load_sem.at[2])
        kv_load.start()
        hop_from = (OWN, OWN - tokens, OWN - 2 * tokens, BLK * 2)
        hop_to = (OWN - tokens, OWN - 2 * tokens, OWN - 3 * tokens, 0)
        hop_rows = (tokens, tokens, tokens, BLK)

        def hop(src, dst, send, recv, device, g, k, w):
            return pltpu.make_async_remote_copy(
                src_ref=src, dst_ref=dst, send_sem=send.at[g, 2 * k + w], recv_sem=recv.at[g, 2 * k + w],
                device_id=device, device_id_type=MESH,
            )

        def outgoing(g, k, w):
            return kv_hbm.at[g, w] if k == 0 else kw.at[g, w, pl.ds(hop_from[k], hop_rows[k])]

        def gather(g, k, w):
            return hop(outgoing(g, k, w), kw.at[g, w, pl.ds(hop_to[k], hop_rows[k])],
                       gather_send, gather_recv, {"seq": seq + 1}, g, k, w)

        def edge(g, k, w):
            return hop(outgoing(g, k, w), relay_v.at[g, w, pl.ds(hop_to[k], hop_rows[k])],
                       gather_send, relay_recv, {"dp": twin, "seq": boundary}, g, k, w)

        def relay(g, k, w):
            at = pl.ds(hop_to[k], hop_rows[k])
            return hop(relay_v.at[g, w, at], kw.at[g, w, at], relay_send, gather_recv, {"dp": twin, "seq": boundary}, g, k, w)

        def gather_arrived(g, k, w, when=True):
            @pl.when((seq > short_rows + k) & when)
            def _():
                gather(g, k, w).wait_recv()

        def gather_step(g, k, when=True):
            for w in range(2):
                if k > 0:
                    gather_arrived(g, k - 1, w, when)

                @pl.when(plain_next & (seq >= short_rows + k) & when)
                def _():
                    gather(g, k, w).start()

                @pl.when(is_edge & when)
                def _():
                    edge(g, k, w).start()

        def relay_step(g, k, when=True):
            @pl.when(is_relay & when)
            def _():
                for w in range(2):
                    edge(g, k, w).wait_recv()
                    relay(g, k, w).start()

        part_at = (0, BLK, 3 * BLK, 5 * BLK, 7 * BLK)
        part_rows = (BLK, tokens, tokens, tokens, tokens)

        def chain(g, k, w):
            return pltpu.make_async_remote_copy(
                src_ref=sbuf.at[g, k, w, pl.ds(0, part_rows[k])],
                dst_ref=rbuf.at[g, k, w, pl.ds(0, part_rows[k])],
                send_sem=chain_send.at[g, 2 * k + w],
                recv_sem=chain_recv.at[g, 2 * k + w],
                device_id={"seq": seq - 1},
                device_id_type=MESH,
            )

        def chain_step(g, k, when=True):
            for w in range(2):
                if k > 0:
                    @pl.when(has_next & (seq >= short_rows + 4 - k) & when)
                    def _():
                        chain(g, k - 1, w).wait_recv()
                        got = part_rows[k - 1]
                        at = pl.ds(part_at[k] + tokens - got, got)
                        dkv[g, w, at] += rbuf[g, k - 1, w, :got].astype(jnp.float32)

                if k < 4:
                    @pl.when(has_prev & (seq >= short_rows + 4 - k) & when)
                    def _():
                        sbuf[g, k, w, : part_rows[k]] = dkv[g, w, pl.ds(part_at[k], part_rows[k])].astype(jnp.bfloat16)
                        chain(g, k, w).start()
                else:
                    @pl.when(when)
                    def _():
                        total = dkv[g, w, pl.ds(OWN, tokens)]
                        if w == 0:
                            dkv_ref[g, 0] = (total * SCALE).astype(jnp.bfloat16)
                        else:
                            dkv_ref[g, 1] = total.astype(jnp.bfloat16)

        def clear_first():
            for n in range(4):
                @pl.when(seq == short_rows + n)
                def _():
                    empty = OWN - n * tokens
                    kw[:, :, :empty] = jnp.zeros((kv_count, 2, empty, DH), kw.dtype)

        gather_step(0, 0)
        clear_first()
        q_load.start()
        up_load.start()
        dkv[...] = jnp.zeros_like(dkv)
        relay_step(0, 0)
        gather_step(0, 1)
        relay_step(0, 1)
        gather_step(0, 2)
        relay_step(0, 2)
        gather_step(1, 0)
        relay_step(1, 0)
        relay_step(0, 3)
        gather_step(0, 3)
        gather_step(1, 1)
        relay_step(1, 1)

        mean = row_mean(dp)
        first = [block_ref[dp, j] * BLK for j in range(SHORTS, rolls)]
        stop = [f + length_ref[dp, j] for f, j in zip(first, range(SHORTS, rolls))]
        gain = [reward_ref[dp, j] - mean for j in range(SHORTS, rolls)]
        base = seq * tokens - OWN

        kv_load.wait()
        q_load.wait()
        up_load.wait()
        gather_arrived(0, 3, 0)
        gather_arrived(0, 3, 1)

        def turn(t, _):
            g = t // here
            i = lax.rem(t, here)
            start_head, end_head = i == 0, i == here - 1
            g1, g2 = jnp.minimum(g + 1, kv_count - 1), jnp.minimum(g + 2, kv_count - 1)
            b1, b2 = jnp.maximum(g - 1, 0), jnp.maximum(g - 2, 0)
            more1, more2, done1, done2 = g < kv_count - 1, g < kv_count - 2, g > 0, g > 1

            def hook(p):
                if p == 0:
                    for n, at in enumerate((start_head, end_head)):
                        relay_step(g1, 2 + n, more1 & at)
                        gather_step(g1, 2 + n, more1 & at)
                    chain_step(b2, 4, done2 & start_head & early)
                    chain_step(0, 2, (g == kv_count - 1) & start_head & late)
                    chain_step(g, 0, end_head)
                if p == 1:
                    for n, at in enumerate((start_head, end_head)):
                        relay_step(g2, n, more2 & at)
                        gather_step(g2, n, more2 & at)
                    chain_step(b1, 2, done1 & start_head & early)
                    chain_step(b1, 3, done1 & end_head & early)
                    chain_step(0, 1, (g == kv_count - 2) & end_head & late)
                    chain_step(0, 3, (g == kv_count - 1) & start_head & late)
                    chain_step(0, 4, (g == kv_count - 1) & end_head & late)
                    chain_step(1, 1, (g == kv_count - 1) & end_head & late)
                if p == 3:
                    chain_step(g, 1, end_head & early)

            @pl.when(start_head)
            def _():
                kt[0] = kw[g, 0].T
                kt[1] = kw[g, 1].T

            off = pl.multiple_of(i * BLK, BLK)

            def at(c):
                return pl.ds(pl.multiple_of(off + c * CHUNK, BLK), CHUNK)

            def add(which):
                def one(c, value):
                    dkv[g, which, at(c)] += value

                return one

            token = OWN + i * BLK + lane_token
            start = jnp.full(token.shape, NEVER, jnp.int32)
            live = jnp.zeros(token.shape, jnp.float32)
            weight = jnp.zeros(token.shape, jnp.float32)
            for f, e, w in zip(first, stop, gain):
                inside = (token >= f - base) & (token < e - base)
                start = jnp.where(inside, f - base, start)
                live = jnp.where(inside, 1.0, live)
                weight = jnp.where(inside, w, weight)

            tile(g, i, start, token, live, weight,
                 lambda c: kw[g, 0, at(c)], lambda c: kw[g, 1, at(c)], lambda c: kt[0, :, at(c)], lambda c: kt[1, :, at(c)],
                 add(0), add(1), off, CHUNK, (WINDOW - BLK) // CHUNK, hook)
            gather_arrived(g1, 3, 0, more1 & end_head)
            gather_arrived(g1, 3, 1, more1 & end_head)
            return 0

        lax.fori_loop(0, kv_count * here, turn, 0)
        final = kv_count - 1

        @pl.when(early)
        def _():
            chain_step(final, 2)
            chain_step(final - 1, 4)
            chain_step(final, 3)
            chain_step(final, 4)

        @pl.when(late)
        def _():
            for total in range(3, final + 5):
                for g in range(1, kv_count):
                    k = total - g
                    if 1 <= k <= 4 and (g, k) != (1, 1):
                        chain_step(g, k)

        for g in range(kv_count):
            for k in range(4):
                for w in range(2):
                    @pl.when(has_next & (seq >= short_rows + k))
                    def _():
                        gather(g, k, w).wait_send()

                    @pl.when(is_relay)
                    def _():
                        relay(g, k, w).wait_send()

                    @pl.when(has_prev & (seq >= short_rows + 4 - k))
                    def _():
                        chain(g, k, w).wait_send()

    @pl.when(jnp.logical_not(is_long))
    def _():
        r1q, s2q, r1k, s2k = (r1q0, r1q1), (s2q0, s2q1), (r1k0, r1k1), (s2k0, s2k1)
        piece = BLK // groups
        parts = groups // (2 * kv_count)
        kv_piece = BLK // parts

        def kv_spot(ref, m, i):
            head = m // (2 * parts)
            which = lax.rem(m // parts, 2)
            return ref.at[head, which, pl.ds(pl.multiple_of(i * BLK + lax.rem(m, parts) * kv_piece, kv_piece), kv_piece)]

        def q_spot(ref, m, i):
            return ref.at[pl.ds(pl.multiple_of(i * BLK + m * piece, piece), piece)]

        def remote(src, dst, n, d):
            return pltpu.make_async_remote_copy(
                src_ref=src, dst_ref=dst, send_sem=x_send.at[n], recv_sem=x_recv.at[n], device_id={"dp": d}, device_id_type=MESH
            )

        for i in range(here):
            pltpu.make_async_copy(q_spot(q_hbm, dp, i), r1q[i].at[dp], x_recv.at[4 * i]).start()
            pltpu.make_async_copy(kv_spot(kv_hbm, dp, i), r1k[i].at[dp], x_recv.at[4 * i + 1]).start()

            def spread(r, _):
                d = lax.rem(dp + r, groups)
                remote(q_spot(q_hbm, d, i), r1q[i].at[dp], 4 * i, d).start()
                remote(kv_spot(kv_hbm, d, i), r1k[i].at[dp], 4 * i + 1, d).start()
                return 0

            lax.fori_loop(1, groups, spread, 0)
        up_load.start()

        def plan(n, _):
            i = n // groups
            d = lax.rem(n, groups)
            found = jnp.int32(0)
            for s in range(groups):
                found = jnp.where(plan_ref[s, seq * here + i] == d, jnp.int32(s), found)
            source_ref[i, d] = found
            return 0

        lax.fori_loop(0, here * groups, plan, 0)

        for i in range(here):
            pltpu.make_async_copy(r1q[i], r1q[i], x_recv.at[4 * i]).wait()
            pltpu.make_async_copy(r1k[i], r1k[i], x_recv.at[4 * i + 1]).wait()

            def send_on(r, _):
                d = lax.rem(dp + r, groups)
                source = source_ref[i, d]
                s2q[i][d] = r1q[i][source]
                s2k[i][d] = r1k[i][source]
                remote(s2q[i].at[d], q_spot(q_v, dp, i), 4 * i + 2, d).start()
                remote(s2k[i].at[d], kv_spot(kw, dp, i), 4 * i + 3, d).start()
                return 0

            lax.fori_loop(1, groups, send_on, 0)
            source = source_ref[i, dp]
            q_v[pl.ds(pl.multiple_of(i * BLK + dp * piece, piece), piece)] = r1q[i][source]
            mine = dp // (2 * parts), lax.rem(dp // parts, 2), pl.multiple_of(i * BLK + lax.rem(dp, parts) * kv_piece, kv_piece)
            kw[mine[0], mine[1], pl.ds(mine[2], kv_piece)] = r1k[i][source]

        up_load.wait()
        most = pl.ds(0, groups - 1)
        for i in range(here):
            pltpu.make_async_copy(s2q[i].at[most], s2q[i].at[most], x_recv.at[4 * i + 2]).wait()
            pltpu.make_async_copy(s2k[i].at[most], s2k[i].at[most], x_recv.at[4 * i + 3]).wait()
            at = pl.ds(i * BLK, BLK)
            source = source_ref[i, dp]
            slot = seq * here + i
            gain = reward_ref[source, slot] - row_mean(source)
            inside = lane_token < length_ref[source, slot]
            live = jnp.where(inside, 1.0, 0.0)
            weight = jnp.where(inside, gain, 0.0)
            start = jnp.where(inside, 0, NEVER)

            def small(g, _):
                kt[0, :, :BLK] = kw[g, 0, at].T
                kt[1, :, :BLK] = kw[g, 1, at].T

                def keys_out(c, value):
                    dkv_ref[g, 0, at] = (value * SCALE).astype(jnp.bfloat16)

                def values_out(c, value):
                    dkv_ref[g, 1, at] = value.astype(jnp.bfloat16)

                tile(g, i, start, lane_token, live, weight,
                     lambda c: kw[g, 0, at], lambda c: kw[g, 1, at], lambda c: kt[0, :, :BLK], lambda c: kt[1, :, :BLK],
                     keys_out, values_out, 0, BLK, 1, lambda p: None)
                return 0

            lax.fori_loop(0, kv_count, small, 0)
        for i in range(here):
            for phase in range(2):
                pltpu.make_async_copy(s2q[i].at[most], s2q[i].at[most], x_send.at[4 * i + 2 * phase]).wait()
                pltpu.make_async_copy(s2k[i].at[most], s2k[i].at[most], x_send.at[4 * i + 2 * phase + 1]).wait()

    pltpu.make_async_copy(o_ref, o_hbm, load_sem.at[3]).wait()
    pltpu.make_async_copy(dq_ref, dq_hbm, load_sem.at[4]).wait()


def attention(q, up, kv, plans, groups, seq_count, short_rows):
    tokens, kv_count, per, _ = q.shape
    half = jnp.bfloat16
    piece = BLK // groups
    kv_piece = BLK // (groups // (2 * kv_count))
    tile_rows = BLK * per
    any_spec = pl.BlockSpec(memory_space=pl.ANY)
    vmem = pl.BlockSpec(memory_space=pltpu.VMEM)
    smem = pl.BlockSpec(memory_space=pltpu.SMEM)
    q_pieces = pltpu.VMEM((groups, piece, kv_count, per, DH), half)
    kv_pieces = pltpu.VMEM((groups, kv_piece, DH), half)
    per_hop = pltpu.SemaphoreType.DMA((kv_count, 8))
    chunks = (WINDOW - BLK) // CHUNK
    return pl.pallas_call(
        functools.partial(kernel, groups, seq_count, short_rows, seq_count // 2),
        in_specs=[any_spec, any_spec, any_spec, smem, smem, smem, smem],
        out_specs=[any_spec, any_spec, vmem],
        out_shape=[
            jax.ShapeDtypeStruct(q.shape, half),
            jax.ShapeDtypeStruct(q.shape, half),
            jax.ShapeDtypeStruct(kv.shape, half),
        ],
        scratch_shapes=[
            pltpu.VMEM(q.shape, half),
            pltpu.VMEM(q.shape, half),
            pltpu.VMEM(q.shape, half),
            pltpu.VMEM(q.shape, half),
            pltpu.VMEM((kv_count, 2, WINDOW, DH), half),
            pltpu.VMEM((kv_count, 2, OWN, DH), half),
            pltpu.VMEM((2, DH, WINDOW), half),
            pltpu.VMEM((kv_count, 2, WINDOW, DH), jnp.float32),
            pltpu.VMEM((chunks, CHUNK, tile_rows), jnp.float32),
            pltpu.VMEM((chunks, CHUNK, tile_rows), half),
            pltpu.VMEM((kv_count, 4, 2, tokens, DH), half),
            pltpu.VMEM((kv_count, 4, 2, tokens, DH), half),
            q_pieces, q_pieces, q_pieces, q_pieces,
            kv_pieces, kv_pieces, kv_pieces, kv_pieces,
            pltpu.SMEM((tokens // BLK, groups), jnp.int32),
            pltpu.SemaphoreType.DMA((5,)),
            per_hop, per_hop, per_hop, per_hop, per_hop, per_hop,
            pltpu.SemaphoreType.DMA((8,)),
            pltpu.SemaphoreType.DMA((8,)),
        ],
        compiler_params=pltpu.CompilerParams(
            collective_id=0, has_side_effects=True, vmem_limit_bytes=52 * 1024 * 1024
        ),
    )(q, up, kv, *plans)


def body(queries, keys, values, upstream, rewards, response_length, block_start, move_plan):
    groups = lax.axis_size("dp")
    seq_count = lax.axis_size("seq")
    tokens, heads, _ = queries.shape
    kv_count = keys.shape[1]
    per = heads // kv_count
    short_rows = SHORTS // (tokens // BLK)
    q = queries.reshape(tokens, kv_count, per, DH)
    up = upstream.reshape(tokens, kv_count, per, DH)
    kv = jnp.stack([keys, values]).transpose(2, 0, 1, 3)
    plans = (rewards, response_length, block_start, move_plan)
    out, dq, grads = attention(q, up, kv, plans, groups, seq_count, short_rows)
    grads = grads.transpose(1, 2, 0, 3)
    return (out.reshape(queries.shape), dq.reshape(queries.shape), grads[0], grads[1])


def solution(mesh):
    spec = P(("dp", "seq"), None, None)
    return jax.shard_map(
        body,
        mesh=mesh,
        in_specs=(spec,) * 4 + (P(),) * 4,
        out_specs=(spec,) * 4,
        check_vma=False,
    )
```
